32 devices in a mesh: batch: 2 (over x), frame: 4 (over z), tensor: 4 (over y, core).
Axes of the slice: x: 2, y: 2, z: 4, core: 2. Of those that a mesh axis runs over, the one named last changes fastest.
Arguments:
- tokens: bfloat16 [16, 4, 256, 1024], P('batch', 'frame', 'tensor'), may hold values from -6 to 6
- noise_level: float32 [16, 4], P('batch', 'frame'), may hold values from 0 to 1
- w_ada: bfloat16 [1024, 6, 1024], P(None, None, 'tensor'), may hold values from -0.375 to 0.375
- b_ada: bfloat16 [6, 1024], P(None, 'tensor'), may hold values from -1.75 to 1.75
- w_qkv: bfloat16 [1024, 3, 1024], P(None, None, 'tensor'), may hold values from -0.1875 to 0.1875
- b_qkv: bfloat16 [3, 1024], P(None, 'tensor'), may hold values from -1.75 to 1.75
- w_out: bfloat16 [1024, 1024], P('tensor'), may hold values from -0.75 to 0.75
- b_out: bfloat16 [1024], replicated, may hold values from -1.75 to 1.75
- w_fc1: bfloat16 [1024, 4096], P(None, 'tensor'), may hold values from -0.1875 to 0.1875
- b_fc1: bfloat16 [4096], P('tensor'), may hold values from -1.75 to 1.75
- w_fc2: bfloat16 [4096, 1024], P('tensor'), may hold values from -0.09375 to 0.09375
- b_fc2: bfloat16 [1024], replicated, may hold values from -1.75 to 1.75
- cotangent: bfloat16 [16, 4, 256, 1024], P('batch', 'frame', 'tensor'), may hold values from -6 to 6
Outputs:
- output: bfloat16 [16, 4, 256, 1024], P('batch', 'frame', 'tensor')
- tokens_grad: float32 [16, 4, 256, 1024], P('batch', 'frame', 'tensor')
- ada_grad: float32 [1024, 6, 1024], P(None, None, 'tensor')
- ada_bias_grad: float32 [6, 1024], P(None, 'tensor')
- qkv_grad: float32 [1024, 3, 1024], P(None, None, 'tensor')
- qkv_bias_grad: float32 [3, 1024], P(None, 'tensor')
- out_grad: float32 [1024, 1024], P('tensor')
- out_bias_grad: float32 [1024], replicated
- fc1_grad: float32 [1024, 4096], P(None, 'tensor')
- fc1_bias_grad: float32 [4096], P('tensor')
- fc2_grad: float32 [4096, 1024], P('tensor')
- fc2_bias_grad: float32 [1024], replicated
The draws below stay inside these ranges and needn't reach their ends.
All inputs are finite; a program needn't handle non-finite values.
Results may differ from the reference program's by a relative error of at most 0.019.
The reference program's roundings to bfloat16 on the way count: a program that leaves them out, or rounds other values in their place, can miss the bound.
Values may be sent and summed in bfloat16 or wider, within the bound.
A program may use at most 256 MiB of HBM per device.

```python
import jax
import jax.numpy as jnp
from jax import lax

D = 1024
HEADS = 16
HD = 64
FF = 4096
GRID = 16
PATCHES = 256
FRAMES = 4
CLIPS = 16


def block_levels(rng, extent, split, least, top_value):
    gain = 1.0
    for axis_at, shards_of in split:
        draws = jax.random.uniform(jax.random.fold_in(jax.random.fold_in(rng, 6), axis_at), (shards_of,), jnp.float32, least / len(split), top_value / len(split))
        gain = gain * jnp.repeat(jnp.exp(draws), extent[axis_at] // shards_of).reshape((-1,) + (1,) * (len(extent) - 1 - axis_at))
    return gain


def normal_values(stream_key, dims, scale, reach, split=(), kind=jnp.bfloat16):
    level = block_levels(stream_key, dims, split, -0.22, 0.18) if split else 1.0
    entries = jax.random.normal(stream_key, dims, jnp.float32) * scale * level
    return jnp.minimum(jnp.maximum(entries, -reach), reach).astype(kind)


def setup_inputs(seed: int = 0) -> dict:
    seeds = jax.random.split(jax.random.key(seed), 14)
    return {
        "tokens": normal_values(seeds[0], (CLIPS, FRAMES, PATCHES, D), 1.0, 6.0, ((0, 2), (1, 4), (2, 4))),
        "noise_level": jnp.clip(1.0 * jax.random.uniform(seeds[1], (CLIPS, FRAMES), jnp.float32) ** block_levels(seeds[1], (CLIPS, FRAMES), ((0, 2), (1, 4)), -0.2, 0.2), 0.0, 1.0),
        "w_ada": normal_values(seeds[2], (D, 6, D), (D // 4) ** -0.5, 0.375, ((2, 4),)),
        "b_ada": normal_values(seeds[3], (6, D), 0.3, 1.75, ((1, 4),)),
        "w_qkv": normal_values(seeds[4], (D, 3, D), D ** -0.5, 0.1875, ((2, 4),)),
        "b_qkv": normal_values(seeds[5], (3, D), 0.3, 1.75, ((1, 4),)),
        "w_out": normal_values(seeds[6], (D, D), (D // 16) ** -0.5, 0.75, ((0, 4),)),
        "b_out": normal_values(seeds[7], (D,), 0.3, 1.75),
        "w_fc1": normal_values(seeds[8], (D, FF), D ** -0.5, 0.1875, ((1, 4),)),
        "b_fc1": normal_values(seeds[9], (FF,), 0.3, 1.75, ((0, 4),)),
        "w_fc2": normal_values(seeds[10], (FF, D), FF ** -0.5, 0.09375, ((0, 4),)),
        "b_fc2": normal_values(seeds[11], (D,), 0.3, 1.75),
        "cotangent": normal_values(seeds[12], (CLIPS, FRAMES, PATCHES, D), 1.0, 6.0, ((0, 2), (1, 4), (2, 4))),
    }


@jax.custom_vjp
def low(v):
    return lax.optimization_barrier(v.astype(jnp.bfloat16)).astype(jnp.float32)

@jax.custom_vjp
def low_back(v):
    return v

def low_keep(v):
    return (low(v), None)

def low_pass(kept, grad):
    return (grad,)

def back_keep(v):
    return (v, None)

def back_low(kept, grad):
    return (low(grad),)
low.defvjp(low_keep, low_pass)
low_back.defvjp(back_keep, back_low)
epsilon = 1e-06

def frequencies(count):
    return 10000.0 ** (-(jnp.arange(count, dtype=jnp.float32) / count))

def rotate_half(segment, position):
    half = segment.shape[-1] // 2
    angle = position[..., None] * frequencies(half)
    cosine = jnp.cos(angle)
    sine = jnp.sin(angle)
    first = segment[..., :half]
    second = segment[..., half:]
    return jnp.concatenate([first * cosine - second * sine, first * sine + second * cosine], axis=-1)

def rotary(vector, frame_pos, row_pos, col_pos):
    width = vector.shape[-1]
    first = width // 4
    middle = (width - first) // 2
    return jnp.concatenate([rotate_half(vector[..., :first], frame_pos), rotate_half(vector[..., first:first + middle], row_pos), rotate_half(vector[..., first + middle:], col_pos)], axis=-1)

def embedding(level, width):
    half = width // 2
    angle = 1000.0 * level[..., None] * frequencies(half)
    return jnp.concatenate([jnp.cos(angle), jnp.sin(angle)], axis=-1)

def normalize(value):
    center = value - lax.optimization_barrier(jnp.mean(value, axis=-1, keepdims=True))
    spread = lax.optimization_barrier(jnp.mean(center * center, axis=-1, keepdims=True))
    return center * lax.rsqrt(spread + epsilon)

def attend_head(inputs):
    query_head, key_head, value_head = inputs
    highest = lax.Precision.HIGHEST
    scores = low_back(jnp.dot(query_head, key_head.T, precision=highest)) * HD ** (-0.5)
    frame_ids = jnp.arange(FRAMES * PATCHES) // PATCHES
    allowed = frame_ids[:, None] >= frame_ids[None, :]
    scores = jnp.where(allowed, scores, -1e+30)
    row_max = lax.optimization_barrier(jnp.max(scores, axis=-1, keepdims=True))
    exp_scores = jnp.exp(scores - row_max)
    prob_map = exp_scores / lax.optimization_barrier(jnp.sum(exp_scores, axis=-1, keepdims=True))
    return jnp.dot(low(prob_map), value_head, precision=highest)

def layer_step(level, resid_in, w_ada, b_ada, w_qkv, b_qkv, w_out, b_out, w_fc1, b_fc1, w_fc2, b_fc2):
    highest = lax.Precision.HIGHEST
    width = resid_in.shape[-1]
    condition = low(jax.nn.silu(embedding(level, width)))
    modulation = jnp.einsum('fd,dke->fke', condition, w_ada, precision=highest) + b_ada
    pieces = [modulation[:, slot][:, None, :] for slot in range(6)]
    attn_in = low(normalize(resid_in) * (1.0 + pieces[1]) + pieces[0])
    projected = low_back(jnp.einsum('fpd,dke->fpke', attn_in, w_qkv, precision=highest) + b_qkv)
    projected = projected.reshape(FRAMES, PATCHES, 3, HEADS, HD)
    frame_pos = jnp.arange(FRAMES, dtype=jnp.float32).reshape(FRAMES, 1, 1)
    patch_ids = jnp.arange(PATCHES)
    row_pos = (patch_ids // GRID).astype(jnp.float32).reshape(1, PATCHES, 1)
    col_pos = (patch_ids % GRID).astype(jnp.float32).reshape(1, PATCHES, 1)
    queries = low(rotary(projected[:, :, 0], frame_pos, row_pos, col_pos))
    keys = low(rotary(projected[:, :, 1], frame_pos, row_pos, col_pos))
    values = low(projected[:, :, 2])
    length = FRAMES * PATCHES

    def by_heads(array):
        return array.reshape(length, HEADS, HD).transpose(1, 0, 2)
    mixed = lax.map(jax.checkpoint(attend_head), (by_heads(queries), by_heads(keys), by_heads(values)))
    mixed = mixed.transpose(1, 0, 2).reshape(FRAMES, PATCHES, width)
    mixed = low_back(low(mixed))
    attn_branch = low_back(jnp.einsum('fpj,jd->fpd', mixed, w_out, precision=highest) + b_out)
    resid_one = resid_in + pieces[2] * attn_branch
    mlp_in = low(normalize(resid_one) * (1.0 + pieces[4]) + pieces[3])
    pre_act = low_back(jnp.einsum('fpd,dj->fpj', mlp_in, w_fc1, precision=highest) + b_fc1)
    activated = low(jax.nn.gelu(pre_act, approximate=True))
    mlp_branch = low_back(jnp.einsum('fpj,jd->fpd', activated, w_fc2, precision=highest) + b_fc2)
    return resid_one + pieces[5] * mlp_branch

def reference(tokens, noise_level, w_ada, b_ada, w_qkv, b_qkv, w_out, b_out, w_fc1, b_fc1, w_fc2, b_fc2, cotangent):
    weights = tuple((item.astype(jnp.float32) for item in (w_ada, b_ada, w_qkv, b_qkv, w_out, b_out, w_fc1, b_fc1, w_fc2, b_fc2)))
    totals = tuple((jnp.zeros_like(item) for item in weights))

    def clip_step(running, inputs):
        tokens_clip, level_clip, cot_clip = inputs

        def on_clip(resid_in, *params):
            return layer_step(level_clip, resid_in, *params)
        out_clip, pull = jax.vjp(on_clip, tokens_clip.astype(jnp.float32), *weights)
        grads = pull(cot_clip.astype(jnp.float32))
        running = tuple((left + right for left, right in zip(running, grads[1:])))
        return (running, (out_clip.astype(jnp.bfloat16), grads[0]))
    totals, (output, tokens_grad) = lax.scan(clip_step, totals, (tokens, noise_level, cotangent))
    return (output, tokens_grad, totals[0], totals[1], totals[2], totals[3], totals[4], totals[5], totals[6], totals[7], totals[8], totals[9])
```

```python
from functools import partial
import math

import jax
import jax.numpy as jnp
import numpy as np
from jax import lax
from jax.experimental import pallas as pl
from jax.experimental.pallas import tpu as pltpu
from jax.sharding import PartitionSpec as P

HD = 64
GRID = 16
PATCHES = 256


epsilon = 1e-06


def frequencies(count):
    return 10000.0 ** (-(jnp.arange(count, dtype=jnp.float32) / count))


def rotate_half(segment, position):
    half = segment.shape[-1] // 2
    angle = position[..., None] * frequencies(half)
    cosine = jnp.cos(angle)
    sine = jnp.sin(angle)
    first = segment[..., :half]
    second = segment[..., half:]
    return jnp.concatenate(
        [first * cosine - second * sine, first * sine + second * cosine], axis=-1
    )


def rotary(vector, frame_pos, row_pos, col_pos):
    width = vector.shape[-1]
    first = width // 4
    middle = (width - first) // 2
    return jnp.concatenate(
        [
            rotate_half(vector[..., :first], frame_pos),
            rotate_half(vector[..., first : first + middle], row_pos),
            rotate_half(vector[..., first + middle :], col_pos),
        ],
        axis=-1,
    )


def embedding(level, width):
    half = width // 2
    angle = 1000.0 * level[..., None] * frequencies(half)
    return jnp.concatenate([jnp.cos(angle), jnp.sin(angle)], axis=-1)


def normalize(value):
    center = value - jnp.mean(value, axis=-1, keepdims=True)
    spread = jnp.mean(center * center, axis=-1, keepdims=True)
    return center * lax.rsqrt(spread + epsilon)


def modulate(value, shift, scale):
    return normalize(value) * (1.0 + scale) + shift


def general_body(
    tokens,
    noise_level,
    w_ada,
    b_ada,
    w_qkv,
    b_qkv,
    w_out,
    b_out,
    w_fc1,
    b_fc1,
    w_fc2,
    b_fc2,
    cotangent,
):
    clips = tokens.shape[0]
    width = tokens.shape[3]
    head_cols = w_qkv.shape[2]
    heads_here = head_cols // HD
    frames = lax.axis_size("frame")
    frame_now = lax.axis_index("frame")
    scale = 1.0 / math.sqrt(HD)
    condition = jax.nn.silu(embedding(noise_level, width)).astype(jnp.bfloat16)
    mod_part = jnp.einsum(
        "cfd,dke->cfke", condition, w_ada, preferred_element_type=jnp.float32
    ) + b_ada.astype(jnp.float32)
    modulation = lax.all_gather(mod_part, "tensor", axis=3, tiled=True)
    pieces = [modulation[:, :, slot : slot + 1, :] for slot in range(6)]
    resid_in = tokens.astype(jnp.float32)
    attn_val, ln_one_back = jax.vjp(modulate, resid_in, pieces[0], pieces[1])
    attn_rows = lax.all_gather(attn_val.astype(jnp.bfloat16), "tensor", axis=2, tiled=True)
    projected = jnp.einsum(
        "cfpd,dke->cfpke", attn_rows, w_qkv, preferred_element_type=jnp.float32
    ) + b_qkv.astype(jnp.float32)
    projected = projected[:, 0]
    patch_ids = jnp.arange(PATCHES)
    row_pos = (patch_ids // GRID).astype(jnp.float32)[:, None]
    col_pos = (patch_ids % GRID).astype(jnp.float32)[:, None]
    frame_pos = frame_now.astype(jnp.float32)

    def turned(vector):
        return rotary(vector.reshape(clips, PATCHES, heads_here, HD), frame_pos, row_pos, col_pos)

    query_rot, query_back = jax.vjp(turned, projected[:, :, 0])
    key_rot, key_back = jax.vjp(turned, projected[:, :, 1])
    queries = query_rot.astype(jnp.bfloat16).reshape(clips, PATCHES, head_cols)
    keys_here = key_rot.astype(jnp.bfloat16).reshape(clips, PATCHES, head_cols)
    values_here = projected[:, :, 2].astype(jnp.bfloat16)
    kv_own = jnp.concatenate([keys_here, values_here], axis=-1)[:, None]
    allowed = jnp.arange(frames * PATCHES) // PATCHES <= frame_now
    kv_all = lax.all_gather(kv_own, "frame", axis=1, tiled=True)

    def fetch(index):
        return lax.dynamic_index_in_dim(kv_all, index, 0, False)

    def score_block(query_clip, kv_clip):
        keys = kv_clip[..., :head_cols].reshape(frames * PATCHES, heads_here, HD)
        values = kv_clip[..., head_cols:].reshape(frames * PATCHES, heads_here, HD)
        scores = (
            jnp.einsum(
                "qhd,khd->hqk",
                query_clip.reshape(PATCHES, heads_here, HD),
                keys,
                preferred_element_type=jnp.float32,
            )
            * scale
        )
        return (jnp.where(allowed[None, None, :], scores, -1e30), keys, values)

    def forward_step(carry, index):
        query_clip = lax.dynamic_index_in_dim(queries, index, 0, False)
        scores, keys, values = score_block(query_clip, fetch(index))
        row_max = jnp.max(scores, axis=-1, keepdims=True)
        exp_scores = jnp.exp(scores - row_max)
        row_sum = jnp.sum(exp_scores, axis=-1, keepdims=True)
        prob_map = exp_scores / row_sum
        mixed = jnp.einsum(
            "hqk,khd->qhd",
            prob_map.astype(jnp.bfloat16),
            values,
            preferred_element_type=jnp.float32,
        ).reshape(PATCHES, head_cols)
        return (carry, (mixed, (row_max + jnp.log(row_sum))[..., 0]))

    _, (mixed_all, log_sums) = lax.scan(forward_step, None, jnp.arange(clips))
    mixed_low = mixed_all.astype(jnp.bfloat16)
    attn_term = jnp.einsum("cpj,jd->cpd", mixed_low, w_out, preferred_element_type=jnp.float32)[
        :, None
    ]
    attn_branch = lax.psum_scatter(
        attn_term, "tensor", scatter_dimension=2, tiled=True
    ) + b_out.astype(jnp.float32)
    resid_one = resid_in + pieces[2] * attn_branch
    mlp_val, ln_two_back = jax.vjp(modulate, resid_one, pieces[3], pieces[4])
    mlp_rows = lax.all_gather(mlp_val.astype(jnp.bfloat16), "tensor", axis=2, tiled=True)
    pre_act = jnp.einsum(
        "cfpd,dj->cfpj", mlp_rows, w_fc1, preferred_element_type=jnp.float32
    ) + b_fc1.astype(jnp.float32)
    act_val, gelu_back = jax.vjp(partial(jax.nn.gelu, approximate=True), pre_act)
    activated = act_val.astype(jnp.bfloat16)
    mlp_term = jnp.einsum("cfpj,jd->cfpd", activated, w_fc2, preferred_element_type=jnp.float32)
    mlp_branch = lax.psum_scatter(
        mlp_term, "tensor", scatter_dimension=2, tiled=True
    ) + b_fc2.astype(jnp.float32)
    output = (resid_one + pieces[5] * mlp_branch).astype(jnp.bfloat16)
    upstream = cotangent.astype(jnp.float32)
    mlp_grad = (pieces[5] * upstream).astype(jnp.bfloat16)
    gate_two_grad = jnp.sum(upstream * mlp_branch, axis=2, keepdims=True)
    mlp_grad_rows = lax.all_gather(mlp_grad, "tensor", axis=2, tiled=True)
    fc2_grad = jnp.einsum(
        "cfpj,cfpd->jd", activated, mlp_grad_rows, preferred_element_type=jnp.float32
    )
    fc2_bias_grad = jnp.sum(mlp_grad_rows.astype(jnp.float32), axis=(0, 1, 2))
    act_grad = jnp.einsum("cfpd,jd->cfpj", mlp_grad_rows, w_fc2, preferred_element_type=jnp.float32)
    pre_grad = gelu_back(act_grad)[0].astype(jnp.bfloat16)
    fc1_grad = jnp.einsum("cfpd,cfpj->dj", mlp_rows, pre_grad, preferred_element_type=jnp.float32)
    fc1_bias_grad = jnp.sum(pre_grad.astype(jnp.float32), axis=(0, 1, 2))
    mlp_in_term = jnp.einsum("cfpj,dj->cfpd", pre_grad, w_fc1, preferred_element_type=jnp.float32)
    mlp_in_grad = lax.psum_scatter(mlp_in_term, "tensor", scatter_dimension=2, tiled=True)
    resid_part, shift_two_grad, scale_two_grad = ln_two_back(mlp_in_grad)
    resid_grad = upstream + resid_part
    attn_grad = (pieces[2] * resid_grad).astype(jnp.bfloat16)
    gate_one_grad = jnp.sum(resid_grad * attn_branch, axis=2, keepdims=True)
    attn_grad_rows = lax.all_gather(attn_grad, "tensor", axis=2, tiled=True)[:, 0]
    out_grad = jnp.einsum(
        "cpj,cpd->jd", mixed_low, attn_grad_rows, preferred_element_type=jnp.float32
    )
    out_bias_grad = jnp.sum(attn_grad_rows.astype(jnp.float32), axis=(0, 1))
    mixed_grad = jnp.einsum(
        "cpd,jd->cpj", attn_grad_rows, w_out, preferred_element_type=jnp.float32
    ).astype(jnp.bfloat16)

    def query_side(index):
        query_clip = lax.dynamic_index_in_dim(queries, index, 0, False)
        grad_clip = lax.dynamic_index_in_dim(mixed_grad, index, 0, False)
        lse_clip = lax.dynamic_index_in_dim(log_sums, index, 0, False)
        scores, keys, values = score_block(query_clip, fetch(index))
        prob_map = jnp.exp(scores - lse_clip[..., None])
        grad_heads = grad_clip.reshape(PATCHES, heads_here, HD)
        prob_grad = jnp.einsum(
            "qhd,khd->hqk", grad_heads, values, preferred_element_type=jnp.float32
        )
        row_dot = jnp.sum(prob_map * prob_grad, axis=-1, keepdims=True)
        score_grad = (scale * prob_map * (prob_grad - row_dot)).astype(jnp.bfloat16)
        query_grad = jnp.einsum(
            "hqk,khd->qhd", score_grad, keys, preferred_element_type=jnp.float32
        ).reshape(PATCHES, head_cols)
        return (query_clip, grad_heads, prob_map, score_grad, row_dot, query_grad)

    def backward_step(carry, index):
        query_clip, grad_heads, prob_map, score_grad, row_dot, query_grad = query_side(index)
        key_grad = jnp.einsum(
            "hqk,qhd->khd",
            score_grad,
            query_clip.reshape(PATCHES, heads_here, HD),
            preferred_element_type=jnp.float32,
        ).reshape(frames, PATCHES, head_cols)
        value_grad = jnp.einsum(
            "hqk,qhd->khd",
            prob_map.astype(jnp.bfloat16),
            grad_heads,
            preferred_element_type=jnp.float32,
        ).reshape(frames, PATCHES, head_cols)
        owned = lax.psum_scatter(
            jnp.concatenate([key_grad, value_grad], axis=-1),
            "frame",
            scatter_dimension=0,
            tiled=True,
        )
        return (carry, (query_grad, owned[0]))

    _, (query_grads, kv_grads) = lax.scan(backward_step, None, jnp.arange(clips))
    query_raw_grad = query_back(query_grads.reshape(clips, PATCHES, heads_here, HD))[0]
    key_raw_grad = key_back(kv_grads[..., :head_cols].reshape(clips, PATCHES, heads_here, HD))[0]
    projected_grad = jnp.stack([query_raw_grad, key_raw_grad, kv_grads[..., head_cols:]], axis=2)
    projected_grad = projected_grad.astype(jnp.bfloat16)[:, None]
    qkv_grad = jnp.einsum(
        "cfpd,cfpke->dke", attn_rows, projected_grad, preferred_element_type=jnp.float32
    )
    qkv_bias_grad = jnp.sum(projected_grad.astype(jnp.float32), axis=(0, 1, 2))
    attn_in_term = jnp.einsum(
        "cfpke,dke->cfpd", projected_grad, w_qkv, preferred_element_type=jnp.float32
    )
    attn_in_grad = lax.psum_scatter(attn_in_term, "tensor", scatter_dimension=2, tiled=True)
    input_part, shift_one_grad, scale_one_grad = ln_one_back(attn_in_grad)
    tokens_grad = resid_grad + input_part
    mod_grad_part = jnp.concatenate(
        [
            shift_one_grad,
            scale_one_grad,
            gate_one_grad,
            shift_two_grad,
            scale_two_grad,
            gate_two_grad,
        ],
        axis=2,
    )
    mod_grad = lax.psum_scatter(mod_grad_part, "tensor", scatter_dimension=3, tiled=True)
    ada_grad = jnp.einsum(
        "cfd,cfke->dke", condition.astype(jnp.float32), mod_grad, precision=lax.Precision.HIGHEST
    )
    ada_bias_grad = jnp.sum(mod_grad, axis=(0, 1))
    summed = lax.psum(
        (
            ada_grad,
            ada_bias_grad,
            qkv_grad,
            qkv_bias_grad,
            out_grad,
            out_bias_grad,
            fc1_grad,
            fc1_bias_grad,
            fc2_grad,
            fc2_bias_grad,
        ),
        ("batch", "frame"),
    )
    return (
        output,
        tokens_grad,
        summed[0],
        summed[1],
        summed[2],
        summed[3],
        summed[4],
        summed[5],
        summed[6],
        summed[7],
        summed[8],
        summed[9],
    )


MIB = 1 << 20


def rotary_tables(core, frames):
    quarter = PATCHES // 4
    inner = np.arange(quarter)
    patch = np.zeros((2, 2, 2, quarter), np.int64)
    for own in range(2):
        for side in range(2):
            for far in range(2):
                patch[own, side, far] = (2 * far + (own ^ side)) * quarter + inner
    patch = patch.reshape(2, PATCHES)
    lane = np.arange(HD)
    first, middle = HD // 4, (HD - HD // 4) // 2
    bounds = [(0, first), (first, middle), (first + middle, HD - first - middle)]
    freq = np.zeros(HD, np.float32)
    sign_up = np.zeros((2, HD), np.float32)
    sign_down = np.zeros((2, HD), np.float32)
    which = np.zeros(HD, np.int64)
    for slot, (start, width) in enumerate(bounds):
        half = width // 2
        ladder = 10000.0 ** (-(np.arange(half, dtype=np.float32) / np.float32(half)))
        freq[start : start + half] = ladder
        freq[start + half : start + width] = ladder
        which[start : start + width] = slot
        kind = 0 if slot == 0 else 1
        sign_up[kind, start : start + half] = -1.0
        sign_down[kind, start + half : start + width] = 1.0
    del lane
    frame_pos = jnp.arange(frames, dtype=jnp.float32)[:, None]
    mine = jnp.asarray(patch)[core]
    row_pos = (mine // GRID).astype(jnp.float32)[None, :]
    col_pos = (mine % GRID).astype(jnp.float32)[None, :]
    shape = (frames, PATCHES)
    spots = jnp.stack(
        [jnp.broadcast_to(item, shape) for item in (frame_pos, row_pos, col_pos)]
    ).reshape(3, frames * PATCHES)
    angle = spots[which].T * jnp.asarray(freq)[None, :]
    cosine, sine = jnp.cos(angle), jnp.sin(angle)
    parts = [cosine]
    for kind in range(2):
        parts.append(sine * sign_up[kind])
        parts.append(sine * sign_down[kind])
    return jnp.stack([jnp.tile(item, (1, 2)) for item in parts])


def turn(value, tables, sign):
    lanes = value.shape[-1]
    near, far = HD // 8, (HD - HD // 4) // 4
    moved = (
        pltpu.roll(value, lanes - near, 1) * tables(1)
        + pltpu.roll(value, near, 1) * tables(2)
        + pltpu.roll(value, lanes - far, 1) * tables(3)
        + pltpu.roll(value, far, 1) * tables(4)
    )
    return value * tables(0) + (moved if sign > 0 else -moved)


def qkv_kernel(rows_ref, w_ref, b_ref, tab_ref, out_ref):
    step = pl.program_id(0)
    block = PATCHES
    for start in range(0, rows_ref.shape[0], block):
        here = pl.ds(start, block)
        value = (
            jnp.dot(rows_ref[here, :], w_ref[...], preferred_element_type=jnp.float32)
            + b_ref[0].astype(jnp.float32)
        )

        @pl.when(step < 2)
        def _():
            for lane in range(0, value.shape[1], 128):
                out_ref[0, here, lane : lane + 128] = turn(
                    value[:, lane : lane + 128], lambda slot: tab_ref[slot, here, :], 1
                ).astype(jnp.bfloat16)

        @pl.when(step == 2)
        def _():
            out_ref[0, here, :] = value.astype(jnp.bfloat16)


def qkv_forward(rows, w, b, tables):
    count, width = rows.shape
    cols = w.shape[1] // 3
    return pl.pallas_call(
        qkv_kernel,
        grid=(3,),
        in_specs=[
            pl.BlockSpec((count, width), lambda i: (0, 0)),
            pl.BlockSpec((width, cols), lambda i: (0, i)),
            pl.BlockSpec((1, 1, cols), lambda i: (i, 0, 0)),
            pl.BlockSpec(tables.shape, lambda i: (0, 0, 0)),
        ],
        out_specs=pl.BlockSpec((1, count, cols), lambda i: (i, 0, 0)),
        out_shape=jax.ShapeDtypeStruct((3, count, cols), jnp.bfloat16),
        compiler_params=pltpu.CompilerParams(vmem_limit_bytes=48 * MIB),
        cost_estimate=pl.CostEstimate(
            flops=2 * count * width * cols * 3, bytes_accessed=12 * MIB, transcendentals=0
        ),
        name="qkv_forward",
    )(rows, w, b[:, None, :], tables)


def attend_kernel(frames, qkv_ref, out_ref, lse_ref):
    lanes = qkv_ref.shape[2]
    low_lane = lax.broadcasted_iota(jnp.int32, (PATCHES, lanes), 1) < HD
    for frame in range(frames):
        here = pl.ds(frame * PATCHES, PATCHES)
        length = (frame + 1) * PATCHES
        query = qkv_ref[0, here, :] * jnp.bfloat16(1.0 / math.sqrt(HD))
        keys = qkv_ref[1, :length, :]
        values = qkv_ref[2, :length, :]
        outs, sums = [], []
        for head in range(2):
            chosen = low_lane if head == 0 else jnp.logical_not(low_lane)
            scores = lax.dot_general(
                jnp.where(chosen, query, jnp.bfloat16(0)),
                keys,
                (((1,), (1,)), ((), ())),
                preferred_element_type=jnp.float32,
            )
            top = jnp.max(scores, axis=1, keepdims=True)
            grown = jnp.exp(scores - top)
            total = jnp.sum(grown, axis=1, keepdims=True)
            prob = (grown * (1.0 / total)).astype(jnp.bfloat16)
            outs.append(jnp.dot(prob, values, preferred_element_type=jnp.float32))
            sums.append(top + jnp.log(total))
        out_ref[here, :] = jnp.where(low_lane, outs[0], outs[1]).astype(jnp.bfloat16)
        lse_ref[0, here, :] = jnp.concatenate(sums, axis=1)


def attend(qkv, frames):
    _, count, cols = qkv.shape
    pairs = cols // 128
    return pl.pallas_call(
        partial(attend_kernel, frames),
        grid=(pairs,),
        in_specs=[pl.BlockSpec((3, count, 128), lambda i: (0, 0, i))],
        out_specs=[
            pl.BlockSpec((count, 128), lambda i: (0, i)),
            pl.BlockSpec((1, count, 2), lambda i: (i, 0, 0)),
        ],
        out_shape=[
            jax.ShapeDtypeStruct((count, cols), jnp.bfloat16),
            jax.ShapeDtypeStruct((pairs, count, 2), jnp.float32),
        ],
        compiler_params=pltpu.CompilerParams(vmem_limit_bytes=48 * MIB),
        cost_estimate=pl.CostEstimate(
            flops=12_000_000_000, bytes_accessed=4 * MIB, transcendentals=2_600_000
        ),
        name="attend",
    )(qkv)


def attend_back_kernel(frames, qkv_ref, grad_ref, lse_ref, tab_ref, out_ref, dk_ref, dv_ref):
    lanes = qkv_ref.shape[2]
    low_lane = lax.broadcasted_iota(jnp.int32, (PATCHES, lanes), 1) < HD
    scale = 1.0 / math.sqrt(HD)
    zero = jnp.bfloat16(0)
    dk_ref[...] = jnp.zeros_like(dk_ref)
    dv_ref[...] = jnp.zeros_like(dv_ref)
    for frame in range(frames):
        here = pl.ds(frame * PATCHES, PATCHES)
        length = (frame + 1) * PATCHES
        query = qkv_ref[0, here, :]
        grad = grad_ref[here, :]
        keys = qkv_ref[1, :length, :]
        values = qkv_ref[2, :length, :]
        outs = []
        for head in range(2):
            chosen = low_lane if head == 0 else jnp.logical_not(low_lane)
            query_head = jnp.where(chosen, query, zero)
            grad_head = jnp.where(chosen, grad, zero)
            scores = lax.dot_general(
                query_head * jnp.bfloat16(scale),
                keys,
                (((1,), (1,)), ((), ())),
                preferred_element_type=jnp.float32,
            )
            prob = jnp.exp(scores - lse_ref[0, here, head : head + 1])
            prob_grad = lax.dot_general(
                grad_head, values, (((1,), (1,)), ((), ())), preferred_element_type=jnp.float32
            )
            row_dot = jnp.sum(prob * prob_grad, axis=1, keepdims=True)
            score_grad = (prob * ((prob_grad - row_dot) * scale)).astype(jnp.bfloat16)
            outs.append(jnp.dot(score_grad, keys, preferred_element_type=jnp.float32))
            dk_ref[:length, :] += lax.dot_general(
                score_grad,
                query_head,
                (((0,), (0,)), ((), ())),
                preferred_element_type=jnp.float32,
            )
            dv_ref[:length, :] += lax.dot_general(
                prob.astype(jnp.bfloat16),
                grad_head,
                (((0,), (0,)), ((), ())),
                preferred_element_type=jnp.float32,
            )
        out_ref[0, here, :] = turn(
            jnp.where(low_lane, outs[0], outs[1]), lambda slot: tab_ref[slot, here, :], -1
        ).astype(jnp.bfloat16)
    out_ref[1] = turn(dk_ref[...], lambda slot: tab_ref[slot], -1).astype(jnp.bfloat16)
    out_ref[2] = dv_ref[...].astype(jnp.bfloat16)


def attend_back(qkv, grad, lse, tables, frames):
    _, count, cols = qkv.shape
    pairs = cols // 128
    return pl.pallas_call(
        partial(attend_back_kernel, frames),
        grid=(pairs,),
        in_specs=[
            pl.BlockSpec((3, count, 128), lambda i: (0, 0, i)),
            pl.BlockSpec((count, 128), lambda i: (0, i)),
            pl.BlockSpec((1, count, 2), lambda i: (i, 0, 0)),
            pl.BlockSpec(tables.shape, lambda i: (0, 0, 0)),
        ],
        out_specs=pl.BlockSpec((3, count, 128), lambda i: (0, 0, i)),
        out_shape=jax.ShapeDtypeStruct((3, count, cols), jnp.bfloat16),
        scratch_shapes=[
            pltpu.VMEM((count, 128), jnp.float32),
            pltpu.VMEM((count, 128), jnp.float32),
        ],
        compiler_params=pltpu.CompilerParams(vmem_limit_bytes=48 * MIB),
        cost_estimate=pl.CostEstimate(
            flops=24_000_000_000, bytes_accessed=6 * MIB, transcendentals=2_600_000
        ),
        name="attend_back",
    )(qkv, grad, lse, tables)


def fast_body(
    tokens,
    noise_level,
    w_ada,
    b_ada,
    w_qkv,
    b_qkv,
    w_out,
    b_out,
    w_fc1,
    b_fc1,
    w_fc2,
    b_fc2,
    cotangent,
):
    clips, _, quarter, width = tokens.shape
    frames = lax.axis_size("frame")
    cols = w_qkv.shape[2]
    batch_now = lax.axis_index("batch")
    frame_now = lax.axis_index("frame")
    tensor_now = lax.axis_index("tensor")
    core = tensor_now % 2
    far = tensor_now // 2
    clip_now = frame_now * 2 + far
    rows_own = clips * quarter
    count = 2 * rows_own
    f32 = jnp.float32
    bf16 = jnp.bfloat16
    groups = [
        [f * 4 + 2 * y + c for f in range(frames) for y in range(2)] for c in range(2)
    ]

    def to_clip(item):
        return lax.all_to_all(item, ("frame", "tensor"), 0, 0, axis_index_groups=groups)

    def swap_y(item):
        return lax.ppermute(item, "tensor", [(t, t ^ 2) for t in range(4)])

    def swap_core(item):
        return lax.ppermute(item, "tensor", [(t, t ^ 1) for t in range(4)])

    def swap_x(item):
        return lax.ppermute(item, "batch", [(0, 1), (1, 0)])

    def swap_z(item, bit):
        return lax.ppermute(item, "frame", [(f, f ^ bit) for f in range(frames)])

    def ordered(mine, theirs, place):
        return jnp.stack(
            [jnp.where(place == 0, mine, theirs), jnp.where(place == 0, theirs, mine)]
        )

    def both_cores(item):
        return jnp.concatenate([item, swap_core(item)], axis=1).reshape(count, width)

    def sum_cores(term):
        split = term.reshape(frames, 2, rows_own // frames, width)
        return split[:, 0] + swap_core(split[:, 1])

    tables = rotary_tables(core, frames)
    condition = jax.nn.silu(embedding(noise_level, width)).astype(bf16)
    mod_part = jnp.einsum(
        "cfd,dke->cfke", condition, w_ada, preferred_element_type=f32
    ) + b_ada.astype(f32)
    tokens_own = to_clip(tokens[:, 0]).reshape(frames, 2 * quarter, width)
    mod_own = to_clip(mod_part[:, 0]).reshape(frames, 2, 6, cols)
    modulation = ordered(mod_own, swap_core(mod_own), core)
    modulation = modulation.transpose(1, 3, 2, 0, 4).reshape(frames, 6, width)
    pieces = [modulation[:, slot : slot + 1, :] for slot in range(6)]
    w_qkv_own = w_qkv.reshape(width, 3 * cols)
    w_qkv_far = swap_y(w_qkv_own)
    b_qkv_far = swap_y(b_qkv)
    b_fc1_far = swap_y(b_fc1)
    w_out_far = swap_y(w_out)
    w_fc1_far = swap_y(w_fc1)
    w_fc2_far = swap_y(w_fc2)
    cot_own = to_clip(cotangent[:, 0]).reshape(frames, 2 * quarter, width)

    resid_in = tokens_own.astype(f32)
    attn_val, ln_one_back = jax.vjp(modulate, resid_in, pieces[0], pieces[1])
    attn_rows = both_cores(attn_val.astype(bf16))
    qkv_own = qkv_forward(attn_rows, w_qkv_own, b_qkv, tables)
    mixed_own, lse_own = attend(qkv_own, frames)
    qkv_far = qkv_forward(attn_rows, w_qkv_far, b_qkv_far, tables)
    mixed_far, lse_far = attend(qkv_far, frames)
    attn_term = jnp.dot(mixed_own, w_out, preferred_element_type=f32) + jnp.dot(
        mixed_far, w_out_far, preferred_element_type=f32
    )
    attn_branch = sum_cores(attn_term) + b_out.astype(f32)
    resid_one = resid_in + pieces[2] * attn_branch
    mlp_val, ln_two_back = jax.vjp(modulate, resid_one, pieces[3], pieces[4])
    mlp_rows = both_cores(mlp_val.astype(bf16))

    upstream = cot_own.astype(f32)
    mlp_grad = (pieces[5] * upstream).astype(bf16)
    mlp_grad_rows = both_cores(mlp_grad)

    def hidden(w_one, b_one, w_two):
        pre_act = jnp.dot(mlp_rows, w_one, preferred_element_type=f32) + b_one.astype(f32)
        act_val, gelu_back = jax.vjp(partial(jax.nn.gelu, approximate=True), pre_act)
        activated = act_val.astype(bf16)
        mlp_term = jnp.dot(activated, w_two, preferred_element_type=f32)
        act_grad = lax.dot_general(
            mlp_grad_rows, w_two, (((1,), (1,)), ((), ())), preferred_element_type=f32
        )
        pre_grad = gelu_back(act_grad)[0].astype(bf16)
        in_term = lax.dot_general(
            pre_grad, w_one, (((1,), (1,)), ((), ())), preferred_element_type=f32
        )
        two_grad = lax.dot_general(
            activated, mlp_grad_rows, (((0,), (0,)), ((), ())), preferred_element_type=f32
        )
        one_grad = lax.dot_general(
            mlp_rows, pre_grad, (((0,), (0,)), ((), ())), preferred_element_type=f32
        )
        bias_grad = jnp.sum(pre_grad.astype(f32), axis=0)
        return mlp_term, in_term, one_grad, two_grad, bias_grad

    term_own, in_own, fc1_own, fc2_own, fc1_bias_own = hidden(w_fc1, b_fc1, w_fc2)
    term_far, in_far, fc1_far, fc2_far, fc1_bias_far = hidden(w_fc1_far, b_fc1_far, w_fc2_far)
    mlp_in_grad = sum_cores(in_own + in_far)
    mlp_branch = sum_cores(term_own + term_far) + b_fc2.astype(f32)
    output_own = (resid_one + pieces[5] * mlp_branch).astype(bf16)
    gate_two_grad = jnp.sum(upstream * mlp_branch, axis=1, keepdims=True)
    fc2_bias_part = jnp.sum(mlp_grad.astype(f32), axis=(0, 1))

    def over_xz(total):
        rows, lanes = total.shape
        low_bit, high_bit = frame_now % 2, frame_now // 2

        def halve(item, place, send):
            split = item.reshape(2, item.shape[0] // 2, lanes)
            keep = lax.dynamic_index_in_dim(split, place, 0, False)
            away = lax.dynamic_index_in_dim(split, 1 - place, 0, False)
            return keep + send(away.astype(bf16)).astype(f32)

        def join(item, place, send):
            return ordered(item, send(item), place).reshape(2 * item.shape[0], lanes)

        part = halve(total, batch_now, swap_x)
        part = halve(part, low_bit, lambda item: swap_z(item, 1))
        part = halve(part, high_bit, lambda item: swap_z(item, 2)).astype(bf16)
        part = join(part, high_bit, lambda item: swap_z(item, 2))
        part = join(part, low_bit, lambda item: swap_z(item, 1))
        return join(part, batch_now, swap_x).astype(f32)

    def reduced(own, other):
        return over_xz(own + swap_y(other.astype(bf16)).astype(f32))

    fc2_grad = reduced(fc2_own, fc2_far)
    fc1_grad = reduced(fc1_own, fc1_far)

    resid_part, shift_two_grad, scale_two_grad = ln_two_back(mlp_in_grad)
    resid_grad = upstream + resid_part
    attn_grad = (pieces[2] * resid_grad).astype(bf16)
    gate_one_grad = jnp.sum(resid_grad * attn_branch, axis=1, keepdims=True)
    out_bias_part = jnp.sum(attn_grad.astype(f32), axis=(0, 1))
    attn_grad_rows = both_cores(attn_grad)

    def heads_back(w, qkv, mixed, lse, w_in):
        mixed_grad = lax.dot_general(
            attn_grad_rows, w, (((1,), (1,)), ((), ())), preferred_element_type=f32
        ).astype(bf16)
        out_grad = lax.dot_general(
            mixed, attn_grad_rows, (((0,), (0,)), ((), ())), preferred_element_type=f32
        )
        back = attend_back(qkv, mixed_grad, lse, tables, frames)
        back = back.transpose(1, 0, 2).reshape(count, 3 * cols)
        qkv_grad = lax.dot_general(
            attn_rows, back, (((0,), (0,)), ((), ())), preferred_element_type=f32
        )
        in_term = lax.dot_general(
            back, w_in, (((1,), (1,)), ((), ())), preferred_element_type=f32
        )
        return out_grad, qkv_grad, jnp.sum(back.astype(f32), axis=0), in_term

    out_far, qkv_grad_far, qkv_bias_far, attn_in_far = heads_back(
        w_out_far, qkv_far, mixed_far, lse_far, w_qkv_far
    )
    out_own, qkv_grad_own, qkv_bias_own, attn_in_own = heads_back(
        w_out, qkv_own, mixed_own, lse_own, w_qkv_own
    )
    out_grad = reduced(out_own, out_far)
    qkv_grad = reduced(qkv_grad_own, qkv_grad_far).reshape(width, 3, cols)
    attn_in_grad = sum_cores(attn_in_own + attn_in_far)
    input_part, shift_one_grad, scale_one_grad = ln_one_back(attn_in_grad)
    tokens_grad_own = resid_grad + input_part
    tokens_grad = to_clip(tokens_grad_own.astype(bf16).reshape(clips, quarter, width))
    output = to_clip(output_own.reshape(clips, quarter, width))

    mod_grad = jnp.concatenate(
        [
            shift_one_grad,
            scale_one_grad,
            gate_one_grad,
            shift_two_grad,
            scale_two_grad,
            gate_two_grad,
        ],
        axis=1,
    )
    mod_grad = mod_grad + swap_core(mod_grad)
    mod_cols = mod_grad.reshape(frames, 6, 4, cols)
    mod_mine = lax.dynamic_index_in_dim(mod_cols, tensor_now, 2, False)
    mod_away = lax.dynamic_index_in_dim(mod_cols, jnp.bitwise_xor(tensor_now, 2), 2, False)
    shared = jnp.concatenate([out_bias_part, fc2_bias_part])
    shared = shared + swap_core(shared)
    shared = shared + swap_y(shared)
    local = jnp.concatenate([fc1_bias_own, qkv_bias_own])
    away = jnp.concatenate([fc1_bias_far, qkv_bias_far])
    small = jnp.concatenate([shared, local + swap_y(away)])
    gathered = jnp.stack([mod_mine, swap_y(mod_away)])
    gathered = jnp.stack([gathered, swap_x(gathered)])
    gathered = jnp.stack([gathered, swap_z(gathered, 1)])
    gathered = jnp.stack([gathered, swap_z(gathered, 2)])
    small = small + swap_x(small)
    small = small + swap_z(small, 1)
    small = small + swap_z(small, 2)
    flips = jnp.arange(32 // 2)
    origin = (
        frame_now * 4 + batch_now * 2 + far
    )
    gathered = gathered.reshape(16, frames, 6, cols)[jnp.bitwise_xor(flips, origin)]
    noise_all = lax.all_gather(noise_level, ("batch", "frame"))[..., 0]
    noise_all = noise_all.reshape(2, frames, frames, 2)
    noise_all = noise_all.transpose(2, 0, 3, 1).reshape(16 * frames)
    condition_all = jax.nn.silu(embedding(noise_all, width)).astype(bf16)
    mod_flat = gathered.reshape(16 * frames, 6 * cols)
    ada_grad = lax.dot_general(
        condition_all.astype(f32),
        mod_flat,
        (((0,), (0,)), ((), ())),
        precision=lax.Precision.HIGHEST,
        preferred_element_type=f32,
    ).reshape(width, 6, cols)
    ada_bias_grad = jnp.sum(gathered, axis=(0, 1))
    hidden_cols = fc1_bias_own.shape[0]
    fc1_end = 2 * width + hidden_cols
    return (
        output[:, None],
        tokens_grad.astype(f32)[:, None],
        ada_grad,
        ada_bias_grad,
        qkv_grad,
        small[fc1_end:].reshape(3, cols),
        out_grad,
        small[:width],
        fc1_grad,
        small[2 * width : fc1_end],
        fc2_grad,
        small[width : 2 * width],
    )


def pick_body(tokens, *rest):
    paired = (
        lax.axis_size("tensor") == 4
        and lax.axis_size("frame") == 4
        and lax.axis_size("batch") == 2
        and tokens.shape[0] == 8
        and rest[1].shape[0] % 256 == 0
        and rest[3].shape[2] % 128 == 0
    )
    return fast_body(tokens, *rest) if paired else general_body(tokens, *rest)


def solution(mesh):
    return jax.shard_map(
        pick_body,
        mesh=mesh,
        in_specs=(
            P("batch", "frame", "tensor", None),
            P("batch", "frame"),
            P(None, None, "tensor"),
            P(None, "tensor"),
            P(None, None, "tensor"),
            P(None, "tensor"),
            P("tensor", None),
            P(),
            P(None, "tensor"),
            P("tensor"),
            P("tensor", None),
            P(),
            P("batch", "frame", "tensor", None),
        ),
        out_specs=(
            P("batch", "frame", "tensor", None),
            P("batch", "frame", "tensor", None),
            P(None, None, "tensor"),
            P(None, "tensor"),
            P(None, None, "tensor"),
            P(None, "tensor"),
            P("tensor", None),
            P(),
            P(None, "tensor"),
            P("tensor"),
            P("tensor", None),
            P(),
        ),
        check_vma=False,
    )
```

```python
from functools import partial
import math

import jax
import jax.numpy as jnp
import numpy as np
from jax import lax
from jax.experimental import pallas as pl
from jax.experimental.pallas import tpu as pltpu
from jax.sharding import PartitionSpec as P

HD = 64
GRID = 16
PATCHES = 256


epsilon = 1e-06


def frequencies(count):
    return 10000.0 ** (-(jnp.arange(count, dtype=jnp.float32) / count))


def rotate_half(segment, position):
    half = segment.shape[-1] // 2
    angle = position[..., None] * frequencies(half)
    cosine = jnp.cos(angle)
    sine = jnp.sin(angle)
    first = segment[..., :half]
    second = segment[..., half:]
    return jnp.concatenate(
        [first * cosine - second * sine, first * sine + second * cosine], axis=-1
    )


def rotary(vector, frame_pos, row_pos, col_pos):
    width = vector.shape[-1]
    first = width // 4
    middle = (width - first) // 2
    return jnp.concatenate(
        [
            rotate_half(vector[..., :first], frame_pos),
            rotate_half(vector[..., first : first + middle], row_pos),
            rotate_half(vector[..., first + middle :], col_pos),
        ],
        axis=-1,
    )


def embedding(level, width):
    half = width // 2
    angle = 1000.0 * level[..., None] * frequencies(half)
    return jnp.concatenate([jnp.cos(angle), jnp.sin(angle)], axis=-1)


def normalize(value):
    center = value - jnp.mean(value, axis=-1, keepdims=True)
    spread = jnp.mean(center * center, axis=-1, keepdims=True)
    return center * lax.rsqrt(spread + epsilon)


def modulate(value, shift, scale):
    return normalize(value) * (1.0 + scale) + shift


def general_body(
    tokens,
    noise_level,
    w_ada,
    b_ada,
    w_qkv,
    b_qkv,
    w_out,
    b_out,
    w_fc1,
    b_fc1,
    w_fc2,
    b_fc2,
    cotangent,
):
    clips = tokens.shape[0]
    width = tokens.shape[3]
    head_cols = w_qkv.shape[2]
    heads_here = head_cols // HD
    frames = lax.axis_size("frame")
    frame_now = lax.axis_index("frame")
    scale = 1.0 / math.sqrt(HD)
    condition = jax.nn.silu(embedding(noise_level, width)).astype(jnp.bfloat16)
    mod_part = jnp.einsum(
        "cfd,dke->cfke", condition, w_ada, preferred_element_type=jnp.float32
    ) + b_ada.astype(jnp.float32)
    modulation = lax.all_gather(mod_part, "tensor", axis=3, tiled=True)
    pieces = [modulation[:, :, slot : slot + 1, :] for slot in range(6)]
    resid_in = tokens.astype(jnp.float32)
    attn_val, ln_one_back = jax.vjp(modulate, resid_in, pieces[0], pieces[1])
    attn_rows = lax.all_gather(attn_val.astype(jnp.bfloat16), "tensor", axis=2, tiled=True)
    projected = jnp.einsum(
        "cfpd,dke->cfpke", attn_rows, w_qkv, preferred_element_type=jnp.float32
    ) + b_qkv.astype(jnp.float32)
    projected = projected[:, 0]
    patch_ids = jnp.arange(PATCHES)
    row_pos = (patch_ids // GRID).astype(jnp.float32)[:, None]
    col_pos = (patch_ids % GRID).astype(jnp.float32)[:, None]
    frame_pos = frame_now.astype(jnp.float32)

    def turned(vector):
        return rotary(vector.reshape(clips, PATCHES, heads_here, HD), frame_pos, row_pos, col_pos)

    query_rot, query_back = jax.vjp(turned, projected[:, :, 0])
    key_rot, key_back = jax.vjp(turned, projected[:, :, 1])
    queries = query_rot.astype(jnp.bfloat16).reshape(clips, PATCHES, head_cols)
    keys_here = key_rot.astype(jnp.bfloat16).reshape(clips, PATCHES, head_cols)
    values_here = projected[:, :, 2].astype(jnp.bfloat16)
    kv_own = jnp.concatenate([keys_here, values_here], axis=-1)[:, None]
    allowed = jnp.arange(frames * PATCHES) // PATCHES <= frame_now
    kv_all = lax.all_gather(kv_own, "frame", axis=1, tiled=True)

    def fetch(index):
        return lax.dynamic_index_in_dim(kv_all, index, 0, False)

    def score_block(query_clip, kv_clip):
        keys = kv_clip[..., :head_cols].reshape(frames * PATCHES, heads_here, HD)
        values = kv_clip[..., head_cols:].reshape(frames * PATCHES, heads_here, HD)
        scores = (
            jnp.einsum(
                "qhd,khd->hqk",
                query_clip.reshape(PATCHES, heads_here, HD),
                keys,
                preferred_element_type=jnp.float32,
            )
            * scale
        )
        return (jnp.where(allowed[None, None, :], scores, -1e30), keys, values)

    def forward_step(carry, index):
        query_clip = lax.dynamic_index_in_dim(queries, index, 0, False)
        scores, keys, values = score_block(query_clip, fetch(index))
        row_max = jnp.max(scores, axis=-1, keepdims=True)
        exp_scores = jnp.exp(scores - row_max)
        row_sum = jnp.sum(exp_scores, axis=-1, keepdims=True)
        prob_map = exp_scores / row_sum
        mixed = jnp.einsum(
            "hqk,khd->qhd",
            prob_map.astype(jnp.bfloat16),
            values,
            preferred_element_type=jnp.float32,
        ).reshape(PATCHES, head_cols)
        return (carry, (mixed, (row_max + jnp.log(row_sum))[..., 0]))

    _, (mixed_all, log_sums) = lax.scan(forward_step, None, jnp.arange(clips))
    mixed_low = mixed_all.astype(jnp.bfloat16)
    attn_term = jnp.einsum("cpj,jd->cpd", mixed_low, w_out, preferred_element_type=jnp.float32)[
        :, None
    ]
    attn_branch = lax.psum_scatter(
        attn_term, "tensor", scatter_dimension=2, tiled=True
    ) + b_out.astype(jnp.float32)
    resid_one = resid_in + pieces[2] * attn_branch
    mlp_val, ln_two_back = jax.vjp(modulate, resid_one, pieces[3], pieces[4])
    mlp_rows = lax.all_gather(mlp_val.astype(jnp.bfloat16), "tensor", axis=2, tiled=True)
    pre_act = jnp.einsum(
        "cfpd,dj->cfpj", mlp_rows, w_fc1, preferred_element_type=jnp.float32
    ) + b_fc1.astype(jnp.float32)
    act_val, gelu_back = jax.vjp(partial(jax.nn.gelu, approximate=True), pre_act)
    activated = act_val.astype(jnp.bfloat16)
    mlp_term = jnp.einsum("cfpj,jd->cfpd", activated, w_fc2, preferred_element_type=jnp.float32)
    mlp_branch = lax.psum_scatter(
        mlp_term, "tensor", scatter_dimension=2, tiled=True
    ) + b_fc2.astype(jnp.float32)
    output = (resid_one + pieces[5] * mlp_branch).astype(jnp.bfloat16)
    upstream = cotangent.astype(jnp.float32)
    mlp_grad = (pieces[5] * upstream).astype(jnp.bfloat16)
    gate_two_grad = jnp.sum(upstream * mlp_branch, axis=2, keepdims=True)
    mlp_grad_rows = lax.all_gather(mlp_grad, "tensor", axis=2, tiled=True)
    fc2_grad = jnp.einsum(
        "cfpj,cfpd->jd", activated, mlp_grad_rows, preferred_element_type=jnp.float32
    )
    fc2_bias_grad = jnp.sum(mlp_grad_rows.astype(jnp.float32), axis=(0, 1, 2))
    act_grad = jnp.einsum("cfpd,jd->cfpj", mlp_grad_rows, w_fc2, preferred_element_type=jnp.float32)
    pre_grad = gelu_back(act_grad)[0].astype(jnp.bfloat16)
    fc1_grad = jnp.einsum("cfpd,cfpj->dj", mlp_rows, pre_grad, preferred_element_type=jnp.float32)
    fc1_bias_grad = jnp.sum(pre_grad.astype(jnp.float32), axis=(0, 1, 2))
    mlp_in_term = jnp.einsum("cfpj,dj->cfpd", pre_grad, w_fc1, preferred_element_type=jnp.float32)
    mlp_in_grad = lax.psum_scatter(mlp_in_term, "tensor", scatter_dimension=2, tiled=True)
    resid_part, shift_two_grad, scale_two_grad = ln_two_back(mlp_in_grad)
    resid_grad = upstream + resid_part
    attn_grad = (pieces[2] * resid_grad).astype(jnp.bfloat16)
    gate_one_grad = jnp.sum(resid_grad * attn_branch, axis=2, keepdims=True)
    attn_grad_rows = lax.all_gather(attn_grad, "tensor", axis=2, tiled=True)[:, 0]
    out_grad = jnp.einsum(
        "cpj,cpd->jd", mixed_low, attn_grad_rows, preferred_element_type=jnp.float32
    )
    out_bias_grad = jnp.sum(attn_grad_rows.astype(jnp.float32), axis=(0, 1))
    mixed_grad = jnp.einsum(
        "cpd,jd->cpj", attn_grad_rows, w_out, preferred_element_type=jnp.float32
    ).astype(jnp.bfloat16)

    def query_side(index):
        query_clip = lax.dynamic_index_in_dim(queries, index, 0, False)
        grad_clip = lax.dynamic_index_in_dim(mixed_grad, index, 0, False)
        lse_clip = lax.dynamic_index_in_dim(log_sums, index, 0, False)
        scores, keys, values = score_block(query_clip, fetch(index))
        prob_map = jnp.exp(scores - lse_clip[..., None])
        grad_heads = grad_clip.reshape(PATCHES, heads_here, HD)
        prob_grad = jnp.einsum(
            "qhd,khd->hqk", grad_heads, values, preferred_element_type=jnp.float32
        )
        row_dot = jnp.sum(prob_map * prob_grad, axis=-1, keepdims=True)
        score_grad = (scale * prob_map * (prob_grad - row_dot)).astype(jnp.bfloat16)
        query_grad = jnp.einsum(
            "hqk,khd->qhd", score_grad, keys, preferred_element_type=jnp.float32
        ).reshape(PATCHES, head_cols)
        return (query_clip, grad_heads, prob_map, score_grad, row_dot, query_grad)

    def backward_step(carry, index):
        query_clip, grad_heads, prob_map, score_grad, row_dot, query_grad = query_side(index)
        key_grad = jnp.einsum(
            "hqk,qhd->khd",
            score_grad,
            query_clip.reshape(PATCHES, heads_here, HD),
            preferred_element_type=jnp.float32,
        ).reshape(frames, PATCHES, head_cols)
        value_grad = jnp.einsum(
            "hqk,qhd->khd",
            prob_map.astype(jnp.bfloat16),
            grad_heads,
            preferred_element_type=jnp.float32,
        ).reshape(frames, PATCHES, head_cols)
        owned = lax.psum_scatter(
            jnp.concatenate([key_grad, value_grad], axis=-1),
            "frame",
            scatter_dimension=0,
            tiled=True,
        )
        return (carry, (query_grad, owned[0]))

    _, (query_grads, kv_grads) = lax.scan(backward_step, None, jnp.arange(clips))
    query_raw_grad = query_back(query_grads.reshape(clips, PATCHES, heads_here, HD))[0]
    key_raw_grad = key_back(kv_grads[..., :head_cols].reshape(clips, PATCHES, heads_here, HD))[0]
    projected_grad = jnp.stack([query_raw_grad, key_raw_grad, kv_grads[..., head_cols:]], axis=2)
    projected_grad = projected_grad.astype(jnp.bfloat16)[:, None]
    qkv_grad = jnp.einsum(
        "cfpd,cfpke->dke", attn_rows, projected_grad, preferred_element_type=jnp.float32
    )
    qkv_bias_grad = jnp.sum(projected_grad.astype(jnp.float32), axis=(0, 1, 2))
    attn_in_term = jnp.einsum(
        "cfpke,dke->cfpd", projected_grad, w_qkv, preferred_element_type=jnp.float32
    )
    attn_in_grad = lax.psum_scatter(attn_in_term, "tensor", scatter_dimension=2, tiled=True)
    input_part, shift_one_grad, scale_one_grad = ln_one_back(attn_in_grad)
    tokens_grad = resid_grad + input_part
    mod_grad_part = jnp.concatenate(
        [
            shift_one_grad,
            scale_one_grad,
            gate_one_grad,
            shift_two_grad,
            scale_two_grad,
            gate_two_grad,
        ],
        axis=2,
    )
    mod_grad = lax.psum_scatter(mod_grad_part, "tensor", scatter_dimension=3, tiled=True)
    ada_grad = jnp.einsum(
        "cfd,cfke->dke", condition.astype(jnp.float32), mod_grad, precision=lax.Precision.HIGHEST
    )
    ada_bias_grad = jnp.sum(mod_grad, axis=(0, 1))
    summed = lax.psum(
        (
            ada_grad,
            ada_bias_grad,
            qkv_grad,
            qkv_bias_grad,
            out_grad,
            out_bias_grad,
            fc1_grad,
            fc1_bias_grad,
            fc2_grad,
            fc2_bias_grad,
        ),
        ("batch", "frame"),
    )
    return (
        output,
        tokens_grad,
        summed[0],
        summed[1],
        summed[2],
        summed[3],
        summed[4],
        summed[5],
        summed[6],
        summed[7],
        summed[8],
        summed[9],
    )


MIB = 1 << 20


def rotary_ladders():
    first, middle = HD // 4, (HD - HD // 4) // 2
    bounds = [(0, first), (first, middle), (first + middle, HD - first - middle)]
    ladders = []
    for slot, (start, width) in enumerate(bounds):
        half = width // 2
        powers = np.arange(half, dtype=np.float32) / np.float32(half)
        freq = (np.float32(10000.0) ** -powers).astype(np.float32)
        angle = np.arange(GRID, dtype=np.float32)[:, None] * freq[None, :]
        cosine, sine = np.cos(angle), np.sin(angle)
        table = np.zeros((5, GRID, HD), np.float32)
        up, down = (1, 2) if slot == 0 else (3, 4)
        table[0, :, start : start + half] = cosine
        table[0, :, start + half : start + width] = cosine
        table[up, :, start : start + half] = -sine
        table[down, :, start + half : start + width] = sine
        ladders.append(np.tile(table, (1, 1, 2)))
    return ladders


def half_turn(cols):
    first, middle = HD // 4, (HD - HD // 4) // 2
    one = np.zeros((HD, HD), np.float32)
    for start, width in ((0, first), (first, middle), (first + middle, HD - first - middle)):
        half = width // 2
        for k in range(half):
            one[start + half + k, start + k] = -1.0
            one[start + k, start + half + k] = 1.0
    return np.kron(np.eye(cols // HD, dtype=np.float32), one)


def rotary_tables(core, frames):
    by_frame, by_row, by_col = rotary_ladders()
    quarter = PATCHES // 4
    steps = quarter // GRID
    order = np.zeros((2, 2, 2, steps), np.int64)
    for own in range(2):
        for side in range(2):
            for far in range(2):
                order[own, side, far] = (2 * far + (own ^ side)) * steps + np.arange(steps)
    order = order.reshape(2, GRID)
    rows = jnp.where(core == 0, by_row[:, order[0]], by_row[:, order[1]])
    full = (
        jnp.asarray(by_frame)[:, :frames, None, None, :]
        + rows[:, None, :, None, :]
        + jnp.asarray(by_col)[:, None, None, :, :]
    )
    return full.reshape(5, frames * PATCHES, 2 * HD)


def turn(value, tables, sign):
    lanes = value.shape[-1]
    near, far = HD // 8, (HD - HD // 4) // 4
    moved = (
        pltpu.roll(value, lanes - near, 1) * tables(1)
        + pltpu.roll(value, near, 1) * tables(2)
        + pltpu.roll(value, lanes - far, 1) * tables(3)
        + pltpu.roll(value, far, 1) * tables(4)
    )
    return value * tables(0) + (moved if sign > 0 else -moved)


ANY = pl.BlockSpec(memory_space=pl.ANY)


def qkv_kernel(near_ref, other_ref, w_ref, swing_ref, b_ref, tab_ref, dep_ref, out_ref, turned, bias):
    del dep_ref
    cols = out_ref.shape[2]

    @pl.when(pl.program_id(0) == 0)
    def _():
        for kind in range(2):
            lanes = slice(kind * cols, (kind + 1) * cols)
            turned[:, lanes] = jnp.dot(
                w_ref[:, lanes], swing_ref[...], preferred_element_type=jnp.float32
            ).astype(jnp.bfloat16)
            bias[:, lanes] = jnp.dot(
                b_ref[:, lanes], swing_ref[...], preferred_element_type=jnp.float32
            )

    rows = jnp.concatenate([near_ref[0], other_ref[0]], axis=0)
    for kind in range(3):
        lanes = slice(kind * cols, (kind + 1) * cols)
        value = jnp.dot(rows, w_ref[:, lanes], preferred_element_type=jnp.float32)
        value += b_ref[0, lanes].astype(jnp.float32)[None, :]
        if kind < 2:
            moved = jnp.dot(rows, turned[:, lanes], preferred_element_type=jnp.float32)
            moved += bias[0, lanes][None, :]
            for lane in range(0, cols, 128):
                part = slice(lane, lane + 128)
                out_ref[kind, :, part] = (
                    value[:, part] * tab_ref[0] + moved[:, part] * tab_ref[1]
                ).astype(jnp.bfloat16)
        else:
            out_ref[kind] = value.astype(jnp.bfloat16)


def qkv_forward(near, other, w, b, two, dep):
    frames, half, width = near.shape
    block = 2 * half
    count = frames * block
    cols = w.shape[1] // 3
    swing = jnp.asarray(half_turn(cols), jnp.bfloat16)
    bias = jnp.pad(b.reshape(1, 3 * cols), ((0, 15), (0, 0)))
    return pl.pallas_call(
        qkv_kernel,
        grid=(frames,),
        in_specs=[
            pl.BlockSpec((1, half, width), lambda i: (i, 0, 0)),
            pl.BlockSpec((1, half, width), lambda i: (i, 0, 0)),
            pl.BlockSpec((width, 3 * cols), lambda i: (0, 0)),
            pl.BlockSpec((cols, cols), lambda i: (0, 0)),
            pl.BlockSpec((16, 3 * cols), lambda i: (0, 0)),
            pl.BlockSpec((2, block, 128), lambda i: (0, i, 0)),
            ANY,
        ],
        out_specs=pl.BlockSpec((3, block, cols), lambda i: (0, i, 0)),
        out_shape=jax.ShapeDtypeStruct((3, count, cols), jnp.bfloat16),
        scratch_shapes=[
            pltpu.VMEM((width, 2 * cols), jnp.bfloat16),
            pltpu.VMEM((16, 2 * cols), jnp.float32),
        ],
        compiler_params=pltpu.CompilerParams(vmem_limit_bytes=48 * MIB),
        cost_estimate=pl.CostEstimate(
            flops=2 * count * width * cols * 5, bytes_accessed=8 * MIB, transcendentals=0
        ),
        name="qkv_forward",
    )(near, other, w, swing, bias, two, dep)


def gate_kernel(value_ref, gate_ref, dep_ref, out_ref):
    del dep_ref
    out_ref[...] = (value_ref[...].astype(jnp.float32) * gate_ref[...]).astype(jnp.bfloat16)


def gated(value, gate, dep):
    frames, half, width = value.shape
    return pl.pallas_call(
        gate_kernel,
        grid=(frames,),
        in_specs=[
            pl.BlockSpec((1, half, width), lambda i: (i, 0, 0)),
            pl.BlockSpec((1, 1, width), lambda i: (i, 0, 0)),
            ANY,
        ],
        out_specs=pl.BlockSpec((1, half, width), lambda i: (i, 0, 0)),
        out_shape=jax.ShapeDtypeStruct(value.shape, jnp.bfloat16),
        name="gated",
    )(value, gate, dep)


def hidden_kernel(
    near_ref, other_ref, gn_ref, go_ref, w1_ref, w2_ref, b_ref, *refs
):
    act_ref, pre_ref, in_near_ref, in_other_ref, rows_ref, grad_ref, bias_ref, total = refs[-8:]
    frames, half, width = near_ref.shape

    @pl.when(pl.program_id(0) == 0)
    def _():
        for frame in range(frames):
            for ref, parts in ((rows_ref, (near_ref, other_ref)), (grad_ref, (gn_ref, go_ref))):
                for side in range(2):
                    start = (2 * frame + side) * half
                    ref[start : start + half, :] = parts[side][frame]
        total[...] = jnp.zeros_like(total)

    root = math.sqrt(2.0 / math.pi)
    block = 512
    for start in range(0, rows_ref.shape[0], block):
        here = slice(start, start + block)
        pre = jnp.dot(rows_ref[here, :], w1_ref[...], preferred_element_type=jnp.float32)
        pre += b_ref[...].astype(jnp.float32)
        back = lax.dot_general(
            grad_ref[here, :], w2_ref[...], (((1,), (1,)), ((), ())),
            preferred_element_type=jnp.float32,
        )
        square = pre * pre
        tanh = jnp.tanh(pre * (root + (root * 0.044715) * square))
        side = 0.5 + 0.5 * tanh
        act_ref[here, :] = (pre * side).astype(jnp.bfloat16)
        slope = side + pre * (side * (1.0 - tanh)) * (root + (3 * root * 0.044715) * square)
        low = (back * slope).astype(jnp.bfloat16)
        pre_ref[here, :] = low
        sums = jnp.sum(low.astype(jnp.float32), axis=0, keepdims=True)
        bias_ref[...] = sums if start == 0 else bias_ref[...] + sums
        total[here, :] += lax.dot_general(
            low, w1_ref[...], (((1,), (1,)), ((), ())), preferred_element_type=jnp.float32
        )

    @pl.when(pl.program_id(0) == pl.num_programs(0) - 1)
    def _():
        for frame in range(frames):
            start = 2 * frame * half
            in_near_ref[frame] = total[start : start + half, :]
            in_other_ref[frame] = total[start + half : start + 2 * half, :].astype(jnp.bfloat16)


def hidden(near, other, grad_near, grad_other, w1, w2, b, *deps):
    frames, half, width = near.shape
    units = w1.shape[1]
    count = 2 * frames * half
    step = 256
    side = pl.BlockSpec((frames, half, width), lambda i: (0, 0, 0))
    wide = pl.BlockSpec((count, step), lambda i: (0, i))
    tall = pl.BlockSpec((count, width), lambda i: (0, 0))
    line = pl.BlockSpec((1, step), lambda i: (0, i))
    bf16, f32 = jnp.bfloat16, jnp.float32
    return pl.pallas_call(
        hidden_kernel,
        grid=(units // step,),
        in_specs=[side] * 4
        + [
            pl.BlockSpec((width, step), lambda i: (0, i)),
            pl.BlockSpec((step, width), lambda i: (i, 0)),
            line,
        ]
        + [ANY] * len(deps),
        out_specs=[wide, wide, side, side, tall, tall, line],
        out_shape=[
            jax.ShapeDtypeStruct((count, units), bf16),
            jax.ShapeDtypeStruct((count, units), bf16),
            jax.ShapeDtypeStruct((frames, half, width), f32),
            jax.ShapeDtypeStruct((frames, half, width), bf16),
            jax.ShapeDtypeStruct((count, width), bf16),
            jax.ShapeDtypeStruct((count, width), bf16),
            jax.ShapeDtypeStruct((1, units), f32),
        ],
        scratch_shapes=[pltpu.VMEM((count, width), f32)],
        compiler_params=pltpu.CompilerParams(vmem_limit_bytes=56 * MIB),
        cost_estimate=pl.CostEstimate(
            flops=6 * count * width * units,
            bytes_accessed=20 * MIB,
            transcendentals=count * units,
        ),
        name="hidden",
    )(near, other, grad_near, grad_other, w1, w2, b.reshape(1, units), *deps)


def normal(value):
    center = value - jnp.mean(value, axis=-1, keepdims=True)
    root = lax.rsqrt(jnp.mean(center * center, axis=-1, keepdims=True) + epsilon)
    return center * root, root


def normal_back(grad, unit, root):
    tilt = jnp.mean(grad * unit, axis=-1, keepdims=True)
    return (grad - jnp.mean(grad, axis=-1, keepdims=True) - unit * tilt) * root


def by_frame(kernel, inputs, outs, deps=(), name=None):
    def spec(shape):
        if shape[0] == 1:
            return pl.BlockSpec((1,) + tuple(shape[1:]), lambda i: (0, 0, 0))
        return pl.BlockSpec((1,) + tuple(shape[1:]), lambda i: (i, 0, 0))

    frames = max(item.shape[0] for item in inputs)
    ready = len(inputs)

    def run(*refs):
        kernel(refs[:ready], refs[ready + len(deps) :])

    return pl.pallas_call(
        run,
        grid=(frames,),
        in_specs=[spec(item.shape) for item in inputs] + [ANY] * len(deps),
        out_specs=[spec(item[0]) for item in outs],
        out_shape=[jax.ShapeDtypeStruct(*item) for item in outs],
        compiler_params=pltpu.CompilerParams(vmem_limit_bytes=40 * MIB),
        name=name,
    )(*inputs, *deps)


def project_kernel(left_ref, w_ref, left_far_ref, w_far_ref, near_ref, other_ref):
    half = near_ref.shape[1]
    total = jnp.dot(left_ref[...], w_ref[...], preferred_element_type=jnp.float32)
    total += jnp.dot(left_far_ref[...], w_far_ref[...], preferred_element_type=jnp.float32)
    for frame in range(near_ref.shape[0]):
        start = 2 * half * frame
        near_ref[frame] = total[start : start + half]
        other_ref[frame] = total[start + half : start + 2 * half].astype(jnp.bfloat16)


def project(left, w, left_far, w_far, frames):
    count, depth = left.shape
    width = w.shape[1]
    half = count // (2 * frames)
    full = lambda rows, lanes: pl.BlockSpec((rows, lanes), lambda i: (i, 0))
    same = pl.BlockSpec((depth, width), lambda i: (0, 0))
    step = 2
    rows = count * step // frames
    out = pl.BlockSpec((step, half, width), lambda i: (i, 0, 0))
    return pl.pallas_call(
        project_kernel,
        grid=(frames // step,),
        in_specs=[full(rows, depth), same, full(rows, depth), same],
        out_specs=[out, out],
        out_shape=[
            jax.ShapeDtypeStruct((frames, half, width), jnp.float32),
            jax.ShapeDtypeStruct((frames, half, width), jnp.bfloat16),
        ],
        compiler_params=pltpu.CompilerParams(vmem_limit_bytes=40 * MIB),
        name="project",
    )(left, w, left_far, w_far)


SMALL_ROWS = 48


def depart_kernel(
    qkv_ref, qkv_far_ref, out_ref, out_far_ref, tokens_ref,
    s1_ref, c1_ref, g1_ref, s2_ref, c2_ref, g2_ref,
    bias_qkv_ref, bias_qkv_far_ref, bias_fc1_ref, bias_out_ref, bias_fc2_ref,
    qkv_sum, out_sum, tokens_out, gathered,
    x_away, x_got, z1_away, z1_got, z2_away, z2_got, keep_half,
    small, small_got, small_low,
    send, recv, small_send, small_recv, token_send, token_recv,
):
    f32, bf16 = jnp.float32, jnp.bfloat16
    batch, frame, tensor = (lax.axis_index(name) for name in ("batch", "frame", "tensor"))
    core, far = lax.rem(tensor, 2), lax.div(tensor, 2)
    low, high = lax.rem(frame, 2), lax.div(frame, 2)
    other_x = 1 - batch
    frame_1 = frame + 1 - 2 * low
    frame_2 = lax.rem(frame + 2, 4)
    other_core = tensor + 1 - 2 * core
    place = 2 * frame + far

    def at(b, f, t):
        return (b, f, t)

    peers = []
    for flip in range(2):
        for gap in range(8):
            if flip or gap:
                spot = lax.rem(place + gap, 8)
                b = batch + flip - 2 * flip * batch
                peers.append((flip, gap, b, spot, lax.div(spot, 2), lax.rem(spot, 2)))

    barrier = pltpu.get_barrier_semaphore()
    for _, _, b, _, f, y in peers:
        pl.semaphore_signal(
            barrier, inc=1, device_id=at(b, f, 2 * y + core), device_id_type=pl.DeviceIdType.MESH
        )
    pl.semaphore_signal(
        barrier, inc=1, device_id=at(batch, frame, other_core),
        device_id_type=pl.DeviceIdType.MESH,
    )
    pl.semaphore_wait(barrier, len(peers) + 1)

    def copy(src, dst, one, two, target):
        item = pltpu.make_async_remote_copy(
            src_ref=src, dst_ref=dst, send_sem=one, recv_sem=two,
            device_id=target, device_id_type=pl.DeviceIdType.MESH,
        )
        item.start()
        return item

    chunks = [(out_ref, out_far_ref, out_sum, 0, out_ref.shape[1])]
    chunks += [
        (qkv_ref, qkv_far_ref, qkv_sum, start, qkv_ref.shape[1])
        for start in range(0, qkv_ref.shape[0], 256)
    ]
    piece = 32

    def rows(start, count):
        return pl.ds(pl.multiple_of(start, piece), count)

    sent = []
    x_copies = []
    for k, (own, other, _, base, lanes) in enumerate(chunks):
        here = rows(base + other_x * 128, 128)
        x_away[k, :, :lanes] = (own[here, :] + other[here, :].astype(f32)).astype(bf16)
        x_copies.append(
            copy(
                x_away.at[k], x_got.at[k], send.at[k, 0], recv.at[k, 0],
                at(other_x, frame, tensor),
            )
        )
    mods = (s1_ref, c1_ref, g1_ref, s2_ref, c2_ref, g2_ref)
    width = small.shape[3]
    small[...] = jnp.zeros_like(small)
    for c in range(2):
        for y in range(2):
            start = (2 * y + c) * width
            for j, ref in enumerate(mods):
                small[c, y, 4 * j : 4 * j + 4, :] = ref[:, 0, start : start + width]
            for j in range(4):
                part = slice(j * width, (j + 1) * width)
                small[c, y, 31 + j : 32 + j, :] = bias_out_ref[:, part]
                small[c, y, 35 + j : 36 + j, :] = bias_fc2_ref[:, part]
    core_copy = copy(
        small.at[1 - core], small_got, small_send.at[15], small_recv.at[15],
        at(batch, frame, other_core),
    )
    token_copies = []
    for flip, gap, b, spot, f, y in peers:
        if not flip:
            token_copies.append(
                copy(
                    tokens_ref.at[spot], tokens_out.at[place],
                    token_send.at[gap - 1], token_recv.at[gap - 1],
                    at(batch, f, 2 * y + core),
                )
            )
    tokens_out[place] = tokens_ref[place]
    core_copy.wait()
    for y in range(2):
        small_low[y] = (small[core, y] + small_got[y]).astype(bf16)
    for j in range(3):
        part = slice(j * width, (j + 1) * width)
        small_low[far, 24 + j : 25 + j, :] = bias_qkv_ref[:, part].astype(bf16)
        small_low[1 - far, 24 + j : 25 + j, :] = bias_qkv_far_ref[:, part].astype(bf16)
    for j in range(4):
        part = slice(j * width, (j + 1) * width)
        small_low[far, 27 + j : 28 + j, :] = bias_fc1_ref[:, part].astype(bf16)
    slot = 8 * batch + place
    small_copies = []
    for n, (_, _, b, _, f, y) in enumerate(peers):
        small_copies.append(
            copy(
                small_low.at[y], gathered.at[slot], small_send.at[n], small_recv.at[n],
                at(b, f, 2 * y + core),
            )
        )
    gathered[slot] = small_low[far]

    z1_copies = []
    for k, (own, other, _, base, lanes) in enumerate(chunks):
        x_copies[k].wait_recv()
        here = rows(base + batch * 128, 128)
        keep_half[k, :, :lanes] = (
            own[here, :] + other[here, :].astype(f32) + x_got[k, :, :lanes].astype(f32)
        )
        for up in range(2):
            z1_away[k, up * piece : (up + 1) * piece, :lanes] = keep_half[
                k, rows((2 * up + 1 - low) * piece, piece), :lanes
            ].astype(bf16)
        z1_copies.append(
            copy(
                z1_away.at[k], z1_got.at[k], send.at[k, 1], recv.at[k, 1],
                at(batch, frame_1, tensor),
            )
        )
    z2_copies = []
    for k, (_, _, _, _, lanes) in enumerate(chunks):
        z1_copies[k].wait_recv()
        z2_away[k, :, :lanes] = (
            keep_half[k, rows(frame_2 * piece, piece), :lanes]
            + z1_got[k, rows((1 - high) * piece, piece), :lanes].astype(f32)
        ).astype(bf16)
        z2_copies.append(
            copy(
                z2_away.at[k], z2_got.at[k], send.at[k, 2], recv.at[k, 2],
                at(batch, frame_2, tensor),
            )
        )

    def share(k, total, base, number, owner, target):
        here = rows(base + batch * 128 + owner * piece, piece)
        return copy(
            total.at[here, :], total.at[here, :], send.at[k, number], recv.at[k, number], target
        )

    shared = []
    for k, (_, _, total, base, lanes) in enumerate(chunks):
        z2_copies[k].wait_recv()
        total[rows(base + batch * 128 + frame * piece, piece), :] = (
            keep_half[k, rows(frame * piece, piece), :lanes]
            + z1_got[k, rows(high * piece, piece), :lanes].astype(f32)
            + z2_got[k, :, :lanes].astype(f32)
        ).astype(bf16)
        shared.append(
            {
                "z2": share(k, total, base, 3, frame, at(batch, frame_2, tensor)),
                "z1": share(k, total, base, 4, frame, at(batch, frame_1, tensor)),
                "x": share(k, total, base, 6, frame, at(other_x, frame, tensor)),
            }
        )
    frame_3 = lax.rem(frame_1 + 2, 4)
    for k, (_, _, total, base, lanes) in enumerate(chunks):
        shared[k]["z2"].wait_recv()
        shared[k]["z1on"] = share(k, total, base, 5, frame_2, at(batch, frame_1, tensor))
        shared[k]["x2"] = share(k, total, base, 7, frame_2, at(other_x, frame, tensor))
        shared[k]["z1"].wait_recv()
        shared[k]["x1"] = share(k, total, base, 8, frame_1, at(other_x, frame, tensor))
    for k, (_, _, total, base, lanes) in enumerate(chunks):
        shared[k]["z1on"].wait_recv()
        shared[k]["x3"] = share(k, total, base, 9, frame_3, at(other_x, frame, tensor))
    for k in range(len(chunks)):
        for name in ("x", "x2", "x1", "x3"):
            shared[k][name].wait_recv()
    for item in small_copies + token_copies:
        item.wait()
    for k in range(len(chunks)):
        x_copies[k].wait_send()
        z1_copies[k].wait_send()
        z2_copies[k].wait_send()
        for name in ("z2", "z1", "x", "z1on", "x2", "x1", "x3"):
            shared[k][name].wait_send()


def depart(qkv, qkv_far, out, out_far, tokens, mods, biases):
    f32, bf16 = jnp.float32, jnp.bfloat16
    chunks = 1 + qkv.shape[0] // 256
    lanes = max(qkv.shape[1], out.shape[1])
    cols = qkv.shape[1] // 3
    vmem = pl.BlockSpec(memory_space=pltpu.VMEM)
    inputs = [qkv, qkv_far, out, out_far, tokens, *mods, *biases]
    return pl.pallas_call(
        depart_kernel,
        in_specs=[vmem] * len(inputs),
        out_specs=[vmem] * 4,
        out_shape=[
            jax.ShapeDtypeStruct(qkv.shape, bf16),
            jax.ShapeDtypeStruct(out.shape, bf16),
            jax.ShapeDtypeStruct(tokens.shape, bf16),
            jax.ShapeDtypeStruct((16, SMALL_ROWS, cols), bf16),
        ],
        scratch_shapes=[
            pltpu.VMEM((chunks, 128, lanes), bf16),
            pltpu.VMEM((chunks, 128, lanes), bf16),
            pltpu.VMEM((chunks, 64, lanes), bf16),
            pltpu.VMEM((chunks, 64, lanes), bf16),
            pltpu.VMEM((chunks, 32, lanes), bf16),
            pltpu.VMEM((chunks, 32, lanes), bf16),
            pltpu.VMEM((chunks, 128, lanes), f32),
            pltpu.VMEM((2, 2, SMALL_ROWS, cols), f32),
            pltpu.VMEM((2, SMALL_ROWS, cols), f32),
            pltpu.VMEM((2, SMALL_ROWS, cols), bf16),
            pltpu.SemaphoreType.DMA((chunks, 10)),
            pltpu.SemaphoreType.DMA((chunks, 10)),
            pltpu.SemaphoreType.DMA((16,)),
            pltpu.SemaphoreType.DMA((16,)),
            pltpu.SemaphoreType.DMA((7,)),
            pltpu.SemaphoreType.DMA((7,)),
        ],
        compiler_params=pltpu.CompilerParams(
            collective_id=1, has_side_effects=True, vmem_limit_bytes=50 * MIB
        ),
        name="depart",
    )(*inputs)


def attend_kernel(frames, qkv_ref, dep_ref, out_ref, lse_ref):
    del dep_ref
    lanes = qkv_ref.shape[2]
    low_lane = lax.broadcasted_iota(jnp.int32, (PATCHES, lanes), 1) < HD
    for frame in range(frames):
        here = pl.ds(frame * PATCHES, PATCHES)
        length = (frame + 1) * PATCHES
        query = qkv_ref[0, here, :] * jnp.bfloat16(1.0 / math.sqrt(HD))
        keys = qkv_ref[1, :length, :]
        values = qkv_ref[2, :length, :]
        outs, sums = [], []
        for head in range(2):
            chosen = low_lane if head == 0 else jnp.logical_not(low_lane)
            scores = lax.dot_general(
                jnp.where(chosen, query, jnp.bfloat16(0)),
                keys,
                (((1,), (1,)), ((), ())),
                preferred_element_type=jnp.float32,
            )
            top = jnp.max(scores, axis=1, keepdims=True)
            grown = jnp.exp(scores - top)
            total = jnp.sum(grown, axis=1, keepdims=True)
            prob = (grown * (1.0 / total)).astype(jnp.bfloat16)
            outs.append(jnp.dot(prob, values, preferred_element_type=jnp.float32))
            sums.append(top + jnp.log(total))
        out_ref[here, :] = jnp.where(low_lane, outs[0], outs[1]).astype(jnp.bfloat16)
        lse_ref[0, here, :] = jnp.concatenate(sums, axis=1)


def attend(qkv, frames, dep):
    _, count, cols = qkv.shape
    pairs = cols // 128
    return pl.pallas_call(
        partial(attend_kernel, frames),
        grid=(pairs,),
        in_specs=[pl.BlockSpec((3, count, 128), lambda i: (0, 0, i)), ANY],
        out_specs=[
            pl.BlockSpec((count, 128), lambda i: (0, i)),
            pl.BlockSpec((1, count, 2), lambda i: (i, 0, 0)),
        ],
        out_shape=[
            jax.ShapeDtypeStruct((count, cols), jnp.bfloat16),
            jax.ShapeDtypeStruct((pairs, count, 2), jnp.float32),
        ],
        compiler_params=pltpu.CompilerParams(vmem_limit_bytes=48 * MIB),
        cost_estimate=pl.CostEstimate(
            flops=12_000_000_000, bytes_accessed=4 * MIB, transcendentals=2_600_000
        ),
        name="attend",
    )(qkv, dep)


def attend_back_kernel(
    frames, qkv_ref, grad_ref, lse_ref, tab_ref, *refs
):
    out_ref, dk_ref, dv_ref = refs[-3:]
    lanes = qkv_ref.shape[2]
    low_lane = lax.broadcasted_iota(jnp.int32, (PATCHES, lanes), 1) < HD
    scale = 1.0 / math.sqrt(HD)
    zero = jnp.bfloat16(0)
    dk_ref[...] = jnp.zeros_like(dk_ref)
    dv_ref[...] = jnp.zeros_like(dv_ref)
    for frame in range(frames):
        here = pl.ds(frame * PATCHES, PATCHES)
        length = (frame + 1) * PATCHES
        query = qkv_ref[0, here, :]
        grad = grad_ref[here, :]
        keys = qkv_ref[1, :length, :]
        values = qkv_ref[2, :length, :]
        outs = []
        for head in range(2):
            chosen = low_lane if head == 0 else jnp.logical_not(low_lane)
            query_head = jnp.where(chosen, query, zero)
            grad_head = jnp.where(chosen, grad, zero)
            scores = lax.dot_general(
                query_head * jnp.bfloat16(scale),
                keys,
                (((1,), (1,)), ((), ())),
                preferred_element_type=jnp.float32,
            )
            prob = jnp.exp(scores - lse_ref[0, here, head : head + 1])
            prob_grad = lax.dot_general(
                grad_head, values, (((1,), (1,)), ((), ())), preferred_element_type=jnp.float32
            )
            row_dot = jnp.sum(prob * prob_grad, axis=1, keepdims=True)
            score_grad = (prob * ((prob_grad - row_dot) * scale)).astype(jnp.bfloat16)
            outs.append(jnp.dot(score_grad, keys, preferred_element_type=jnp.float32))
            dk_ref[:length, :] += lax.dot_general(
                score_grad,
                query_head,
                (((0,), (0,)), ((), ())),
                preferred_element_type=jnp.float32,
            )
            dv_ref[:length, :] += lax.dot_general(
                prob.astype(jnp.bfloat16),
                grad_head,
                (((0,), (0,)), ((), ())),
                preferred_element_type=jnp.float32,
            )
        out_ref[0, here, :] = turn(
            jnp.where(low_lane, outs[0], outs[1]), lambda slot: tab_ref[slot, here, :], -1
        ).astype(jnp.bfloat16)
    out_ref[1] = turn(dk_ref[...], lambda slot: tab_ref[slot], -1).astype(jnp.bfloat16)
    out_ref[2] = dv_ref[...].astype(jnp.bfloat16)


def attend_back(qkv, grad, lse, tables, frames, *deps):
    _, count, cols = qkv.shape
    pairs = cols // 128
    return pl.pallas_call(
        partial(attend_back_kernel, frames),
        grid=(pairs,),
        in_specs=[
            pl.BlockSpec((3, count, 128), lambda i: (0, 0, i)),
            pl.BlockSpec((count, 128), lambda i: (0, i)),
            pl.BlockSpec((1, count, 2), lambda i: (i, 0, 0)),
            pl.BlockSpec(tables.shape, lambda i: (0, 0, 0)),
        ]
        + [ANY] * len(deps),
        out_specs=pl.BlockSpec((3, count, 128), lambda i: (0, 0, i)),
        out_shape=jax.ShapeDtypeStruct((3, count, cols), jnp.bfloat16),
        scratch_shapes=[
            pltpu.VMEM((count, 128), jnp.float32),
            pltpu.VMEM((count, 128), jnp.float32),
        ],
        compiler_params=pltpu.CompilerParams(vmem_limit_bytes=48 * MIB),
        cost_estimate=pl.CostEstimate(
            flops=24_000_000_000, bytes_accessed=6 * MIB, transcendentals=2_600_000
        ),
        name="attend_back",
    )(qkv, grad, lse, tables, *deps)


def fast_body(
    tokens,
    noise_level,
    w_ada,
    b_ada,
    w_qkv,
    b_qkv,
    w_out,
    b_out,
    w_fc1,
    b_fc1,
    w_fc2,
    b_fc2,
    cotangent,
):
    clips, _, quarter, width = tokens.shape
    frames = lax.axis_size("frame")
    cols = w_qkv.shape[2]
    batch_now = lax.axis_index("batch")
    frame_now = lax.axis_index("frame")
    tensor_now = lax.axis_index("tensor")
    core = tensor_now % 2
    far = tensor_now // 2
    clip_now = frame_now * 2 + far
    rows_own = clips * quarter
    count = 2 * rows_own
    f32 = jnp.float32
    bf16 = jnp.bfloat16
    groups = [
        [f * 4 + 2 * y + c for f in range(frames) for y in range(2)] for c in range(2)
    ]

    def to_clip(item):
        return lax.all_to_all(item, ("frame", "tensor"), 0, 0, axis_index_groups=groups)

    def swap_y(item):
        return lax.ppermute(item, "tensor", [(t, t ^ 2) for t in range(4)])

    def swap_core(item):
        return lax.ppermute(item, "tensor", [(t, t ^ 1) for t in range(4)])

    def swap_x(item):
        return lax.ppermute(item, "batch", [(0, 1), (1, 0)])

    def swap_z(item, bit):
        return lax.ppermute(item, "frame", [(f, f ^ bit) for f in range(frames)])

    def ordered(mine, theirs, place):
        return jnp.stack(
            [jnp.where(place == 0, mine, theirs), jnp.where(place == 0, theirs, mine)]
        )

    def both_cores(item):
        return jnp.concatenate([item, swap_core(item)], axis=1).reshape(count, width)

    def sum_cores(term):
        split = term.reshape(frames, 2, rows_own // frames, width)
        return split[:, 0] + swap_core(split[:, 1].astype(bf16)).astype(f32)

    noise_all = lax.all_to_all(
        jnp.broadcast_to(noise_level[None, :, 0], (2 * frames, clips)), ("batch", "frame"), 0, 0
    ).reshape(2, frames, frames, 2)
    condition = jax.nn.silu(embedding(noise_level, width)).astype(bf16)
    mod_part = jnp.einsum(
        "cfd,dke->cfke", condition, w_ada, preferred_element_type=f32
    ) + b_ada.astype(f32)
    tokens_own = to_clip(tokens[:, 0]).reshape(frames, 2 * quarter, width)
    mod_own = to_clip(mod_part[:, 0]).reshape(frames, 2, 6, cols)
    modulation = ordered(mod_own, swap_core(mod_own), core)
    modulation = modulation.transpose(1, 3, 2, 0, 4).reshape(frames, 6, width)
    pieces = [modulation[:, slot : slot + 1, :] for slot in range(6)]
    tables = rotary_tables(core, frames)
    two = jnp.stack([tables[0], (tables[2] + tables[4]) - (tables[1] + tables[3])])
    w_qkv_own = w_qkv.reshape(width, 3 * cols)
    w_qkv_far = swap_y(w_qkv_own)
    b_qkv_far = swap_y(b_qkv)
    w_out_far = swap_y(w_out)

    shape = (frames, 2 * quarter, width)
    line = (frames, 1, width)

    def first_norm(ins, outs):
        unit, _ = normal(ins[0][0].astype(f32))
        outs[0][0] = (unit * (1.0 + ins[2][0]) + ins[1][0]).astype(bf16)

    (attn_in,) = by_frame(
        first_norm, [tokens_own, pieces[0], pieces[1]], [(shape, bf16)], name="first_norm"
    )
    attn_in_other = swap_core(attn_in)
    attn_rows = jnp.concatenate([attn_in, attn_in_other], axis=1).reshape(count, width)
    qkv_own = qkv_forward(attn_in, attn_in_other, w_qkv_own, b_qkv, two, noise_level)
    mixed_own, lse_own = attend(qkv_own, frames, noise_level)
    qkv_far = qkv_forward(attn_in, attn_in_other, w_qkv_far, b_qkv_far, two, mixed_own)

    cot_own = to_clip(cotangent[:, 0]).reshape(shape)
    mlp_grad = gated(cot_own, pieces[5], qkv_far)
    mixed_far, lse_far = attend(qkv_far, frames, mlp_grad)
    mlp_grad_far = swap_y(mlp_grad)
    fc2_bias_part = jnp.sum(mlp_grad.astype(f32), axis=(0, 1))

    term_near, term_other = project(mixed_own, w_out, mixed_far, w_out_far, frames)

    def second_norm(ins, outs):
        near, other, bias, value, gate, shift, scale = (item[0].astype(f32) for item in ins)
        branch = near + other + bias
        resid = value + gate * branch
        unit, _ = normal(resid)
        outs[0][0] = branch
        outs[1][0] = resid
        outs[2][0] = (unit * (1.0 + scale) + shift).astype(bf16)

    attn_branch, resid_one, mlp_in = by_frame(
        second_norm,
        [term_near, swap_core(term_other), b_out.reshape(1, 1, width), tokens_own]
        + [pieces[2], pieces[3], pieces[4]],
        [(shape, f32), (shape, f32), (shape, bf16)],
        name="second_norm",
    )
    mlp_in_far = swap_y(mlp_in)

    act_near, pre_near, in_near, in_near_away, rows_near, grad_near, bias_near = hidden(
        mlp_in, swap_core(mlp_in), mlp_grad, swap_core(mlp_grad), w_fc1, w_fc2, b_fc1
    )
    act_far, pre_far, in_far, in_far_away, rows_far, grad_far, bias_far = hidden(
        mlp_in_far, swap_core(mlp_in_far), mlp_grad_far, swap_core(mlp_grad_far),
        w_fc1, w_fc2, b_fc1, act_near,
    )
    in_back = swap_y((in_far + swap_core(in_far_away).astype(f32)).astype(bf16))
    fc1_bias_own = (bias_near + bias_far)[0]

    def outer(left_near, right_near, left_far, right_far):
        dims = (((0,), (0,)), ((), ()))
        return lax.dot_general(
            left_near, right_near, dims, preferred_element_type=f32
        ) + lax.dot_general(left_far, right_far, dims, preferred_element_type=f32)

    fc2_own = outer(act_near, grad_near, act_far, grad_far).astype(bf16)
    fc1_own = outer(rows_near, pre_near, rows_far, pre_far).astype(bf16)
    fc2_sum, fc1_sum = lax.psum((fc2_own, fc1_own), ("batch", "frame"))

    def branch_parts(activated):
        term = jnp.dot(activated, w_fc2, preferred_element_type=f32)
        term = term.reshape(frames, 2, 2 * quarter, width)
        return term[:, 0], swap_core(term[:, 1].astype(bf16))

    far_near, far_other = branch_parts(act_far)
    branch_back = swap_y((far_near + far_other.astype(f32)).astype(bf16))
    branch_near, branch_other = branch_parts(act_near)

    def second_back(ins, outs):
        near, other, back, resid, cot, branch, gate, scale = (item[0].astype(f32) for item in ins)
        grad = near + other + back
        unit, root = normal(resid)
        outs[0][0] = jnp.sum(grad, axis=0, keepdims=True)
        outs[1][0] = jnp.sum(grad * unit, axis=0, keepdims=True)
        through = cot + normal_back(grad * (1.0 + scale), unit, root)
        outs[2][0] = through
        low = (gate * through).astype(bf16)
        outs[3][0] = low
        outs[4][0] = jnp.sum(through * branch, axis=0, keepdims=True)
        outs[5][0] = jnp.sum(low.astype(f32), axis=0, keepdims=True)

    shift_two_grad, scale_two_grad, resid_grad, attn_grad, gate_one_grad, out_bias = by_frame(
        second_back,
        [in_near, swap_core(in_near_away), in_back, resid_one, cot_own, attn_branch]
        + [pieces[2], pieces[4]],
        [(line, f32), (line, f32), (shape, f32), (shape, bf16), (line, f32), (line, f32)],
        [fc1_own, fc2_own, far_near, branch_near],
        name="second_back",
    )
    out_bias_part = jnp.sum(out_bias, axis=(0, 1))
    attn_grad_rows = both_cores(attn_grad)

    def last_gate(ins, outs):
        near, other, back, bias, resid, gate, cot = (item[0].astype(f32) for item in ins)
        branch = near + other + back + bias
        outs[0][0] = (resid + gate * branch).astype(bf16)
        outs[1][0] = jnp.sum(cot * branch, axis=0, keepdims=True)

    def back_mixed(w):
        return lax.dot_general(
            attn_grad_rows, w, (((1,), (1,)), ((), ())), preferred_element_type=f32
        ).astype(bf16)

    def out_outer(mixed):
        return lax.dot_general(
            mixed, attn_grad_rows, (((0,), (0,)), ((), ())), preferred_element_type=f32
        )

    def heads_back(qkv, mixed_grad, lse, w_in, *deps):
        back = attend_back(qkv, mixed_grad, lse, tables, frames, *deps)
        back = back.transpose(1, 0, 2).reshape(count, 3 * cols)
        qkv_grad = lax.dot_general(
            attn_rows, back, (((0,), (0,)), ((), ())), preferred_element_type=f32
        )
        in_term = lax.dot_general(
            back, w_in, (((1,), (1,)), ((), ())), preferred_element_type=f32
        )
        return back, qkv_grad, jnp.sum(back.astype(f32), axis=0), in_term

    out_arrived = swap_y(out_outer(mixed_far).astype(bf16))
    mixed_grad_far = back_mixed(w_out_far)
    mixed_grad_own = back_mixed(w_out)
    back_far, qkv_grad_far, qkv_bias_far, attn_in_far = heads_back(
        qkv_far, mixed_grad_far, lse_far, w_qkv_far, mixed_grad_own
    )
    qkv_low_far = qkv_grad_far.astype(bf16)
    qkv_arrived = swap_y(qkv_low_far)
    output_own, gate_two_grad = by_frame(
        last_gate,
        [branch_near, branch_other, branch_back, b_fc2.reshape(1, 1, width), resid_one]
        + [pieces[5], cot_own],
        [(shape, bf16), (line, f32)],
        [back_far],
        name="last_gate",
    )
    output = to_clip(output_own.reshape(clips, quarter, width))
    back_own, qkv_grad_own, qkv_bias_own, attn_in_own = heads_back(
        qkv_own, mixed_grad_own, lse_own, w_qkv_own, qkv_low_far, output_own
    )
    in_term = (attn_in_own + attn_in_far).reshape(frames, 2, 2 * quarter, width)

    def first_back(ins, outs):
        near, other, value, above, scale = (item[0].astype(f32) for item in ins)
        grad = near + other
        unit, root = normal(value)
        outs[0][0] = jnp.sum(grad, axis=0, keepdims=True)
        outs[1][0] = jnp.sum(grad * unit, axis=0, keepdims=True)
        outs[2][0] = (above + normal_back(grad * (1.0 + scale), unit, root)).astype(bf16)

    shift_one_grad, scale_one_grad, tokens_low = by_frame(
        first_back,
        [in_term[:, 0], swap_core(in_term[:, 1].astype(bf16)), tokens_own, resid_grad, pieces[1]],
        [(line, f32), (line, f32), (shape, bf16)],
        name="first_back",
    )
    mods = [shift_one_grad, scale_one_grad, gate_one_grad]
    mods += [shift_two_grad, scale_two_grad, gate_two_grad]
    biases = [qkv_bias_own, qkv_bias_far, fc1_bias_own, out_bias_part, fc2_bias_part]
    qkv_sum, out_sum, tokens_grad, gathered = depart(
        qkv_grad_own, qkv_arrived, out_outer(mixed_own), out_arrived,
        tokens_low.reshape(clips, quarter, width), mods, [item[None, :] for item in biases],
    )
    noise_all = noise_all.transpose(0, 2, 3, 1).reshape(16 * frames)
    condition_all = jax.nn.silu(embedding(noise_all, width)).astype(bf16)
    mod_all = gathered[:, : 6 * frames].reshape(16, 6, frames, cols).transpose(0, 2, 1, 3)
    ada_grad = lax.dot_general(
        condition_all,
        mod_all.reshape(16 * frames, 6 * cols),
        (((0,), (0,)), ((), ())),
        preferred_element_type=f32,
    ).reshape(width, 6, cols)
    rows_sum = jnp.sum(gathered.astype(f32), axis=0)
    ada_bias_grad = jnp.sum(rows_sum[: 6 * frames].reshape(6, frames, cols), axis=1)
    hidden_rows = fc1_bias_own.shape[0] // cols
    return (
        output[:, None],
        tokens_grad.astype(f32)[:, None],
        ada_grad,
        ada_bias_grad,
        qkv_sum.astype(f32).reshape(width, 3, cols),
        rows_sum[24:27],
        out_sum.astype(f32),
        rows_sum[31:35].reshape(width),
        fc1_sum.astype(f32),
        rows_sum[27 : 27 + hidden_rows].reshape(4 * cols),
        fc2_sum.astype(f32),
        rows_sum[35:39].reshape(width),
    )


def pick_body(tokens, *rest):
    paired = (
        lax.axis_size("tensor") == 4
        and lax.axis_size("frame") == 4
        and lax.axis_size("batch") == 2
        and tokens.shape[0] == 8
        and rest[1].shape[0] % 256 == 0
        and rest[3].shape[2] % 128 == 0
    )
    return fast_body(tokens, *rest) if paired else general_body(tokens, *rest)


def solution(mesh):
    return jax.shard_map(
        pick_body,
        mesh=mesh,
        in_specs=(
            P("batch", "frame", "tensor", None),
            P("batch", "frame"),
            P(None, None, "tensor"),
            P(None, "tensor"),
            P(None, None, "tensor"),
            P(None, "tensor"),
            P("tensor", None),
            P(),
            P(None, "tensor"),
            P("tensor"),
            P("tensor", None),
            P(),
            P("batch", "frame", "tensor", None),
        ),
        out_specs=(
            P("batch", "frame", "tensor", None),
            P("batch", "frame", "tensor", None),
            P(None, None, "tensor"),
            P(None, "tensor"),
            P(None, None, "tensor"),
            P(None, "tensor"),
            P("tensor", None),
            P(),
            P(None, "tensor"),
            P("tensor"),
            P("tensor", None),
            P(),
        ),
        check_vma=False,
    )
```

```python
from functools import partial
import math

import jax
import jax.numpy as jnp
import numpy as np
from jax import lax
from jax.experimental import pallas as pl
from jax.experimental.pallas import tpu as pltpu
from jax.sharding import PartitionSpec as P

HD = 64
GRID = 16
PATCHES = 256


epsilon = 1e-06


def frequencies(count):
    return 10000.0 ** (-(jnp.arange(count, dtype=jnp.float32) / count))


def rotate_half(segment, position):
    half = segment.shape[-1] // 2
    angle = position[..., None] * frequencies(half)
    cosine = jnp.cos(angle)
    sine = jnp.sin(angle)
    first = segment[..., :half]
    second = segment[..., half:]
    return jnp.concatenate(
        [first * cosine - second * sine, first * sine + second * cosine], axis=-1
    )


def rotary(vector, frame_pos, row_pos, col_pos):
    width = vector.shape[-1]
    first = width // 4
    middle = (width - first) // 2
    return jnp.concatenate(
        [
            rotate_half(vector[..., :first], frame_pos),
            rotate_half(vector[..., first : first + middle], row_pos),
            rotate_half(vector[..., first + middle :], col_pos),
        ],
        axis=-1,
    )


def embedding(level, width):
    half = width // 2
    angle = 1000.0 * level[..., None] * frequencies(half)
    return jnp.concatenate([jnp.cos(angle), jnp.sin(angle)], axis=-1)


def normalize(value):
    center = value - jnp.mean(value, axis=-1, keepdims=True)
    spread = jnp.mean(center * center, axis=-1, keepdims=True)
    return center * lax.rsqrt(spread + epsilon)


def modulate(value, shift, scale):
    return normalize(value) * (1.0 + scale) + shift


def general_body(
    tokens,
    noise_level,
    w_ada,
    b_ada,
    w_qkv,
    b_qkv,
    w_out,
    b_out,
    w_fc1,
    b_fc1,
    w_fc2,
    b_fc2,
    cotangent,
):
    clips = tokens.shape[0]
    width = tokens.shape[3]
    head_cols = w_qkv.shape[2]
    heads_here = head_cols // HD
    frames = lax.axis_size("frame")
    frame_now = lax.axis_index("frame")
    scale = 1.0 / math.sqrt(HD)
    condition = jax.nn.silu(embedding(noise_level, width)).astype(jnp.bfloat16)
    mod_part = jnp.einsum(
        "cfd,dke->cfke", condition, w_ada, preferred_element_type=jnp.float32
    ) + b_ada.astype(jnp.float32)
    modulation = lax.all_gather(mod_part, "tensor", axis=3, tiled=True)
    pieces = [modulation[:, :, slot : slot + 1, :] for slot in range(6)]
    resid_in = tokens.astype(jnp.float32)
    attn_val, ln_one_back = jax.vjp(modulate, resid_in, pieces[0], pieces[1])
    attn_rows = lax.all_gather(attn_val.astype(jnp.bfloat16), "tensor", axis=2, tiled=True)
    projected = jnp.einsum(
        "cfpd,dke->cfpke", attn_rows, w_qkv, preferred_element_type=jnp.float32
    ) + b_qkv.astype(jnp.float32)
    projected = projected[:, 0]
    patch_ids = jnp.arange(PATCHES)
    row_pos = (patch_ids // GRID).astype(jnp.float32)[:, None]
    col_pos = (patch_ids % GRID).astype(jnp.float32)[:, None]
    frame_pos = frame_now.astype(jnp.float32)

    def turned(vector):
        return rotary(vector.reshape(clips, PATCHES, heads_here, HD), frame_pos, row_pos, col_pos)

    query_rot, query_back = jax.vjp(turned, projected[:, :, 0])
    key_rot, key_back = jax.vjp(turned, projected[:, :, 1])
    queries = query_rot.astype(jnp.bfloat16).reshape(clips, PATCHES, head_cols)
    keys_here = key_rot.astype(jnp.bfloat16).reshape(clips, PATCHES, head_cols)
    values_here = projected[:, :, 2].astype(jnp.bfloat16)
    kv_own = jnp.concatenate([keys_here, values_here], axis=-1)[:, None]
    allowed = jnp.arange(frames * PATCHES) // PATCHES <= frame_now
    kv_all = lax.all_gather(kv_own, "frame", axis=1, tiled=True)

    def fetch(index):
        return lax.dynamic_index_in_dim(kv_all, index, 0, False)

    def score_block(query_clip, kv_clip):
        keys = kv_clip[..., :head_cols].reshape(frames * PATCHES, heads_here, HD)
        values = kv_clip[..., head_cols:].reshape(frames * PATCHES, heads_here, HD)
        scores = (
            jnp.einsum(
                "qhd,khd->hqk",
                query_clip.reshape(PATCHES, heads_here, HD),
                keys,
                preferred_element_type=jnp.float32,
            )
            * scale
        )
        return (jnp.where(allowed[None, None, :], scores, -1e30), keys, values)

    def forward_step(carry, index):
        query_clip = lax.dynamic_index_in_dim(queries, index, 0, False)
        scores, keys, values = score_block(query_clip, fetch(index))
        row_max = jnp.max(scores, axis=-1, keepdims=True)
        exp_scores = jnp.exp(scores - row_max)
        row_sum = jnp.sum(exp_scores, axis=-1, keepdims=True)
        prob_map = exp_scores / row_sum
        mixed = jnp.einsum(
            "hqk,khd->qhd",
            prob_map.astype(jnp.bfloat16),
            values,
            preferred_element_type=jnp.float32,
        ).reshape(PATCHES, head_cols)
        return (carry, (mixed, (row_max + jnp.log(row_sum))[..., 0]))

    _, (mixed_all, log_sums) = lax.scan(forward_step, None, jnp.arange(clips))
    mixed_low = mixed_all.astype(jnp.bfloat16)
    attn_term = jnp.einsum("cpj,jd->cpd", mixed_low, w_out, preferred_element_type=jnp.float32)[
        :, None
    ]
    attn_branch = lax.psum_scatter(
        attn_term, "tensor", scatter_dimension=2, tiled=True
    ) + b_out.astype(jnp.float32)
    resid_one = resid_in + pieces[2] * attn_branch
    mlp_val, ln_two_back = jax.vjp(modulate, resid_one, pieces[3], pieces[4])
    mlp_rows = lax.all_gather(mlp_val.astype(jnp.bfloat16), "tensor", axis=2, tiled=True)
    pre_act = jnp.einsum(
        "cfpd,dj->cfpj", mlp_rows, w_fc1, preferred_element_type=jnp.float32
    ) + b_fc1.astype(jnp.float32)
    act_val, gelu_back = jax.vjp(partial(jax.nn.gelu, approximate=True), pre_act)
    activated = act_val.astype(jnp.bfloat16)
    mlp_term = jnp.einsum("cfpj,jd->cfpd", activated, w_fc2, preferred_element_type=jnp.float32)
    mlp_branch = lax.psum_scatter(
        mlp_term, "tensor", scatter_dimension=2, tiled=True
    ) + b_fc2.astype(jnp.float32)
    output = (resid_one + pieces[5] * mlp_branch).astype(jnp.bfloat16)
    upstream = cotangent.astype(jnp.float32)
    mlp_grad = (pieces[5] * upstream).astype(jnp.bfloat16)
    gate_two_grad = jnp.sum(upstream * mlp_branch, axis=2, keepdims=True)
    mlp_grad_rows = lax.all_gather(mlp_grad, "tensor", axis=2, tiled=True)
    fc2_grad = jnp.einsum(
        "cfpj,cfpd->jd", activated, mlp_grad_rows, preferred_element_type=jnp.float32
    )
    fc2_bias_grad = jnp.sum(mlp_grad_rows.astype(jnp.float32), axis=(0, 1, 2))
    act_grad = jnp.einsum("cfpd,jd->cfpj", mlp_grad_rows, w_fc2, preferred_element_type=jnp.float32)
    pre_grad = gelu_back(act_grad)[0].astype(jnp.bfloat16)
    fc1_grad = jnp.einsum("cfpd,cfpj->dj", mlp_rows, pre_grad, preferred_element_type=jnp.float32)
    fc1_bias_grad = jnp.sum(pre_grad.astype(jnp.float32), axis=(0, 1, 2))
    mlp_in_term = jnp.einsum("cfpj,dj->cfpd", pre_grad, w_fc1, preferred_element_type=jnp.float32)
    mlp_in_grad = lax.psum_scatter(mlp_in_term, "tensor", scatter_dimension=2, tiled=True)
    resid_part, shift_two_grad, scale_two_grad = ln_two_back(mlp_in_grad)
    resid_grad = upstream + resid_part
    attn_grad = (pieces[2] * resid_grad).astype(jnp.bfloat16)
    gate_one_grad = jnp.sum(resid_grad * attn_branch, axis=2, keepdims=True)
    attn_grad_rows = lax.all_gather(attn_grad, "tensor", axis=2, tiled=True)[:, 0]
    out_grad = jnp.einsum(
        "cpj,cpd->jd", mixed_low, attn_grad_rows, preferred_element_type=jnp.float32
    )
    out_bias_grad = jnp.sum(attn_grad_rows.astype(jnp.float32), axis=(0, 1))
    mixed_grad = jnp.einsum(
        "cpd,jd->cpj", attn_grad_rows, w_out, preferred_element_type=jnp.float32
    ).astype(jnp.bfloat16)

    def query_side(index):
        query_clip = lax.dynamic_index_in_dim(queries, index, 0, False)
        grad_clip = lax.dynamic_index_in_dim(mixed_grad, index, 0, False)
        lse_clip = lax.dynamic_index_in_dim(log_sums, index, 0, False)
        scores, keys, values = score_block(query_clip, fetch(index))
        prob_map = jnp.exp(scores - lse_clip[..., None])
        grad_heads = grad_clip.reshape(PATCHES, heads_here, HD)
        prob_grad = jnp.einsum(
            "qhd,khd->hqk", grad_heads, values, preferred_element_type=jnp.float32
        )
        row_dot = jnp.sum(prob_map * prob_grad, axis=-1, keepdims=True)
        score_grad = (scale * prob_map * (prob_grad - row_dot)).astype(jnp.bfloat16)
        query_grad = jnp.einsum(
            "hqk,khd->qhd", score_grad, keys, preferred_element_type=jnp.float32
        ).reshape(PATCHES, head_cols)
        return (query_clip, grad_heads, prob_map, score_grad, row_dot, query_grad)

    def backward_step(carry, index):
        query_clip, grad_heads, prob_map, score_grad, row_dot, query_grad = query_side(index)
        key_grad = jnp.einsum(
            "hqk,qhd->khd",
            score_grad,
            query_clip.reshape(PATCHES, heads_here, HD),
            preferred_element_type=jnp.float32,
        ).reshape(frames, PATCHES, head_cols)
        value_grad = jnp.einsum(
            "hqk,qhd->khd",
            prob_map.astype(jnp.bfloat16),
            grad_heads,
            preferred_element_type=jnp.float32,
        ).reshape(frames, PATCHES, head_cols)
        owned = lax.psum_scatter(
            jnp.concatenate([key_grad, value_grad], axis=-1),
            "frame",
            scatter_dimension=0,
            tiled=True,
        )
        return (carry, (query_grad, owned[0]))

    _, (query_grads, kv_grads) = lax.scan(backward_step, None, jnp.arange(clips))
    query_raw_grad = query_back(query_grads.reshape(clips, PATCHES, heads_here, HD))[0]
    key_raw_grad = key_back(kv_grads[..., :head_cols].reshape(clips, PATCHES, heads_here, HD))[0]
    projected_grad = jnp.stack([query_raw_grad, key_raw_grad, kv_grads[..., head_cols:]], axis=2)
    projected_grad = projected_grad.astype(jnp.bfloat16)[:, None]
    qkv_grad = jnp.einsum(
        "cfpd,cfpke->dke", attn_rows, projected_grad, preferred_element_type=jnp.float32
    )
    qkv_bias_grad = jnp.sum(projected_grad.astype(jnp.float32), axis=(0, 1, 2))
    attn_in_term = jnp.einsum(
        "cfpke,dke->cfpd", projected_grad, w_qkv, preferred_element_type=jnp.float32
    )
    attn_in_grad = lax.psum_scatter(attn_in_term, "tensor", scatter_dimension=2, tiled=True)
    input_part, shift_one_grad, scale_one_grad = ln_one_back(attn_in_grad)
    tokens_grad = resid_grad + input_part
    mod_grad_part = jnp.concatenate(
        [
            shift_one_grad,
            scale_one_grad,
            gate_one_grad,
            shift_two_grad,
            scale_two_grad,
            gate_two_grad,
        ],
        axis=2,
    )
    mod_grad = lax.psum_scatter(mod_grad_part, "tensor", scatter_dimension=3, tiled=True)
    ada_grad = jnp.einsum(
        "cfd,cfke->dke", condition.astype(jnp.float32), mod_grad, precision=lax.Precision.HIGHEST
    )
    ada_bias_grad = jnp.sum(mod_grad, axis=(0, 1))
    summed = lax.psum(
        (
            ada_grad,
            ada_bias_grad,
            qkv_grad,
            qkv_bias_grad,
            out_grad,
            out_bias_grad,
            fc1_grad,
            fc1_bias_grad,
            fc2_grad,
            fc2_bias_grad,
        ),
        ("batch", "frame"),
    )
    return (
        output,
        tokens_grad,
        summed[0],
        summed[1],
        summed[2],
        summed[3],
        summed[4],
        summed[5],
        summed[6],
        summed[7],
        summed[8],
        summed[9],
    )


MIB = 1 << 20


def rotary_ladders():
    first, middle = HD // 4, (HD - HD // 4) // 2
    bounds = [(0, first), (first, middle), (first + middle, HD - first - middle)]
    ladders = []
    for slot, (start, width) in enumerate(bounds):
        half = width // 2
        powers = np.arange(half, dtype=np.float32) / np.float32(half)
        freq = (np.float32(10000.0) ** -powers).astype(np.float32)
        angle = np.arange(GRID, dtype=np.float32)[:, None] * freq[None, :]
        cosine, sine = np.cos(angle), np.sin(angle)
        table = np.zeros((5, GRID, HD), np.float32)
        up, down = (1, 2) if slot == 0 else (3, 4)
        table[0, :, start : start + half] = cosine
        table[0, :, start + half : start + width] = cosine
        table[up, :, start : start + half] = -sine
        table[down, :, start + half : start + width] = sine
        ladders.append(np.tile(table, (1, 1, 2)))
    return ladders


def half_turn(cols):
    first, middle = HD // 4, (HD - HD // 4) // 2
    one = np.zeros((HD, HD), np.float32)
    for start, width in ((0, first), (first, middle), (first + middle, HD - first - middle)):
        half = width // 2
        for k in range(half):
            one[start + half + k, start + k] = -1.0
            one[start + k, start + half + k] = 1.0
    return np.kron(np.eye(cols // HD, dtype=np.float32), one)


def rotary_tables(core, frames):
    by_frame, by_row, by_col = rotary_ladders()
    quarter = PATCHES // 4
    steps = quarter // GRID
    order = np.zeros((2, 2, 2, steps), np.int64)
    for own in range(2):
        for side in range(2):
            for far in range(2):
                order[own, side, far] = (2 * far + (own ^ side)) * steps + np.arange(steps)
    order = order.reshape(2, GRID)
    rows = jnp.where(core == 0, by_row[:, order[0]], by_row[:, order[1]])
    full = (
        jnp.asarray(by_frame)[:, :frames, None, None, :]
        + rows[:, None, :, None, :]
        + jnp.asarray(by_col)[:, None, None, :, :]
    )
    return full.reshape(5, frames * PATCHES, 2 * HD)


def turn(value, tables, sign):
    lanes = value.shape[-1]
    near, far = HD // 8, (HD - HD // 4) // 4
    moved = (
        pltpu.roll(value, lanes - near, 1) * tables(1)
        + pltpu.roll(value, near, 1) * tables(2)
        + pltpu.roll(value, lanes - far, 1) * tables(3)
        + pltpu.roll(value, far, 1) * tables(4)
    )
    return value * tables(0) + (moved if sign > 0 else -moved)


ANY = pl.BlockSpec(memory_space=pl.ANY)


def normal(value):
    center = value - jnp.mean(value, axis=-1, keepdims=True)
    root = lax.rsqrt(jnp.mean(center * center, axis=-1, keepdims=True) + epsilon)
    return center * root, root


def normal_back(grad, unit, root):
    tilt = jnp.mean(grad * unit, axis=-1, keepdims=True)
    return (grad - jnp.mean(grad, axis=-1, keepdims=True) - unit * tilt) * root


def by_frame(kernel, inputs, outs, deps=(), name=None):
    def spec(shape):
        if shape[0] == 1:
            return pl.BlockSpec((1,) + tuple(shape[1:]), lambda i: (0, 0, 0))
        return pl.BlockSpec((1,) + tuple(shape[1:]), lambda i: (i, 0, 0))

    frames = max(item.shape[0] for item in inputs)
    ready = len(inputs)

    def run(*refs):
        kernel(refs[:ready], refs[ready + len(deps) :])

    return pl.pallas_call(
        run,
        grid=(frames,),
        in_specs=[spec(item.shape) for item in inputs] + [ANY] * len(deps),
        out_specs=[spec(item[0]) for item in outs],
        out_shape=[jax.ShapeDtypeStruct(*item) for item in outs],
        compiler_params=pltpu.CompilerParams(vmem_limit_bytes=40 * MIB),
        name=name,
    )(*inputs, *deps)


SMALL_ROWS = 64


def places(batch, flips):
    place_now = 2 * lax.axis_index("frame") + lax.div(lax.axis_index("tensor"), 2)
    found = []
    for flip in range(flips):
        for gap in range(8):
            if flip or gap:
                spot = lax.rem(place_now + gap, 8)
                b = batch + flip - 2 * flip * batch
                found.append((b, spot, lax.div(spot, 2), lax.rem(spot, 2)))
    return found


def signal_all(targets):
    barrier = pltpu.get_barrier_semaphore()
    for target in targets:
        pl.semaphore_signal(
            barrier, inc=1, device_id=target, device_id_type=pl.DeviceIdType.MESH
        )
    pl.semaphore_wait(barrier, len(targets))


def start_copy(src, dst, send, recv, target):
    item = pltpu.make_async_remote_copy(
        src_ref=src, dst_ref=dst, send_sem=send, recv_sem=recv,
        device_id=target, device_id_type=pl.DeviceIdType.MESH,
    )
    item.start()
    return item


def attend_rows(load_query, load_key, load_value, frame, store):
    length = (frame + 1) * PATCHES
    query = load_query(frame) * jnp.bfloat16(1.0 / math.sqrt(HD))
    keys, values = load_key(length), load_value(length)
    low_lane = lax.broadcasted_iota(jnp.int32, query.shape, 1) < HD
    outs, sums = [], []
    for head in range(2):
        chosen = low_lane if head == 0 else jnp.logical_not(low_lane)
        scores = lax.dot_general(
            jnp.where(chosen, query, jnp.bfloat16(0)),
            keys,
            (((1,), (1,)), ((), ())),
            preferred_element_type=jnp.float32,
        )
        top = jnp.max(scores, axis=1, keepdims=True)
        grown = jnp.exp(scores - top)
        total = jnp.sum(grown, axis=1, keepdims=True)
        prob = (grown * (1.0 / total)).astype(jnp.bfloat16)
        outs.append(jnp.dot(prob, values, preferred_element_type=jnp.float32))
        sums.append(top + jnp.log(total))
    store(
        jnp.where(low_lane, outs[0], outs[1]).astype(jnp.bfloat16),
        jnp.concatenate(sums, axis=1),
    )


def mlp_side(pre):
    root = math.sqrt(2.0 / math.pi)
    square = pre * pre
    tanh = jnp.tanh(pre * (root + (root * 0.044715) * square))
    side = 0.5 + 0.5 * tanh
    slope = side + pre * (side * (1.0 - tanh)) * (root + (3 * root * 0.044715) * square)
    return pre * side, slope


NT = (((1,), (1,)), ((), ()))
TN = (((0,), (0,)), ((), ()))


def forward_kernel(
    tokens_ref, mod_ref, w_ref, bq_ref, two_ref, swing_ref, wo_ref, bo_ref, b1_ref,
    w1_hbm, w2_hbm, cot_ref,
    cond_out, p0, p1, p2, p3, p4, p5, bias1_out, bias2_out,
    o_tok, o_rows, o_wq, o_wo, o_qkv, o_mixed, o_lse, o_cot, o_grad, o_mrows,
    o_branch, o_resid, o_act, o_pre, o_near, o_got, o_far,
    tok, mods, rows, wq, wo_far, bq_far, qkv, mixed, lse, cotb, grad, mrows,
    branch, resid, t_send, t_got, wf1, wf2, act, pre_low, total, in_near, in_send, in_got,
    token_send, token_recv, cot_send, cot_recv, mod_send, mod_recv, row_send, row_recv,
    wide_send, wide_recv, frame_send, frame_recv, local,
):
    f32, bf16 = jnp.float32, jnp.bfloat16
    batch, frame_now, tensor = (lax.axis_index(name) for name in ("batch", "frame", "tensor"))
    core, far = lax.rem(tensor, 2), lax.div(tensor, 2)
    other_core = (batch, frame_now, tensor + 1 - 2 * core)
    other_y = (batch, frame_now, lax.rem(tensor + 2, 4))
    place = 2 * frame_now + far
    peers = places(batch, 1)
    targets = [(b, f, 2 * y + core) for b, _, f, y in peers]
    saves = []

    def save(src, dst):
        item = pltpu.make_async_copy(src, dst, local.at[2 + len(saves)])
        item.start()
        saves.append(item)

    load_1 = pltpu.make_async_copy(w1_hbm, wf1, local.at[0])
    load_2 = pltpu.make_async_copy(w2_hbm, wf2, local.at[1])
    load_1.start()
    load_2.start()
    signal_all(targets + [other_core])
    mod_copies, token_copies = [], []
    for n, (_, spot, _, _) in enumerate(peers):
        mod_copies.append(
            start_copy(
                mod_ref.at[spot], mods.at[core, place], mod_send.at[n], mod_recv.at[n], targets[n]
            )
        )
    for n, (_, spot, _, _) in enumerate(peers):
        token_copies.append(
            start_copy(
                tokens_ref.at[spot], tok.at[place], token_send.at[n], token_recv.at[n], targets[n]
            )
        )
    mods[core, place] = mod_ref[place]
    tok[place] = tokens_ref[place]
    cols = w_ref.shape[2]
    for kind in range(3):
        wq[0, :, kind * cols : (kind + 1) * cols] = w_ref[:, kind, :]
    w_copies = [
        start_copy(wq.at[0], wq.at[1], wide_send.at[0], wide_recv.at[0], other_y),
        start_copy(bq_ref, bq_far, wide_send.at[1], wide_recv.at[1], other_y),
        start_copy(wo_ref, wo_far, wide_send.at[2], wide_recv.at[2], other_y),
    ]
    for item in mod_copies:
        item.wait_recv()
    swap = start_copy(mods.at[core], mods.at[core], mod_send.at[7], mod_recv.at[7], other_core)
    swap.wait_recv()
    pieces = (p0, p1, p2, p3, p4, p5)
    for f in range(4):
        for y in range(2):
            for c in range(2):
                lanes = slice((2 * y + c) * cols, (2 * y + c + 1) * cols)
                for j, ref in enumerate(pieces):
                    ref[f, :, lanes] = mods[c, 2 * f + y, j : j + 1, :]
        for k in range(4):
            cond_out[4 * f + k : 4 * f + k + 1, :] = mods[0, 2 * f, 6 + k : 7 + k, :]
    row_copies, cot_copies = [], []
    for n in range(8):
        spot = place if n == 0 else lax.rem(place + 8 - n, 8)
        if n:
            token_copies[n - 1].wait_recv()
        f, y = lax.div(spot, 2), lax.rem(spot, 2)
        unit, _ = normal(tok[spot].astype(f32))
        low = (unit * (1.0 + p1[f]) + p0[f]).astype(bf16)
        here = pl.ds(pl.multiple_of(f * 256 + y * 64, 64), 64)
        there = pl.ds(pl.multiple_of(f * 256 + y * 64 + 128, 64), 64)
        rows[here, :] = low
        row_copies.append(
            start_copy(
                rows.at[here, :], rows.at[there, :], row_send.at[n], row_recv.at[n], other_core
            )
        )
    for n, (_, spot, _, _) in enumerate(peers):
        cot_copies.append(
            start_copy(
                cot_ref.at[spot], cotb.at[place], cot_send.at[n], cot_recv.at[n], targets[n]
            )
        )
    cotb[place] = cot_ref[place]
    for item in row_copies:
        item.wait_recv()

    def project_heads(side):
        for kind in range(3):
            w = wq[side, :, kind * cols : (kind + 1) * cols]
            bias = (bq_ref if side == 0 else bq_far)[:, kind * cols : (kind + 1) * cols]
            if kind < 2:
                turned = jnp.dot(w, swing_ref[...], preferred_element_type=f32).astype(bf16)
                bias_turned = jnp.dot(bias, swing_ref[...], preferred_element_type=f32)[:1]
            bias = bias[:1].astype(f32)
            for start in range(0, rows.shape[0], 512):
                here = slice(start, start + 512)
                value = jnp.dot(rows[here, :], w, preferred_element_type=f32) + bias
                if kind < 2:
                    moved = jnp.dot(rows[here, :], turned, preferred_element_type=f32)
                    moved += bias_turned
                for pair in range(2):
                    part = slice(pair * 128, (pair + 1) * 128)
                    out = value[:, part]
                    if kind < 2:
                        out = out * two_ref[0, here, :] + moved[:, part] * two_ref[1, here, :]
                    qkv[2 * side + pair, kind, here, :] = out.astype(bf16)

    def attend_pair(side, pair):
        spot = 2 * side + pair
        for f in range(4):
            here = slice(f * PATCHES, (f + 1) * PATCHES)

            def store(out, sums):
                mixed[side, here, pair * 128 : (pair + 1) * 128] = out
                lse[spot, here, :] = sums

            attend_rows(
                lambda f: qkv[spot, 0, here, :],
                lambda length: qkv[spot, 1, :length, :],
                lambda length: qkv[spot, 2, :length, :],
                f,
                store,
            )

    def to_frames(src, dst, number, target, start_there):
        found = []
        for f in range(4):
            here, there = pl.ds(256 * f, 128), pl.ds(256 * f + start_there, 128)
            found.append(
                start_copy(
                    src.at[here, :], dst.at[there, :],
                    frame_send.at[number, f], frame_recv.at[number, f], target,
                )
            )
        return found

    project_heads(0)
    for pair in range(2):
        attend_pair(0, pair)
    for item in cot_copies:
        item.wait_recv()
    sums = jnp.zeros_like(bias2_out[...])
    for f in range(4):
        for y in range(2):
            low = (p5[f] * cotb[2 * f + y].astype(f32)).astype(bf16)
            grad[0, 256 * f + 64 * y : 256 * f + 64 * y + 64, :] = low
            sums += jnp.sum(low.astype(f32), axis=0, keepdims=True)
    bias2_out[...] = sums
    for item in w_copies:
        item.wait_recv()
    grad_core = to_frames(grad.at[0], grad.at[0], 0, other_core, 128)
    grad_y = to_frames(grad.at[0], grad.at[1], 1, other_y, 0)
    save(tok, o_tok)
    save(rows, o_rows)
    save(wq, o_wq)
    save(wo_far, o_wo)
    save(cotb, o_cot)
    project_heads(1)
    save(qkv, o_qkv)
    for pair in range(2):
        attend_pair(1, pair)
    save(mixed, o_mixed)
    save(lse, o_lse)
    term_core = []
    for f in range(4):
        here = slice(256 * f, 256 * f + 256)
        own = slice(128 * f, 128 * f + 128)
        term = jnp.dot(mixed[0, here, :], wo_ref[...], preferred_element_type=f32)
        term += jnp.dot(mixed[1, here, :], wo_far[...], preferred_element_type=f32)
        branch[own, :] = term[:128]
        t_send[own, :] = term[128:].astype(bf16)
        term_core.append(
            start_copy(
                t_send.at[own, :], t_got.at[own, :],
                frame_send.at[2, f], frame_recv.at[2, f], other_core,
            )
        )
    for item in grad_y:
        item.wait_recv()
    far_core = to_frames(grad.at[1], grad.at[1], 3, other_core, 128)
    row_core, row_y = [], []
    for f in range(4):
        term_core[f].wait_recv()
        own = slice(128 * f, 128 * f + 128)
        value = branch[own, :] + t_got[own, :].astype(f32) + bo_ref[...].astype(f32)
        branch[own, :] = value
        source = jnp.concatenate([tok[2 * f], tok[2 * f + 1]], axis=0).astype(f32)
        value = source + p2[f] * value
        resid[own, :] = value
        unit, _ = normal(value)
        here = pl.ds(256 * f, 128)
        mrows[0, 256 * f : 256 * f + 128, :] = (unit * (1.0 + p4[f]) + p3[f]).astype(bf16)
        row_y.append(
            start_copy(
                mrows.at[0, here, :], mrows.at[1, here, :],
                frame_send.at[4, f], frame_recv.at[4, f], other_y,
            )
        )
        row_core.append(
            start_copy(
                mrows.at[0, here, :], mrows.at[0, pl.ds(256 * f + 128, 128), :],
                frame_send.at[5, f], frame_recv.at[5, f], other_core,
            )
        )
    save(branch, o_branch)
    save(resid, o_resid)
    load_1.wait()
    load_2.wait()
    units = wf1.shape[1]
    step = 256

    def hidden_set(side):
        for start in range(0, units, step):
            part = slice(start, start + step)
            sums = None
            for first in range(0, 1024, 512):
                here = slice(first, first + 512)
                pre = jnp.dot(mrows[side, here, :], wf1[:, part], preferred_element_type=f32)
                pre += b1_ref[:, part].astype(f32)
                back = lax.dot_general(
                    grad[side, here, :], wf2[part, :], NT, preferred_element_type=f32
                )
                value, slope = mlp_side(pre)
                act[side, here, part] = value.astype(bf16)
                low = (back * slope).astype(bf16)
                pre_low[side, here, part] = low
                some = jnp.sum(low.astype(f32), axis=0, keepdims=True)
                sums = some if sums is None else sums + some
                term = lax.dot_general(low, wf1[:, part], NT, preferred_element_type=f32)
                if start == 0:
                    total[here, :] = term
                else:
                    total[here, :] += term
            bias1_out[:, part] = sums if side == 0 else bias1_out[:, part] + sums

    def swap_terms(side):
        for f in range(4):
            own = slice(128 * f, 128 * f + 128)
            in_send[side, own, :] = total[256 * f + 128 : 256 * f + 256, :].astype(bf16)
            if side == 0:
                in_near[own, :] = total[256 * f : 256 * f + 128, :]
        return start_copy(
            in_send.at[side], in_got.at[side],
            wide_send.at[3 + side], wide_recv.at[3 + side], other_core,
        )

    for item in row_core + grad_core + far_core:
        item.wait_recv()
    hidden_set(0)
    near_swap = swap_terms(0)
    save(act.at[0], o_act.at[0])
    save(pre_low.at[0], o_pre.at[0])
    save(grad, o_grad)
    save(in_near, o_near)
    for item in row_y:
        item.wait_recv()
    rows_far_core = to_frames(mrows.at[1], mrows.at[1], 6, other_core, 128)
    for item in rows_far_core:
        item.wait_recv()
    save(mrows, o_mrows)
    hidden_set(1)
    far_swap = swap_terms(1)
    save(act.at[1], o_act.at[1])
    save(pre_low.at[1], o_pre.at[1])
    near_swap.wait_recv()
    save(in_got.at[0], o_got)
    far_swap.wait_recv()
    for f in range(4):
        own = slice(128 * f, 128 * f + 128)
        t_got[own, :] = (
            total[256 * f : 256 * f + 128, :] + in_got[1, own, :].astype(f32)
        ).astype(bf16)
    save(t_got, o_far)
    remote = mod_copies + token_copies + w_copies + [swap] + row_copies + cot_copies
    remote += grad_core + grad_y + term_core + far_core + row_core + row_y + rows_far_core
    for item in remote + [near_swap, far_swap]:
        item.wait_send()
    for item in saves:
        item.wait()


def forward(tokens, mod, w_qkv, b_qkv, two, w_out, b_out, b_fc1, w_fc1, w_fc2, cot):
    f32, bf16 = jnp.float32, jnp.bfloat16
    clips, quarter, width = tokens.shape
    cols = mod.shape[2]
    units = w_fc1.shape[1]
    count = 2 * clips * quarter
    half = count // 2
    vmem = pl.BlockSpec(memory_space=pltpu.VMEM)
    like = jax.ShapeDtypeStruct
    swing = jnp.asarray(half_turn(cols), bf16)
    small = [like((16, cols), f32)] + [like((4, 1, width), f32)] * 6
    small += [like((1, units), f32), like((1, width), f32)]
    buffers = dict(
        tok=((8, 64, width), bf16), rows=((count, width), bf16),
        wq=((2, width, 3 * cols), bf16), wo=((cols, width), bf16),
        qkv=((4, 3, count, 128), bf16), mixed=((2, count, cols), bf16),
        lse=((4, count, 2), f32), cot=((8, 64, width), bf16),
        grad=((2, count, width), bf16), mrows=((2, count, width), bf16),
        branch=((half, width), f32), resid=((half, width), f32),
        act=((2, count, units), bf16), pre=((2, count, units), bf16),
        near=((half, width), f32), got=((half, width), bf16), far=((half, width), bf16),
    )
    shape = {name: pltpu.VMEM(*item) for name, item in buffers.items()}
    dma = lambda *dims: pltpu.SemaphoreType.DMA(dims)
    return pl.pallas_call(
        forward_kernel,
        in_specs=[vmem] * 9 + [ANY] * 2 + [vmem],
        out_specs=[vmem] * len(small) + [ANY] * len(buffers),
        out_shape=small + [like(*item) for item in buffers.values()],
        scratch_shapes=[
            shape["tok"], pltpu.VMEM((2,) + mod.shape, f32), shape["rows"], shape["wq"],
            shape["wo"], pltpu.VMEM((16, 3 * cols), bf16), shape["qkv"], shape["mixed"],
            shape["lse"], shape["cot"], shape["grad"], shape["mrows"], shape["branch"],
            shape["resid"], shape["got"], shape["got"],
            pltpu.VMEM((width, units), bf16), pltpu.VMEM((units, width), bf16),
            shape["act"], shape["pre"], pltpu.VMEM((count, width), f32), shape["near"],
            pltpu.VMEM((2, half, width), bf16), pltpu.VMEM((2, half, width), bf16),
            dma(7), dma(7), dma(7), dma(7), dma(8), dma(8), dma(8), dma(8),
            dma(5), dma(5), dma(7, 4), dma(7, 4), dma(24),
        ],
        compiler_params=pltpu.CompilerParams(
            collective_id=2, has_side_effects=True, vmem_limit_bytes=63 * MIB
        ),
        name="forward",
    )(
        tokens, mod, w_qkv, jnp.broadcast_to(b_qkv, (16, 3 * cols)), two, swing, w_out,
        b_out.reshape(1, width), b_fc1.reshape(1, units), w_fc1, w_fc2, cot,
    )


def depart_kernel(
    qkv_ref, qkv_far_ref, out_ref, out_far_ref, tokens_ref,
    s1_ref, c1_ref, g1_ref, s2_ref, c2_ref, g2_ref,
    bias_qkv_ref, bias_qkv_far_ref, bias_fc1_ref, bias_out_ref, bias_fc2_ref, cond_ref,
    qkv_sum, out_sum, tokens_out, gathered,
    x_away, x_got, z1_away, z1_got, z2_away, z2_got, keep_half,
    small, small_got, small_low,
    send, recv, small_send, small_recv, token_send, token_recv,
):
    f32, bf16 = jnp.float32, jnp.bfloat16
    batch, frame, tensor = (lax.axis_index(name) for name in ("batch", "frame", "tensor"))
    core, far = lax.rem(tensor, 2), lax.div(tensor, 2)
    low, high = lax.rem(frame, 2), lax.div(frame, 2)
    other_x = 1 - batch
    frame_1 = frame + 1 - 2 * low
    frame_2 = lax.rem(frame + 2, 4)
    other_core = tensor + 1 - 2 * core
    place = 2 * frame + far

    def at(b, f, t):
        return (b, f, t)

    peers = []
    for flip in range(2):
        for gap in range(8):
            if flip or gap:
                spot = lax.rem(place + gap, 8)
                b = batch + flip - 2 * flip * batch
                peers.append((flip, gap, b, spot, lax.div(spot, 2), lax.rem(spot, 2)))

    barrier = pltpu.get_barrier_semaphore()
    for _, _, b, _, f, y in peers:
        pl.semaphore_signal(
            barrier, inc=1, device_id=at(b, f, 2 * y + core), device_id_type=pl.DeviceIdType.MESH
        )
    pl.semaphore_signal(
        barrier, inc=1, device_id=at(batch, frame, other_core),
        device_id_type=pl.DeviceIdType.MESH,
    )
    pl.semaphore_wait(barrier, len(peers) + 1)

    def copy(src, dst, one, two, target):
        item = pltpu.make_async_remote_copy(
            src_ref=src, dst_ref=dst, send_sem=one, recv_sem=two,
            device_id=target, device_id_type=pl.DeviceIdType.MESH,
        )
        item.start()
        return item

    chunks = [(out_ref, out_far_ref, out_sum, 0, out_ref.shape[1])]
    chunks += [
        (qkv_ref, qkv_far_ref, qkv_sum, start, qkv_ref.shape[1])
        for start in range(0, qkv_ref.shape[0], 256)
    ]
    piece = 32

    def rows(start, count):
        return pl.ds(pl.multiple_of(start, piece), count)

    sent = []
    x_copies = []
    for k, (own, other, _, base, lanes) in enumerate(chunks):
        here = rows(base + other_x * 128, 128)
        x_away[k, :, :lanes] = (own[here, :] + other[here, :].astype(f32)).astype(bf16)
        x_copies.append(
            copy(
                x_away.at[k], x_got.at[k], send.at[k, 0], recv.at[k, 0],
                at(other_x, frame, tensor),
            )
        )
    mods = (s1_ref, c1_ref, g1_ref, s2_ref, c2_ref, g2_ref)
    width = small.shape[3]
    small[...] = jnp.zeros_like(small)
    for c in range(2):
        for y in range(2):
            start = (2 * y + c) * width
            for j, ref in enumerate(mods):
                small[c, y, 4 * j : 4 * j + 4, :] = ref[:, 0, start : start + width]
            for j in range(4):
                part = slice(j * width, (j + 1) * width)
                small[c, y, 31 + j : 32 + j, :] = bias_out_ref[:, part]
                small[c, y, 35 + j : 36 + j, :] = bias_fc2_ref[:, part]
    core_copy = copy(
        small.at[1 - core], small_got, small_send.at[15], small_recv.at[15],
        at(batch, frame, other_core),
    )
    token_copies = []
    for flip, gap, b, spot, f, y in peers:
        if not flip:
            token_copies.append(
                copy(
                    tokens_ref.at[spot], tokens_out.at[place],
                    token_send.at[gap - 1], token_recv.at[gap - 1],
                    at(batch, f, 2 * y + core),
                )
            )
    tokens_out[place] = tokens_ref[place]
    core_copy.wait()
    for y in range(2):
        small_low[y] = (small[core, y] + small_got[y]).astype(bf16)
    for j in range(3):
        part = slice(j * width, (j + 1) * width)
        small_low[far, 24 + j : 25 + j, :] = bias_qkv_ref[:, part].astype(bf16)
        small_low[1 - far, 24 + j : 25 + j, :] = bias_qkv_far_ref[:, part].astype(bf16)
    for j in range(4):
        part = slice(j * width, (j + 1) * width)
        small_low[far, 27 + j : 28 + j, :] = bias_fc1_ref[:, part].astype(bf16)
    for y in range(2):
        small_low[y, 48:64, :] = cond_ref[...].astype(bf16)
    slot = 8 * batch + place
    small_copies = []
    for n, (_, _, b, _, f, y) in enumerate(peers):
        small_copies.append(
            copy(
                small_low.at[y], gathered.at[slot], small_send.at[n], small_recv.at[n],
                at(b, f, 2 * y + core),
            )
        )
    gathered[slot] = small_low[far]

    z1_copies = []
    for k, (own, other, _, base, lanes) in enumerate(chunks):
        x_copies[k].wait_recv()
        here = rows(base + batch * 128, 128)
        keep_half[k, :, :lanes] = (
            own[here, :] + other[here, :].astype(f32) + x_got[k, :, :lanes].astype(f32)
        )
        for up in range(2):
            z1_away[k, up * piece : (up + 1) * piece, :lanes] = keep_half[
                k, rows((2 * up + 1 - low) * piece, piece), :lanes
            ].astype(bf16)
        z1_copies.append(
            copy(
                z1_away.at[k], z1_got.at[k], send.at[k, 1], recv.at[k, 1],
                at(batch, frame_1, tensor),
            )
        )
    z2_copies = []
    for k, (_, _, _, _, lanes) in enumerate(chunks):
        z1_copies[k].wait_recv()
        z2_away[k, :, :lanes] = (
            keep_half[k, rows(frame_2 * piece, piece), :lanes]
            + z1_got[k, rows((1 - high) * piece, piece), :lanes].astype(f32)
        ).astype(bf16)
        z2_copies.append(
            copy(
                z2_away.at[k], z2_got.at[k], send.at[k, 2], recv.at[k, 2],
                at(batch, frame_2, tensor),
            )
        )

    def share(k, total, base, number, owner, target):
        here = rows(base + batch * 128 + owner * piece, piece)
        return copy(
            total.at[here, :], total.at[here, :], send.at[k, number], recv.at[k, number], target
        )

    shared = []
    for k, (_, _, total, base, lanes) in enumerate(chunks):
        z2_copies[k].wait_recv()
        total[rows(base + batch * 128 + frame * piece, piece), :] = (
            keep_half[k, rows(frame * piece, piece), :lanes]
            + z1_got[k, rows(high * piece, piece), :lanes].astype(f32)
            + z2_got[k, :, :lanes].astype(f32)
        ).astype(bf16)
        shared.append(
            {
                "z2": share(k, total, base, 3, frame, at(batch, frame_2, tensor)),
                "z1": share(k, total, base, 4, frame, at(batch, frame_1, tensor)),
                "x": share(k, total, base, 6, frame, at(other_x, frame, tensor)),
            }
        )
    frame_3 = lax.rem(frame_1 + 2, 4)
    for k, (_, _, total, base, lanes) in enumerate(chunks):
        shared[k]["z2"].wait_recv()
        shared[k]["z1on"] = share(k, total, base, 5, frame_2, at(batch, frame_1, tensor))
        shared[k]["x2"] = share(k, total, base, 7, frame_2, at(other_x, frame, tensor))
        shared[k]["z1"].wait_recv()
        shared[k]["x1"] = share(k, total, base, 8, frame_1, at(other_x, frame, tensor))
    for k, (_, _, total, base, lanes) in enumerate(chunks):
        shared[k]["z1on"].wait_recv()
        shared[k]["x3"] = share(k, total, base, 9, frame_3, at(other_x, frame, tensor))
    for k in range(len(chunks)):
        for name in ("x", "x2", "x1", "x3"):
            shared[k][name].wait_recv()
    for item in small_copies + token_copies:
        item.wait()
    for k in range(len(chunks)):
        x_copies[k].wait_send()
        z1_copies[k].wait_send()
        z2_copies[k].wait_send()
        for name in ("z2", "z1", "x", "z1on", "x2", "x1", "x3"):
            shared[k][name].wait_send()


def depart(qkv, qkv_far, out, out_far, tokens, mods, biases):
    f32, bf16 = jnp.float32, jnp.bfloat16
    chunks = 1 + qkv.shape[0] // 256
    lanes = max(qkv.shape[1], out.shape[1])
    cols = qkv.shape[1] // 3
    vmem = pl.BlockSpec(memory_space=pltpu.VMEM)
    inputs = [qkv, qkv_far, out, out_far, tokens, *mods, *biases]
    return pl.pallas_call(
        depart_kernel,
        in_specs=[vmem] * len(inputs),
        out_specs=[vmem] * 4,
        out_shape=[
            jax.ShapeDtypeStruct(qkv.shape, bf16),
            jax.ShapeDtypeStruct(out.shape, bf16),
            jax.ShapeDtypeStruct(tokens.shape, bf16),
            jax.ShapeDtypeStruct((16, SMALL_ROWS, cols), bf16),
        ],
        scratch_shapes=[
            pltpu.VMEM((chunks, 128, lanes), bf16),
            pltpu.VMEM((chunks, 128, lanes), bf16),
            pltpu.VMEM((chunks, 64, lanes), bf16),
            pltpu.VMEM((chunks, 64, lanes), bf16),
            pltpu.VMEM((chunks, 32, lanes), bf16),
            pltpu.VMEM((chunks, 32, lanes), bf16),
            pltpu.VMEM((chunks, 128, lanes), f32),
            pltpu.VMEM((2, 2, SMALL_ROWS, cols), f32),
            pltpu.VMEM((2, SMALL_ROWS, cols), f32),
            pltpu.VMEM((2, SMALL_ROWS, cols), bf16),
            pltpu.SemaphoreType.DMA((chunks, 10)),
            pltpu.SemaphoreType.DMA((chunks, 10)),
            pltpu.SemaphoreType.DMA((16,)),
            pltpu.SemaphoreType.DMA((16,)),
            pltpu.SemaphoreType.DMA((7,)),
            pltpu.SemaphoreType.DMA((7,)),
        ],
        compiler_params=pltpu.CompilerParams(
            collective_id=1, has_side_effects=True, vmem_limit_bytes=50 * MIB
        ),
        name="depart",
    )(*inputs)


def attend_back_kernel(
    frames, qkv_ref, grad_ref, lse_ref, tab_ref, *refs
):
    out_ref, dk_ref, dv_ref = refs[-3:]
    lanes = qkv_ref.shape[3]
    low_lane = lax.broadcasted_iota(jnp.int32, (PATCHES, lanes), 1) < HD
    scale = 1.0 / math.sqrt(HD)
    zero = jnp.bfloat16(0)
    dk_ref[...] = jnp.zeros_like(dk_ref)
    dv_ref[...] = jnp.zeros_like(dv_ref)
    for frame in range(frames):
        here = pl.ds(frame * PATCHES, PATCHES)
        length = (frame + 1) * PATCHES
        query = qkv_ref[0, 0, here, :]
        grad = grad_ref[here, :]
        keys = qkv_ref[0, 1, :length, :]
        values = qkv_ref[0, 2, :length, :]
        outs = []
        for head in range(2):
            chosen = low_lane if head == 0 else jnp.logical_not(low_lane)
            query_head = jnp.where(chosen, query, zero)
            grad_head = jnp.where(chosen, grad, zero)
            scores = lax.dot_general(
                query_head * jnp.bfloat16(scale),
                keys,
                (((1,), (1,)), ((), ())),
                preferred_element_type=jnp.float32,
            )
            prob = jnp.exp(scores - lse_ref[0, here, head : head + 1])
            prob_grad = lax.dot_general(
                grad_head, values, (((1,), (1,)), ((), ())), preferred_element_type=jnp.float32
            )
            row_dot = jnp.sum(prob * prob_grad, axis=1, keepdims=True)
            score_grad = (prob * ((prob_grad - row_dot) * scale)).astype(jnp.bfloat16)
            outs.append(jnp.dot(score_grad, keys, preferred_element_type=jnp.float32))
            dk_ref[:length, :] += lax.dot_general(
                score_grad,
                query_head,
                (((0,), (0,)), ((), ())),
                preferred_element_type=jnp.float32,
            )
            dv_ref[:length, :] += lax.dot_general(
                prob.astype(jnp.bfloat16),
                grad_head,
                (((0,), (0,)), ((), ())),
                preferred_element_type=jnp.float32,
            )
        out_ref[0, here, :] = turn(
            jnp.where(low_lane, outs[0], outs[1]), lambda slot: tab_ref[slot, here, :], -1
        ).astype(jnp.bfloat16)
    out_ref[1] = turn(dk_ref[...], lambda slot: tab_ref[slot], -1).astype(jnp.bfloat16)
    out_ref[2] = dv_ref[...].astype(jnp.bfloat16)


def attend_back(qkv, grad, lse, tables, frames, side, *deps):
    count, cols = grad.shape
    pairs = cols // 128
    return pl.pallas_call(
        partial(attend_back_kernel, frames),
        grid=(pairs,),
        in_specs=[
            pl.BlockSpec((1, 3, count, 128), lambda i: (i + pairs * side, 0, 0, 0)),
            pl.BlockSpec((count, 128), lambda i: (0, i)),
            pl.BlockSpec((1, count, 2), lambda i: (i + pairs * side, 0, 0)),
            pl.BlockSpec(tables.shape, lambda i: (0, 0, 0)),
        ]
        + [ANY] * len(deps),
        out_specs=pl.BlockSpec((3, count, 128), lambda i: (0, 0, i)),
        out_shape=jax.ShapeDtypeStruct((3, count, cols), jnp.bfloat16),
        scratch_shapes=[
            pltpu.VMEM((count, 128), jnp.float32),
            pltpu.VMEM((count, 128), jnp.float32),
        ],
        compiler_params=pltpu.CompilerParams(vmem_limit_bytes=48 * MIB),
        cost_estimate=pl.CostEstimate(
            flops=24_000_000_000, bytes_accessed=6 * MIB, transcendentals=2_600_000
        ),
        name="attend_back",
    )(qkv, grad, lse, tables, *deps)


def fast_body(
    tokens,
    noise_level,
    w_ada,
    b_ada,
    w_qkv,
    b_qkv,
    w_out,
    b_out,
    w_fc1,
    b_fc1,
    w_fc2,
    b_fc2,
    cotangent,
):
    clips, _, quarter, width = tokens.shape
    frames = lax.axis_size("frame")
    cols = w_qkv.shape[2]
    batch_now = lax.axis_index("batch")
    frame_now = lax.axis_index("frame")
    tensor_now = lax.axis_index("tensor")
    core = tensor_now % 2
    far = tensor_now // 2
    clip_now = frame_now * 2 + far
    rows_own = clips * quarter
    count = 2 * rows_own
    f32 = jnp.float32
    bf16 = jnp.bfloat16
    groups = [
        [f * 4 + 2 * y + c for f in range(frames) for y in range(2)] for c in range(2)
    ]

    def to_clip(item):
        return lax.all_to_all(item, ("frame", "tensor"), 0, 0, axis_index_groups=groups)

    def swap_y(item):
        return lax.ppermute(item, "tensor", [(t, t ^ 2) for t in range(4)])

    def swap_core(item):
        return lax.ppermute(item, "tensor", [(t, t ^ 1) for t in range(4)])

    def swap_x(item):
        return lax.ppermute(item, "batch", [(0, 1), (1, 0)])

    def swap_z(item, bit):
        return lax.ppermute(item, "frame", [(f, f ^ bit) for f in range(frames)])

    def ordered(mine, theirs, place):
        return jnp.stack(
            [jnp.where(place == 0, mine, theirs), jnp.where(place == 0, theirs, mine)]
        )

    def both_cores(item):
        return jnp.concatenate([item, swap_core(item)], axis=1).reshape(count, width)

    def sum_cores(term):
        split = term.reshape(frames, 2, rows_own // frames, width)
        return split[:, 0] + swap_core(split[:, 1].astype(bf16)).astype(f32)

    condition = jax.nn.silu(embedding(noise_level, width)).astype(bf16)
    mod_part = jnp.einsum(
        "cfd,dke->cfke", condition, w_ada, preferred_element_type=f32
    ) + b_ada.astype(f32)
    message = jnp.concatenate(
        [
            mod_part[:, 0],
            condition.astype(f32).reshape(clips, 4, cols),
            jnp.zeros((clips, 6, cols), f32),
        ],
        axis=1,
    )
    tables = rotary_tables(core, frames)
    two = jnp.stack([tables[0], (tables[2] + tables[4]) - (tables[1] + tables[3])])
    shape = (frames, 2 * quarter, width)
    line = (frames, 1, width)
    (
        cond_own, p0, p1, p2, p3, p4, p5, fc1_bias_own, fc2_bias_part,
        tokens_own, attn_rows, w_qkv_both, w_out_far, qkv, mixed, lse, cot_own, grads, mlp_rows,
        attn_branch, resid_one, activated, pre_grad, in_near, in_other, in_far,
    ) = forward(
        tokens[:, 0], message, w_qkv, b_qkv.reshape(1, 3 * cols), two,
        w_out, b_out, b_fc1, w_fc1, w_fc2, cotangent[:, 0],
    )
    pieces = [p0, p1, p2, p3, p4, p5]
    tokens_own, cot_own = tokens_own.reshape(shape), cot_own.reshape(shape)
    attn_branch, resid_one = attn_branch.reshape(shape), resid_one.reshape(shape)
    in_back = swap_y(in_far).reshape(shape)

    def outer(left, right):
        return lax.dot_general(
            left.reshape(2 * count, left.shape[2]), right.reshape(2 * count, right.shape[2]),
            TN, preferred_element_type=f32,
        )

    fc2_own = outer(activated, grads).astype(bf16)
    fc1_own = outer(mlp_rows, pre_grad).astype(bf16)
    fc2_sum, fc1_sum = lax.psum((fc2_own, fc1_own), ("batch", "frame"))

    def branch_parts(activated):
        term = jnp.dot(activated, w_fc2, preferred_element_type=f32)
        term = term.reshape(frames, 2, 2 * quarter, width)
        return term[:, 0], swap_core(term[:, 1].astype(bf16))

    far_near, far_other = branch_parts(activated[1])
    branch_back = swap_y((far_near + far_other.astype(f32)).astype(bf16))
    branch_near, branch_other = branch_parts(activated[0])

    def second_back(ins, outs):
        near, other, back, resid, cot, branch, gate, scale = (item[0].astype(f32) for item in ins)
        grad = near + other + back
        unit, root = normal(resid)
        outs[0][0] = jnp.sum(grad, axis=0, keepdims=True)
        outs[1][0] = jnp.sum(grad * unit, axis=0, keepdims=True)
        through = cot + normal_back(grad * (1.0 + scale), unit, root)
        outs[2][0] = through
        low = (gate * through).astype(bf16)
        outs[3][0] = low
        outs[4][0] = jnp.sum(through * branch, axis=0, keepdims=True)
        outs[5][0] = jnp.sum(low.astype(f32), axis=0, keepdims=True)

    shift_two_grad, scale_two_grad, resid_grad, attn_grad, gate_one_grad, out_bias = by_frame(
        second_back,
        [in_near.reshape(shape), in_other.reshape(shape), in_back, resid_one, cot_own, attn_branch]
        + [pieces[2], pieces[4]],
        [(line, f32), (line, f32), (shape, f32), (shape, bf16), (line, f32), (line, f32)],
        [fc1_own, fc2_own, far_near, branch_near],
        name="second_back",
    )
    out_bias_part = jnp.sum(out_bias, axis=(0, 1))
    attn_grad_rows = both_cores(attn_grad)

    def last_gate(ins, outs):
        near, other, back, bias, resid, gate, cot = (item[0].astype(f32) for item in ins)
        branch = near + other + back + bias
        outs[0][0] = (resid + gate * branch).astype(bf16)
        outs[1][0] = jnp.sum(cot * branch, axis=0, keepdims=True)

    def back_mixed(w):
        return lax.dot_general(
            attn_grad_rows, w, (((1,), (1,)), ((), ())), preferred_element_type=f32
        ).astype(bf16)

    def out_outer(mixed):
        return lax.dot_general(
            mixed, attn_grad_rows, (((0,), (0,)), ((), ())), preferred_element_type=f32
        )

    def heads_back(side, mixed_grad, *deps):
        back = attend_back(qkv, mixed_grad, lse, tables, frames, side, *deps)
        back = back.transpose(1, 0, 2).reshape(count, 3 * cols)
        qkv_grad = lax.dot_general(attn_rows, back, TN, preferred_element_type=f32)
        in_term = lax.dot_general(back, w_qkv_both[side], NT, preferred_element_type=f32)
        return back, qkv_grad, jnp.sum(back.astype(f32), axis=0), in_term

    out_arrived = swap_y(out_outer(mixed[1]).astype(bf16))
    mixed_grad_far = back_mixed(w_out_far)
    mixed_grad_own = back_mixed(w_out)
    back_far, qkv_grad_far, qkv_bias_far, attn_in_far = heads_back(
        1, mixed_grad_far, mixed_grad_own
    )
    qkv_low_far = qkv_grad_far.astype(bf16)
    qkv_arrived = swap_y(qkv_low_far)
    output_own, gate_two_grad = by_frame(
        last_gate,
        [branch_near, branch_other, branch_back, b_fc2.reshape(1, 1, width), resid_one]
        + [pieces[5], cot_own],
        [(shape, bf16), (line, f32)],
        [back_far],
        name="last_gate",
    )
    output = to_clip(output_own.reshape(clips, quarter, width))
    back_own, qkv_grad_own, qkv_bias_own, attn_in_own = heads_back(
        0, mixed_grad_own, qkv_low_far, output_own
    )
    in_term = (attn_in_own + attn_in_far).reshape(frames, 2, 2 * quarter, width)

    def first_back(ins, outs):
        near, other, value, above, scale = (item[0].astype(f32) for item in ins)
        grad = near + other
        unit, root = normal(value)
        outs[0][0] = jnp.sum(grad, axis=0, keepdims=True)
        outs[1][0] = jnp.sum(grad * unit, axis=0, keepdims=True)
        outs[2][0] = (above + normal_back(grad * (1.0 + scale), unit, root)).astype(bf16)

    shift_one_grad, scale_one_grad, tokens_low = by_frame(
        first_back,
        [in_term[:, 0], swap_core(in_term[:, 1].astype(bf16)), tokens_own, resid_grad, pieces[1]],
        [(line, f32), (line, f32), (shape, bf16)],
        name="first_back",
    )
    mods = [shift_one_grad, scale_one_grad, gate_one_grad]
    mods += [shift_two_grad, scale_two_grad, gate_two_grad]
    biases = [qkv_bias_own, qkv_bias_far, fc1_bias_own, out_bias_part, fc2_bias_part]
    biases = [item.reshape(1, -1) for item in biases] + [cond_own]
    qkv_sum, out_sum, tokens_grad, gathered = depart(
        qkv_grad_own, qkv_arrived, out_outer(mixed[0]), out_arrived,
        tokens_low.reshape(clips, quarter, width), mods, biases,
    )
    condition_all = gathered[:, 48:64].reshape(16 * frames, width)
    mod_all = gathered[:, : 6 * frames].reshape(16, 6, frames, cols).transpose(0, 2, 1, 3)
    ada_grad = lax.dot_general(
        condition_all,
        mod_all.reshape(16 * frames, 6 * cols),
        (((0,), (0,)), ((), ())),
        preferred_element_type=f32,
    ).reshape(width, 6, cols)
    rows_sum = jnp.sum(gathered.astype(f32), axis=0)
    ada_bias_grad = jnp.sum(rows_sum[: 6 * frames].reshape(6, frames, cols), axis=1)
    hidden_rows = fc1_bias_own.shape[1] // cols
    return (
        output[:, None],
        tokens_grad.astype(f32)[:, None],
        ada_grad,
        ada_bias_grad,
        qkv_sum.astype(f32).reshape(width, 3, cols),
        rows_sum[24:27],
        out_sum.astype(f32),
        rows_sum[31:35].reshape(width),
        fc1_sum.astype(f32),
        rows_sum[27 : 27 + hidden_rows].reshape(4 * cols),
        fc2_sum.astype(f32),
        rows_sum[35:39].reshape(width),
    )


def pick_body(tokens, *rest):
    paired = (
        lax.axis_size("tensor") == 4
        and lax.axis_size("frame") == 4
        and lax.axis_size("batch") == 2
        and tokens.shape[0] == 8
        and rest[1].shape[0] % 256 == 0
        and rest[3].shape[2] % 128 == 0
    )
    return fast_body(tokens, *rest) if paired else general_body(tokens, *rest)


def solution(mesh):
    return jax.shard_map(
        pick_body,
        mesh=mesh,
        in_specs=(
            P("batch", "frame", "tensor", None),
            P("batch", "frame"),
            P(None, None, "tensor"),
            P(None, "tensor"),
            P(None, None, "tensor"),
            P(None, "tensor"),
            P("tensor", None),
            P(),
            P(None, "tensor"),
            P("tensor"),
            P("tensor", None),
            P(),
            P("batch", "frame", "tensor", None),
        ),
        out_specs=(
            P("batch", "frame", "tensor", None),
            P("batch", "frame", "tensor", None),
            P(None, None, "tensor"),
            P(None, "tensor"),
            P(None, None, "tensor"),
            P(None, "tensor"),
            P("tensor", None),
            P(),
            P(None, "tensor"),
            P("tensor"),
            P("tensor", None),
            P(),
        ),
        check_vma=False,
    )
```

```python
from functools import partial
import math

import jax
import jax.numpy as jnp
import numpy as np
from jax import lax
from jax.experimental import pallas as pl
from jax.experimental.pallas import tpu as pltpu
from jax.sharding import PartitionSpec as P

HD = 64
GRID = 16
PATCHES = 256


epsilon = 1e-06


def frequencies(count):
    return 10000.0 ** (-(jnp.arange(count, dtype=jnp.float32) / count))


def rotate_half(segment, position):
    half = segment.shape[-1] // 2
    angle = position[..., None] * frequencies(half)
    cosine = jnp.cos(angle)
    sine = jnp.sin(angle)
    first = segment[..., :half]
    second = segment[..., half:]
    return jnp.concatenate(
        [first * cosine - second * sine, first * sine + second * cosine], axis=-1
    )


def rotary(vector, frame_pos, row_pos, col_pos):
    width = vector.shape[-1]
    first = width // 4
    middle = (width - first) // 2
    return jnp.concatenate(
        [
            rotate_half(vector[..., :first], frame_pos),
            rotate_half(vector[..., first : first + middle], row_pos),
            rotate_half(vector[..., first + middle :], col_pos),
        ],
        axis=-1,
    )


def embedding(level, width):
    half = width // 2
    angle = 1000.0 * level[..., None] * frequencies(half)
    return jnp.concatenate([jnp.cos(angle), jnp.sin(angle)], axis=-1)


def normalize(value):
    center = value - jnp.mean(value, axis=-1, keepdims=True)
    spread = jnp.mean(center * center, axis=-1, keepdims=True)
    return center * lax.rsqrt(spread + epsilon)


def modulate(value, shift, scale):
    return normalize(value) * (1.0 + scale) + shift


def general_body(
    tokens,
    noise_level,
    w_ada,
    b_ada,
    w_qkv,
    b_qkv,
    w_out,
    b_out,
    w_fc1,
    b_fc1,
    w_fc2,
    b_fc2,
    cotangent,
):
    clips = tokens.shape[0]
    width = tokens.shape[3]
    head_cols = w_qkv.shape[2]
    heads_here = head_cols // HD
    frames = lax.axis_size("frame")
    frame_now = lax.axis_index("frame")
    scale = 1.0 / math.sqrt(HD)
    condition = jax.nn.silu(embedding(noise_level, width)).astype(jnp.bfloat16)
    mod_part = jnp.einsum(
        "cfd,dke->cfke", condition, w_ada, preferred_element_type=jnp.float32
    ) + b_ada.astype(jnp.float32)
    modulation = lax.all_gather(mod_part, "tensor", axis=3, tiled=True)
    pieces = [modulation[:, :, slot : slot + 1, :] for slot in range(6)]
    resid_in = tokens.astype(jnp.float32)
    attn_val, ln_one_back = jax.vjp(modulate, resid_in, pieces[0], pieces[1])
    attn_rows = lax.all_gather(attn_val.astype(jnp.bfloat16), "tensor", axis=2, tiled=True)
    projected = jnp.einsum(
        "cfpd,dke->cfpke", attn_rows, w_qkv, preferred_element_type=jnp.float32
    ) + b_qkv.astype(jnp.float32)
    projected = projected[:, 0]
    patch_ids = jnp.arange(PATCHES)
    row_pos = (patch_ids // GRID).astype(jnp.float32)[:, None]
    col_pos = (patch_ids % GRID).astype(jnp.float32)[:, None]
    frame_pos = frame_now.astype(jnp.float32)

    def turned(vector):
        return rotary(vector.reshape(clips, PATCHES, heads_here, HD), frame_pos, row_pos, col_pos)

    query_rot, query_back = jax.vjp(turned, projected[:, :, 0])
    key_rot, key_back = jax.vjp(turned, projected[:, :, 1])
    queries = query_rot.astype(jnp.bfloat16).reshape(clips, PATCHES, head_cols)
    keys_here = key_rot.astype(jnp.bfloat16).reshape(clips, PATCHES, head_cols)
    values_here = projected[:, :, 2].astype(jnp.bfloat16)
    kv_own = jnp.concatenate([keys_here, values_here], axis=-1)[:, None]
    allowed = jnp.arange(frames * PATCHES) // PATCHES <= frame_now
    kv_all = lax.all_gather(kv_own, "frame", axis=1, tiled=True)

    def fetch(index):
        return lax.dynamic_index_in_dim(kv_all, index, 0, False)

    def score_block(query_clip, kv_clip):
        keys = kv_clip[..., :head_cols].reshape(frames * PATCHES, heads_here, HD)
        values = kv_clip[..., head_cols:].reshape(frames * PATCHES, heads_here, HD)
        scores = (
            jnp.einsum(
                "qhd,khd->hqk",
                query_clip.reshape(PATCHES, heads_here, HD),
                keys,
                preferred_element_type=jnp.float32,
            )
            * scale
        )
        return (jnp.where(allowed[None, None, :], scores, -1e30), keys, values)

    def forward_step(carry, index):
        query_clip = lax.dynamic_index_in_dim(queries, index, 0, False)
        scores, keys, values = score_block(query_clip, fetch(index))
        row_max = jnp.max(scores, axis=-1, keepdims=True)
        exp_scores = jnp.exp(scores - row_max)
        row_sum = jnp.sum(exp_scores, axis=-1, keepdims=True)
        prob_map = exp_scores / row_sum
        mixed = jnp.einsum(
            "hqk,khd->qhd",
            prob_map.astype(jnp.bfloat16),
            values,
            preferred_element_type=jnp.float32,
        ).reshape(PATCHES, head_cols)
        return (carry, (mixed, (row_max + jnp.log(row_sum))[..., 0]))

    _, (mixed_all, log_sums) = lax.scan(forward_step, None, jnp.arange(clips))
    mixed_low = mixed_all.astype(jnp.bfloat16)
    attn_term = jnp.einsum("cpj,jd->cpd", mixed_low, w_out, preferred_element_type=jnp.float32)[
        :, None
    ]
    attn_branch = lax.psum_scatter(
        attn_term, "tensor", scatter_dimension=2, tiled=True
    ) + b_out.astype(jnp.float32)
    resid_one = resid_in + pieces[2] * attn_branch
    mlp_val, ln_two_back = jax.vjp(modulate, resid_one, pieces[3], pieces[4])
    mlp_rows = lax.all_gather(mlp_val.astype(jnp.bfloat16), "tensor", axis=2, tiled=True)
    pre_act = jnp.einsum(
        "cfpd,dj->cfpj", mlp_rows, w_fc1, preferred_element_type=jnp.float32
    ) + b_fc1.astype(jnp.float32)
    act_val, gelu_back = jax.vjp(partial(jax.nn.gelu, approximate=True), pre_act)
    activated = act_val.astype(jnp.bfloat16)
    mlp_term = jnp.einsum("cfpj,jd->cfpd", activated, w_fc2, preferred_element_type=jnp.float32)
    mlp_branch = lax.psum_scatter(
        mlp_term, "tensor", scatter_dimension=2, tiled=True
    ) + b_fc2.astype(jnp.float32)
    output = (resid_one + pieces[5] * mlp_branch).astype(jnp.bfloat16)
    upstream = cotangent.astype(jnp.float32)
    mlp_grad = (pieces[5] * upstream).astype(jnp.bfloat16)
    gate_two_grad = jnp.sum(upstream * mlp_branch, axis=2, keepdims=True)
    mlp_grad_rows = lax.all_gather(mlp_grad, "tensor", axis=2, tiled=True)
    fc2_grad = jnp.einsum(
        "cfpj,cfpd->jd", activated, mlp_grad_rows, preferred_element_type=jnp.float32
    )
    fc2_bias_grad = jnp.sum(mlp_grad_rows.astype(jnp.float32), axis=(0, 1, 2))
    act_grad = jnp.einsum("cfpd,jd->cfpj", mlp_grad_rows, w_fc2, preferred_element_type=jnp.float32)
    pre_grad = gelu_back(act_grad)[0].astype(jnp.bfloat16)
    fc1_grad = jnp.einsum("cfpd,cfpj->dj", mlp_rows, pre_grad, preferred_element_type=jnp.float32)
    fc1_bias_grad = jnp.sum(pre_grad.astype(jnp.float32), axis=(0, 1, 2))
    mlp_in_term = jnp.einsum("cfpj,dj->cfpd", pre_grad, w_fc1, preferred_element_type=jnp.float32)
    mlp_in_grad = lax.psum_scatter(mlp_in_term, "tensor", scatter_dimension=2, tiled=True)
    resid_part, shift_two_grad, scale_two_grad = ln_two_back(mlp_in_grad)
    resid_grad = upstream + resid_part
    attn_grad = (pieces[2] * resid_grad).astype(jnp.bfloat16)
    gate_one_grad = jnp.sum(resid_grad * attn_branch, axis=2, keepdims=True)
    attn_grad_rows = lax.all_gather(attn_grad, "tensor", axis=2, tiled=True)[:, 0]
    out_grad = jnp.einsum(
        "cpj,cpd->jd", mixed_low, attn_grad_rows, preferred_element_type=jnp.float32
    )
    out_bias_grad = jnp.sum(attn_grad_rows.astype(jnp.float32), axis=(0, 1))
    mixed_grad = jnp.einsum(
        "cpd,jd->cpj", attn_grad_rows, w_out, preferred_element_type=jnp.float32
    ).astype(jnp.bfloat16)

    def query_side(index):
        query_clip = lax.dynamic_index_in_dim(queries, index, 0, False)
        grad_clip = lax.dynamic_index_in_dim(mixed_grad, index, 0, False)
        lse_clip = lax.dynamic_index_in_dim(log_sums, index, 0, False)
        scores, keys, values = score_block(query_clip, fetch(index))
        prob_map = jnp.exp(scores - lse_clip[..., None])
        grad_heads = grad_clip.reshape(PATCHES, heads_here, HD)
        prob_grad = jnp.einsum(
            "qhd,khd->hqk", grad_heads, values, preferred_element_type=jnp.float32
        )
        row_dot = jnp.sum(prob_map * prob_grad, axis=-1, keepdims=True)
        score_grad = (scale * prob_map * (prob_grad - row_dot)).astype(jnp.bfloat16)
        query_grad = jnp.einsum(
            "hqk,khd->qhd", score_grad, keys, preferred_element_type=jnp.float32
        ).reshape(PATCHES, head_cols)
        return (query_clip, grad_heads, prob_map, score_grad, row_dot, query_grad)

    def backward_step(carry, index):
        query_clip, grad_heads, prob_map, score_grad, row_dot, query_grad = query_side(index)
        key_grad = jnp.einsum(
            "hqk,qhd->khd",
            score_grad,
            query_clip.reshape(PATCHES, heads_here, HD),
            preferred_element_type=jnp.float32,
        ).reshape(frames, PATCHES, head_cols)
        value_grad = jnp.einsum(
            "hqk,qhd->khd",
            prob_map.astype(jnp.bfloat16),
            grad_heads,
            preferred_element_type=jnp.float32,
        ).reshape(frames, PATCHES, head_cols)
        owned = lax.psum_scatter(
            jnp.concatenate([key_grad, value_grad], axis=-1),
            "frame",
            scatter_dimension=0,
            tiled=True,
        )
        return (carry, (query_grad, owned[0]))

    _, (query_grads, kv_grads) = lax.scan(backward_step, None, jnp.arange(clips))
    query_raw_grad = query_back(query_grads.reshape(clips, PATCHES, heads_here, HD))[0]
    key_raw_grad = key_back(kv_grads[..., :head_cols].reshape(clips, PATCHES, heads_here, HD))[0]
    projected_grad = jnp.stack([query_raw_grad, key_raw_grad, kv_grads[..., head_cols:]], axis=2)
    projected_grad = projected_grad.astype(jnp.bfloat16)[:, None]
    qkv_grad = jnp.einsum(
        "cfpd,cfpke->dke", attn_rows, projected_grad, preferred_element_type=jnp.float32
    )
    qkv_bias_grad = jnp.sum(projected_grad.astype(jnp.float32), axis=(0, 1, 2))
    attn_in_term = jnp.einsum(
        "cfpke,dke->cfpd", projected_grad, w_qkv, preferred_element_type=jnp.float32
    )
    attn_in_grad = lax.psum_scatter(attn_in_term, "tensor", scatter_dimension=2, tiled=True)
    input_part, shift_one_grad, scale_one_grad = ln_one_back(attn_in_grad)
    tokens_grad = resid_grad + input_part
    mod_grad_part = jnp.concatenate(
        [
            shift_one_grad,
            scale_one_grad,
            gate_one_grad,
            shift_two_grad,
            scale_two_grad,
            gate_two_grad,
        ],
        axis=2,
    )
    mod_grad = lax.psum_scatter(mod_grad_part, "tensor", scatter_dimension=3, tiled=True)
    ada_grad = jnp.einsum(
        "cfd,cfke->dke", condition.astype(jnp.float32), mod_grad, precision=lax.Precision.HIGHEST
    )
    ada_bias_grad = jnp.sum(mod_grad, axis=(0, 1))
    summed = lax.psum(
        (
            ada_grad,
            ada_bias_grad,
            qkv_grad,
            qkv_bias_grad,
            out_grad,
            out_bias_grad,
            fc1_grad,
            fc1_bias_grad,
            fc2_grad,
            fc2_bias_grad,
        ),
        ("batch", "frame"),
    )
    return (
        output,
        tokens_grad,
        summed[0],
        summed[1],
        summed[2],
        summed[3],
        summed[4],
        summed[5],
        summed[6],
        summed[7],
        summed[8],
        summed[9],
    )


MIB = 1 << 20


def rotary_ladders():
    first, middle = HD // 4, (HD - HD // 4) // 2
    bounds = [(0, first), (first, middle), (first + middle, HD - first - middle)]
    ladders = []
    for slot, (start, width) in enumerate(bounds):
        half = width // 2
        powers = np.arange(half, dtype=np.float32) / np.float32(half)
        freq = (np.float32(10000.0) ** -powers).astype(np.float32)
        angle = np.arange(GRID, dtype=np.float32)[:, None] * freq[None, :]
        cosine, sine = np.cos(angle), np.sin(angle)
        table = np.zeros((5, GRID, HD), np.float32)
        up, down = (1, 2) if slot == 0 else (3, 4)
        table[0, :, start : start + half] = cosine
        table[0, :, start + half : start + width] = cosine
        table[up, :, start : start + half] = -sine
        table[down, :, start + half : start + width] = sine
        ladders.append(np.tile(table, (1, 1, 2)))
    return ladders


def half_turn(cols):
    first, middle = HD // 4, (HD - HD // 4) // 2
    one = np.zeros((HD, HD), np.float32)
    for start, width in ((0, first), (first, middle), (first + middle, HD - first - middle)):
        half = width // 2
        for k in range(half):
            one[start + half + k, start + k] = -1.0
            one[start + k, start + half + k] = 1.0
    return np.kron(np.eye(cols // HD, dtype=np.float32), one)


def rotary_tables(core, frames):
    by_frame, by_row, by_col = rotary_ladders()
    quarter = PATCHES // 4
    steps = quarter // GRID
    order = np.zeros((2, 2, 2, steps), np.int64)
    for own in range(2):
        for side in range(2):
            for far in range(2):
                order[own, side, far] = (2 * far + (own ^ side)) * steps + np.arange(steps)
    order = order.reshape(2, GRID)
    rows = jnp.where(core == 0, by_row[:, order[0]], by_row[:, order[1]])
    full = (
        jnp.asarray(by_frame)[:, :frames, None, None, :]
        + rows[:, None, :, None, :]
        + jnp.asarray(by_col)[:, None, None, :, :]
    )
    return full.reshape(5, frames * PATCHES, 2 * HD)


ANY = pl.BlockSpec(memory_space=pl.ANY)


def normal(value):
    center = value - jnp.mean(value, axis=-1, keepdims=True)
    root = lax.rsqrt(jnp.mean(center * center, axis=-1, keepdims=True) + epsilon)
    return center * root, root


def normal_back(grad, unit, root):
    tilt = jnp.mean(grad * unit, axis=-1, keepdims=True)
    return (grad - jnp.mean(grad, axis=-1, keepdims=True) - unit * tilt) * root


def places(batch, flips):
    place_now = 2 * lax.axis_index("frame") + lax.div(lax.axis_index("tensor"), 2)
    found = []
    for flip in range(flips):
        for gap in range(8):
            if flip or gap:
                spot = lax.rem(place_now + gap, 8)
                b = batch + flip - 2 * flip * batch
                found.append((b, spot, lax.div(spot, 2), lax.rem(spot, 2)))
    return found


def signal_all(targets):
    barrier = pltpu.get_barrier_semaphore()
    for target in targets:
        pl.semaphore_signal(
            barrier, inc=1, device_id=target, device_id_type=pl.DeviceIdType.MESH
        )
    pl.semaphore_wait(barrier, len(targets))


def start_copy(src, dst, send, recv, target):
    item = pltpu.make_async_remote_copy(
        src_ref=src, dst_ref=dst, send_sem=send, recv_sem=recv,
        device_id=target, device_id_type=pl.DeviceIdType.MESH,
    )
    item.start()
    return item


def attend_rows(load_query, load_key, load_value, frame, store):
    length = (frame + 1) * PATCHES
    query = load_query(frame) * jnp.bfloat16(1.0 / math.sqrt(HD))
    keys, values = load_key(length), load_value(length)
    low_lane = lax.broadcasted_iota(jnp.int32, query.shape, 1) < HD
    outs, sums = [], []
    for head in range(2):
        chosen = low_lane if head == 0 else jnp.logical_not(low_lane)
        scores = lax.dot_general(
            jnp.where(chosen, query, jnp.bfloat16(0)),
            keys,
            (((1,), (1,)), ((), ())),
            preferred_element_type=jnp.float32,
        )
        top = jnp.max(scores, axis=1, keepdims=True)
        grown = jnp.exp(scores - top)
        total = jnp.sum(grown, axis=1, keepdims=True)
        prob = (grown * (1.0 / total)).astype(jnp.bfloat16)
        outs.append(jnp.dot(prob, values, preferred_element_type=jnp.float32))
        sums.append(top + jnp.log(total))
    store(
        jnp.where(low_lane, outs[0], outs[1]).astype(jnp.bfloat16),
        jnp.concatenate(sums, axis=1),
    )


def mlp_side(pre):
    root = math.sqrt(2.0 / math.pi)
    square = pre * pre
    tanh = jnp.tanh(pre * (root + (root * 0.044715) * square))
    side = 0.5 + 0.5 * tanh
    slope = side + pre * (side * (1.0 - tanh)) * (root + (3 * root * 0.044715) * square)
    return pre * side, slope


NT = (((1,), (1,)), ((), ()))
TN = (((0,), (0,)), ((), ()))


def forward_kernel(
    tokens_ref, mod_ref, w_ref, bq_ref, two_ref, swing_ref, wo_ref, biases,
    w1_hbm, w2_hbm, cot_ref,
    cond_out, p0, p1, p2, p3, p4, p5, bias1_out, bias2_out,
    o_tok, o_rows, o_wq, o_wo, o_qkv, o_mixed, o_lse, o_cot,
    o_branch, o_resid, o_near, o_got, o_back, o_fc2, o_fc1, o_bnear, o_bfar,
    o_got0,
    tok, mods, rows, wq, wo_far, bq_far, p5_far, got0, qkv, mixed, lse, cotb, grad, mrows,
    branch, resid, t_send, t_got, wf1, wf2, act, pre_low, total, in_near, in_send, in_got, in_back, b_got,
    token_send, token_recv, cot_send, cot_recv, mod_send, mod_recv, row_send, row_recv,
    wide_send, wide_recv, frame_send, frame_recv, first_send, first_recv, local,
):
    f32, bf16 = jnp.float32, jnp.bfloat16
    batch, frame_now, tensor = (lax.axis_index(name) for name in ("batch", "frame", "tensor"))
    core, far = lax.rem(tensor, 2), lax.div(tensor, 2)
    other_core = (batch, frame_now, tensor + 1 - 2 * core)
    other_y = (batch, frame_now, lax.rem(tensor + 2, 4))
    other_x = (1 - batch, frame_now, tensor)
    low_bit = lax.rem(frame_now, 2)
    other_low = (batch, frame_now + 1 - 2 * low_bit, tensor)
    place = 2 * frame_now + far
    peers = places(batch, 1)
    targets = [(b, f, 2 * y + core) for b, _, f, y in peers]
    saves = []

    def save(src, dst):
        item = pltpu.make_async_copy(src, dst, local.at[2 + len(saves)])
        item.start()
        saves.append(item)
        return item

    load_1 = pltpu.make_async_copy(w1_hbm, wf1, local.at[0])
    load_2 = pltpu.make_async_copy(w2_hbm, wf2, local.at[1])
    load_1.start()
    load_2.start()
    signal_all(targets + [other_core, other_x])
    mod_copies, token_copies = [], []
    for n, (_, spot, _, _) in enumerate(peers):
        mod_copies.append(
            start_copy(
                mod_ref.at[spot], mods.at[core, place], mod_send.at[n], mod_recv.at[n], targets[n]
            )
        )
    for n, (_, spot, _, _) in enumerate(peers):
        token_copies.append(
            start_copy(
                tokens_ref.at[spot], tok.at[place], token_send.at[n], token_recv.at[n], targets[n]
            )
        )
    mods[core, place] = mod_ref[place]
    tok[place] = tokens_ref[place]
    cols = w_ref.shape[2]
    wide = lambda n: (wide_send.at[n], wide_recv.at[n])
    w_rows = pl.ds(pl.multiple_of(batch * (w_ref.shape[1] // 2), 128), w_ref.shape[1] // 2)
    o_rows_half = pl.ds(pl.multiple_of(batch * (cols // 2), 128), cols // 2)
    w_copies = [
        start_copy(w_ref.at[kind, w_rows, :], wq.at[kind, w_rows, :], *wide(kind), other_y)
        for kind in range(3)
    ]
    w_copies.append(
        start_copy(wo_ref.at[o_rows_half, :], wo_far.at[o_rows_half, :], *wide(3), other_y)
    )
    w_copies.append(start_copy(bq_ref, bq_far, *wide(4), other_y))
    w_onward = []

    def pass_on(n):
        w_copies[n].wait_recv()
        ref = wo_far.at[o_rows_half, :] if n == 3 else wq.at[n, w_rows, :]
        w_onward.append(start_copy(ref, ref, *wide(5 + n), other_x))

    for item in mod_copies:
        item.wait_recv()
    swap = start_copy(mods.at[core], mods.at[core], mod_send.at[7], mod_recv.at[7], other_core)
    swap.wait_recv()
    pieces = (p0, p1, p2, p3, p4, p5)
    for f in range(4):
        for y in range(2):
            for c in range(2):
                lanes = slice((2 * y + c) * cols, (2 * y + c + 1) * cols)
                for j, ref in enumerate(pieces):
                    ref[f, :, lanes] = mods[c, 2 * f + y, j : j + 1, :]
        for k in range(4):
            cond_out[4 * f + k : 4 * f + k + 1, :] = mods[0, 2 * f, 6 + k : 7 + k, :]
    gate_copy = start_copy(p5, p5_far, *wide(9), other_y)
    row_copies, cot_copies, cot_far_copies = [], [], []
    for n in range(8):
        spot = place if n == 0 else lax.rem(place + 8 - n, 8)
        if n:
            token_copies[n - 1].wait_recv()
        f, y = lax.div(spot, 2), lax.rem(spot, 2)
        unit, _ = normal(tok[spot].astype(f32))
        low = (unit * (1.0 + p1[f]) + p0[f]).astype(bf16)
        here = pl.ds(pl.multiple_of(f * 256 + y * 64, 64), 64)
        there = pl.ds(pl.multiple_of(f * 256 + y * 64 + 128, 64), 64)
        rows[here, :] = low
        row_copies.append(
            start_copy(
                rows.at[here, :], rows.at[there, :], row_send.at[n], row_recv.at[n], other_core
            )
        )
    for n, (_, spot, _, _) in enumerate(peers):
        cot_copies.append(
            start_copy(
                cot_ref.at[spot], cotb.at[0, place], cot_send.at[n], cot_recv.at[n], targets[n]
            )
        )
    cotb[0, place] = cot_ref[place]
    cotb[1, place] = cot_ref[2 * frame_now + 1 - far]
    for item in row_copies:
        item.wait_recv()
    pass_on(0)

    def project_heads(side):
        for kind in range(3):
            w = (w_ref if side == 0 else wq)[kind]
            bias = (bq_ref if side == 0 else bq_far)[:, kind * cols : (kind + 1) * cols]
            if kind < 2:
                turned = jnp.dot(w, swing_ref[...], preferred_element_type=f32).astype(bf16)
                bias_turned = jnp.dot(bias, swing_ref[...], preferred_element_type=f32)[:1]
            bias = bias[:1].astype(f32)
            for start in range(0, rows.shape[0], 512):
                here = slice(start, start + 512)
                value = jnp.dot(rows[here, :], w, preferred_element_type=f32) + bias
                if kind < 2:
                    moved = jnp.dot(rows[here, :], turned, preferred_element_type=f32)
                    moved += bias_turned
                for pair in range(2):
                    part = slice(pair * 128, (pair + 1) * 128)
                    out = value[:, part]
                    if kind < 2:
                        out = out * two_ref[0, here, :] + moved[:, part] * two_ref[1, here, :]
                    qkv[2 * side + pair, kind, here, :] = out.astype(bf16)

    def attend_pair(side, pair):
        spot = 2 * side + pair
        for f in range(4):
            here = slice(f * PATCHES, (f + 1) * PATCHES)

            def store(out, sums):
                mixed[side, here, pair * 128 : (pair + 1) * 128] = out
                lse[here, 2 * spot : 2 * spot + 2] = sums

            attend_rows(
                lambda f: qkv[spot, 0, here, :],
                lambda length: qkv[spot, 1, :length, :],
                lambda length: qkv[spot, 2, :length, :],
                f,
                store,
            )

    def to_frames(src, dst, number, target, start_there):
        found = []
        for f in range(4):
            here, there = pl.ds(256 * f, 128), pl.ds(256 * f + start_there, 128)
            found.append(
                start_copy(
                    src.at[here, :], dst.at[there, :],
                    frame_send.at[number, f], frame_recv.at[number, f], target,
                )
            )
        return found

    def gate_cot(side, gate):
        sums = jnp.zeros_like(bias2_out[...])
        for f in range(4):
            for y in range(2):
                low = (gate[f] * cotb[side, 2 * f + y].astype(f32)).astype(bf16)
                grad[side, 256 * f + 64 * y : 256 * f + 64 * y + 64, :] = low
                sums += jnp.sum(low.astype(f32), axis=0, keepdims=True)
        if side == 0:
            bias2_out[...] = sums

    pass_on(1)
    project_heads(0)
    pass_on(2)
    attend_pair(0, 0)
    pass_on(3)
    attend_pair(0, 1)
    for item in cot_copies:
        item.wait_recv()
    for n, (_, _, f, y) in enumerate(peers):
        cot_far_copies.append(
            start_copy(
                cot_ref.at[2 * f + 1 - y], cotb.at[1, place],
                cot_send.at[7 + n], cot_recv.at[7 + n], targets[n],
            )
        )
    gate_cot(0, p5)
    grad_core = to_frames(grad.at[0], grad.at[0], 0, other_core, 128)
    save(tok, o_tok)
    rows_save = save(rows, o_rows)
    save(cotb.at[0], o_cot)
    w_copies[4].wait_recv()
    for item in w_onward:
        item.wait_recv()
    save(wq, o_wq)
    save(wo_far, o_wo)
    project_heads(1)
    save(qkv, o_qkv)
    for pair in range(2):
        attend_pair(1, pair)
    save(mixed, o_mixed)
    save(lse, o_lse)
    term_core = []
    for f in range(4):
        here = slice(256 * f, 256 * f + 256)
        own = slice(128 * f, 128 * f + 128)
        term = jnp.dot(mixed[0, here, :], wo_ref[...], preferred_element_type=f32)
        term += jnp.dot(mixed[1, here, :], wo_far[...], preferred_element_type=f32)
        branch[own, :] = term[:128]
        t_send[own, :] = term[128:].astype(bf16)
        term_core.append(
            start_copy(
                t_send.at[own, :], t_got.at[own, :],
                frame_send.at[2, f], frame_recv.at[2, f], other_core,
            )
        )
    row_core, row_y = [], []
    for f in range(4):
        term_core[f].wait_recv()
        own = slice(128 * f, 128 * f + 128)
        value = branch[own, :] + t_got[own, :].astype(f32) + biases[0:1, :]
        branch[own, :] = value
        source = jnp.concatenate([tok[2 * f], tok[2 * f + 1]], axis=0).astype(f32)
        value = source + p2[f] * value
        resid[own, :] = value
        unit, _ = normal(value)
        here = pl.ds(256 * f, 128)
        mrows[0, 256 * f : 256 * f + 128, :] = (unit * (1.0 + p4[f]) + p3[f]).astype(bf16)
        row_y.append(
            start_copy(
                mrows.at[0, here, :], mrows.at[1, here, :],
                frame_send.at[4, f], frame_recv.at[4, f], other_y,
            )
        )
        row_core.append(
            start_copy(
                mrows.at[0, here, :], mrows.at[0, pl.ds(256 * f + 128, 128), :],
                frame_send.at[5, f], frame_recv.at[5, f], other_core,
            )
        )
    save(branch, o_branch)
    resid_save = save(resid, o_resid)
    load_1.wait()
    load_2.wait()
    units = wf1.shape[1]
    step = 256

    def hidden_block(side, first):
        here = slice(first, first + 512)
        for start in range(0, units, step):
            part = slice(start, start + step)
            pre = jnp.dot(mrows[side, here, :], wf1[:, part], preferred_element_type=f32)
            pre += biases[1:2, part]
            back = lax.dot_general(
                grad[side, here, :], wf2[part, :], NT, preferred_element_type=f32
            )
            value, slope = mlp_side(pre)
            act[side, here, part] = value.astype(bf16)
            low = (back * slope).astype(bf16)
            pre_low[side, here, part] = low
            sums = jnp.sum(low.astype(f32), axis=0, keepdims=True)
            if side == 0 and first == 0:
                bias1_out[:, part] = sums
            else:
                bias1_out[:, part] += sums
            term = lax.dot_general(low, wf1[:, part], NT, preferred_element_type=f32)
            if start == 0:
                total[here, :] = term
            else:
                total[here, :] += term

    def swap_terms(side, block):
        for f in (2 * block, 2 * block + 1):
            own = slice(128 * f, 128 * f + 128)
            in_send[side, own, :] = total[256 * f + 128 : 256 * f + 256, :].astype(bf16)
            if side == 0:
                in_near[own, :] = total[256 * f : 256 * f + 128, :]
        part = pl.ds(256 * block, 256)
        return start_copy(
            in_send.at[side, part, :], in_got.at[side, part, :],
            *wide(10 + 2 * side + block), other_core,
        )

    for item in row_core + grad_core:
        item.wait_recv()
    hidden_block(0, 0)
    near_swaps = [swap_terms(0, 0)]
    for item in cot_far_copies:
        item.wait_recv()
    gate_copy.wait_recv()
    gate_cot(1, p5_far)
    far_core = to_frames(grad.at[1], grad.at[1], 3, other_core, 128)
    hidden_block(0, 512)
    near_swaps.append(swap_terms(0, 1))
    save(in_near, o_near)
    for item in far_core:
        item.wait_recv()
    far_swaps, back_copies, rows_far_core = [], [], []

    def far_rows(block):
        for f in (2 * block, 2 * block + 1):
            row_y[f].wait_recv()
            rows_far_core.append(
                start_copy(
                    mrows.at[1, pl.ds(256 * f, 128), :], mrows.at[1, pl.ds(256 * f + 128, 128), :],
                    frame_send.at[6, f], frame_recv.at[6, f], other_core,
                )
            )

    def far_return(block):
        far_swaps[block].wait_recv()
        for f in (2 * block, 2 * block + 1):
            own = slice(128 * f, 128 * f + 128)
            t_got[own, :] = (
                total[256 * f : 256 * f + 128, :] + in_got[1, own, :].astype(f32)
            ).astype(bf16)
        part = pl.ds(256 * block, 256)
        back_copies.append(
            start_copy(t_got.at[part, :], in_back.at[part, :], *wide(14 + block), other_y)
        )

    far_rows(0)
    rows_far_core[0].wait_recv()
    rows_far_core[1].wait_recv()
    hidden_block(1, 0)
    far_swaps.append(swap_terms(1, 0))
    far_rows(1)
    far_return(0)
    rows_far_core[2].wait_recv()
    rows_far_core[3].wait_recv()
    hidden_block(1, 512)
    far_swaps.append(swap_terms(1, 1))
    for item in near_swaps:
        item.wait_recv()
    save(in_got.at[0], o_got)
    far_return(1)
    rows_save.wait()
    resid_save.wait()
    for item in near_swaps + far_swaps + term_core + row_copies:
        item.wait_send()
    firsts = []

    def outer(left, right, out, base, bit, target):
        for k in range(4):
            part = slice(256 * k, 256 * k + 256)
            value = lax.dot_general(
                left[0, :, part], right[0], TN, preferred_element_type=f32
            ) + lax.dot_general(left[1, :, part], right[1], TN, preferred_element_type=f32)
            out[part, :] = value.astype(bf16)
            away = pl.ds(pl.multiple_of(256 * k + (1 - bit) * 128, 128), 128)
            firsts.append(
                start_copy(
                    out.at[away, :], got0.at[base + k],
                    first_send.at[base + k], first_recv.at[base + k], target,
                )
            )

    outer(act, grad, rows, 0, batch, other_x)
    save(rows, o_fc2)
    outer(mrows, pre_low, wf1, 4, low_bit, other_low)
    save(wf1, o_fc1)
    branch_swaps = []
    for side in (1, 0):
        for f in range(4):
            own = slice(128 * f, 128 * f + 128)
            here = slice(256 * f, 256 * f + 256)
            value = jnp.dot(act[side, here, :], wf2[...], preferred_element_type=f32)
            (resid if side == 0 else total)[own, :] = value[:128]
            in_send[side, own, :] = value[128:].astype(bf16)
        branch_swaps.append(
            start_copy(
                in_send.at[side], b_got.at[side], *wide(16 + side), other_core,
            )
        )
    for item in branch_swaps:
        item.wait_recv()
    resid[...] = resid[...] + b_got[0].astype(f32)
    save(resid, o_bnear)
    t_send[...] = (total[: resid.shape[0], :] + b_got[1].astype(f32)).astype(bf16)
    save(t_send, o_bfar)
    for item in back_copies:
        item.wait_recv()
    save(in_back, o_back)
    for item in firsts:
        item.wait_recv()
    save(got0, o_got0)
    remote = mod_copies + token_copies + w_copies + w_onward + [swap, gate_copy]
    remote += cot_copies + cot_far_copies + grad_core + far_core + row_core + row_y
    for item in remote + rows_far_core + back_copies + branch_swaps + firsts:
        item.wait_send()
    for item in saves:
        if item is not rows_save and item is not resid_save:
            item.wait()


def forward(tokens, mod, w_qkv, b_qkv, two, w_out, biases, w_fc1, w_fc2, cot):
    f32, bf16 = jnp.float32, jnp.bfloat16
    clips, quarter, width = tokens.shape
    cols = mod.shape[2]
    units = w_fc1.shape[1]
    count = 2 * clips * quarter
    half = count // 2
    vmem = pl.BlockSpec(memory_space=pltpu.VMEM)
    like = jax.ShapeDtypeStruct
    swing = jnp.asarray(half_turn(cols), bf16)
    small = [like((16, cols), f32)] + [like((4, 1, width), f32)] * 6
    small += [like((1, units), f32), like((1, width), f32)]
    inside = dict(
        grad=((2, count, width), bf16), mrows=((2, count, width), bf16),
        act=((2, count, units), bf16), pre=((2, count, units), bf16),
    )
    buffers = dict(
        tok=((8, 64, width), bf16), rows=((count, width), bf16),
        wq=((3, width, cols), bf16), wo=((cols, width), bf16),
        qkv=((4, 3, count, 128), bf16), mixed=((2, count, cols), bf16),
        lse=((count, 8), f32), cot=((8, 64, width), bf16),
        branch=((half, width), f32), resid=((half, width), f32),
        near=((half, width), f32), got=((half, width), bf16), back=((half, width), bf16),
        fc2=((units, width), bf16), fc1=((width, units), bf16),
        bnear=((half, width), f32), bfar=((half, width), bf16),
        got0=((8, 128, width), bf16),
    )
    shape = {name: pltpu.VMEM(*item) for name, item in {**inside, **buffers}.items()}
    dma = lambda *dims: pltpu.SemaphoreType.DMA(dims)
    return pl.pallas_call(
        forward_kernel,
        in_specs=[vmem] * 8 + [ANY] * 2 + [vmem],
        out_specs=[vmem] * len(small) + [ANY] * len(buffers),
        out_shape=small + [like(*item) for item in buffers.values()],
        scratch_shapes=[
            shape["tok"], pltpu.VMEM((2,) + mod.shape, f32), shape["rows"], shape["wq"],
            shape["wo"], pltpu.VMEM((16, 3 * cols), bf16), pltpu.VMEM((4, 1, width), f32),
            shape["got0"], shape["qkv"], shape["mixed"],
            shape["lse"], pltpu.VMEM((2,) + tokens.shape, bf16), shape["grad"], shape["mrows"], shape["branch"],
            shape["resid"], shape["got"], shape["got"],
            pltpu.VMEM((width, units), bf16), pltpu.VMEM((units, width), bf16),
            shape["act"], shape["pre"], pltpu.VMEM((count, width), f32), shape["near"],
            pltpu.VMEM((2, half, width), bf16), pltpu.VMEM((2, half, width), bf16),
            shape["back"], pltpu.VMEM((2, half, width), bf16),
            dma(7), dma(7), dma(14), dma(14), dma(8), dma(8), dma(8), dma(8),
            dma(18), dma(18), dma(7, 4), dma(7, 4), dma(8), dma(8), dma(24),
        ],
        compiler_params=pltpu.CompilerParams(
            collective_id=2, has_side_effects=True, vmem_limit_bytes=63 * MIB
        ),
        name="forward",
    )(
        tokens, mod, w_qkv, jnp.broadcast_to(b_qkv, (16, 3 * cols)), two, swing, w_out,
        biases, w_fc1, w_fc2, cot,
    )


def turn_back(value, two, rows):
    lane = lax.rem(lax.broadcasted_iota(jnp.int32, (1, 128), 1), HD)
    first, middle = HD // 4, (HD - HD // 4) // 2
    near, far = first // 2, middle // 2
    swung = value * two[1, rows, :]
    moved = jnp.where(
        lane < near,
        pltpu.roll(swung, 128 - near, 1),
        jnp.where(
            lane < first,
            -pltpu.roll(swung, near, 1),
            jnp.where(
                lax.rem(lane + middle - first, middle) < far,
                pltpu.roll(swung, 128 - far, 1),
                -pltpu.roll(swung, far, 1),
            ),
        ),
    )
    return value * two[0, rows, :] + moved


SMALL_ROWS = 64


def backward_kernel(
    p1, p2, p4, p5, two, cond_ref, bias1_ref, bias2_ref, b2_ref,
    h_fc2, h_fc1, h_near, h_other, h_back, h_resid, h_cot, h_branch, h_bnear, h_bfar,
    h_wo, h_wo_far, h_mixed, h_qkv, h_lse, h_wq, h_wq_far, h_rows, h_tok, h_got0,
    gathered, o_fc2, o_fc1, o_qkv, o_out, o_tokens, o_output,
    fc2, fc1, near, other, back_in, resid, cot, branch, bnear, bfar,
    wo, mixed, qkv, lse, wq, rows, tok,
    agrows, mgrad, back, dk, dv, far_low, far_got, arrived, out_far, out_far_got, out_arrived,
    qkv_tot, out_tot,
    t_send, t_got, blanded, tokens_low, tokens_out, out_low, out_landed,
    got0, got1, got2, gq0, gq1, gq2, mod_grads, sums, small, small_got, small_low,
    load, store, own_sem, msend, mrecv, csend, crecv, ysend, yrecv, fsend, frecv, ssend, srecv, tsend, trecv,
    osend, orecv,
):
    f32, bf16 = jnp.float32, jnp.bfloat16
    batch, frame, tensor = (lax.axis_index(name) for name in ("batch", "frame", "tensor"))
    core, far = lax.rem(tensor, 2), lax.div(tensor, 2)
    low, high = lax.rem(frame, 2), lax.div(frame, 2)
    place = 2 * frame + far
    other_core = (batch, frame, tensor + 1 - 2 * core)
    other_y = (batch, frame, lax.rem(tensor + 2, 4))
    peers = places(batch, 2)
    targets = [(b, f, 2 * y + core) for b, _, f, y in peers]
    ways = {
        "x": (batch, (1 - batch, frame, tensor)),
        "low": (low, (batch, frame + 1 - 2 * low, tensor)),
        "high": (high, (batch, lax.rem(frame + 2, 4), tensor)),
    }
    loads = {}
    sources = (
        ("got0", h_got0, got0.at[pl.ds(0, 8), 0]), ("fc2", h_fc2, fc2.at[0]),
        ("fc1", h_fc1, fc1.at[0]), ("near", h_near, near),
        ("other", h_other, other), ("back", h_back, back_in), ("resid", h_resid, resid),
        ("cot", h_cot, cot), ("branch", h_branch, branch), ("bfar", h_bfar, bfar),
        ("wo", h_wo, wo.at[0]), ("wo_far", h_wo_far, wo.at[1]), ("mixed", h_mixed, mixed), ("qkv", h_qkv, qkv), ("lse", h_lse, lse),
        ("rows", h_rows, rows), ("bnear", h_bnear, bnear), ("wq", h_wq, wq.at[0]), ("wq_far", h_wq_far, wq.at[1]),
        ("tok", h_tok, tok),
    )
    for n, (name, src, dst) in enumerate(sources):
        loads[name] = pltpu.make_async_copy(src, dst, load.at[n])
        loads[name].start()
    signal_all(targets + [other_core])

    remote, saves = [], []

    def send(src, dst, one, two_, target):
        item = start_copy(src, dst, one, two_, target)
        remote.append(item)
        return item

    def save(src, dst):
        item = pltpu.make_async_copy(src, dst, store.at[len(saves)])
        item.start()
        saves.append(item)

    class Chunk:
        def __init__(self, number, buffer, out, base, stride, order, got, extra=None):
            self.k, self.buffer, self.got, self.extra = number, buffer, got, extra
            self.out = out
            self.bits = [ways[name][0] for name in order]
            self.partners = [ways[name][1] for name in order]
            self.starts, self.away = [base], []
            for bit, step in zip(self.bits, (stride, 64, 32)):
                self.away.append(self.starts[-1] + (1 - bit) * step)
                self.starts.append(self.starts[-1] + bit * step)
            self.copy = None

        def rows(self, start, size):
            return pl.ds(pl.multiple_of(start, 32), size)

        def sum_of(self, level, start, size):
            total = self.buffer[:, self.rows(start, size), :].astype(f32)
            for step in range(level):
                inside = start - self.starts[step + 1]
                total += self.got[step][:, self.rows(inside, size), :].astype(f32)
            if self.extra is not None:
                ref, first_row = self.extra
                total += ref[:, self.rows(start - first_row, size), :].astype(f32)
            return total

        def halve(self, level):
            size = (128, 64, 32)[level]
            here = self.rows(self.away[level], size)
            if level:
                if self.copy is not None:
                    self.copy.wait_recv()
                self.buffer[:, here, :] = self.sum_of(level, self.away[level], size).astype(bf16)
            self.copy = send(
                self.buffer.at[:, here, :], self.got[level],
                msend.at[self.k, level], mrecv.at[self.k, level], self.partners[level],
            )

        def join(self, level):
            size = (128, 64, 32)[level]
            self.copy.wait_recv()
            here = self.rows(self.starts[level + 1], size)
            source = self.out
            if level == 2:
                self.buffer[:, here, :] = self.sum_of(3, self.starts[3], 32).astype(bf16)
                source = self.buffer
                self.own = pltpu.make_async_copy(
                    source.at[:, here, :], self.out.at[:, here, :], own_sem.at[self.k]
                )
                self.own.start()
            if level == 1:
                self.own.wait()
            self.copy = send(
                source.at[:, here, :], self.out.at[:, here, :],
                msend.at[self.k, 3 + level], mrecv.at[self.k, 3 + level], self.partners[level],
            )

        def advance(self, phase):
            if phase < 3:
                self.halve(phase)
            elif phase < 6:
                self.join(5 - phase)
            else:
                self.copy.wait_recv()

    class Away:
        def __init__(self, number, low_ref, got, landed_ref):
            self.n, self.low, self.got, self.landed = number, low_ref, got, landed_ref
            self.half = low_ref.shape[1] // 2

        def rows(self, bit):
            return pl.ds(pl.multiple_of(bit * self.half, 128), self.half)

        def start(self):
            self.copy = send(
                self.low.at[:, self.rows(1 - batch), :], self.got,
                fsend.at[self.n, 0], frecv.at[self.n, 0], ways["x"][1],
            )

        def pass_on(self):
            self.copy.wait_recv()
            here = self.rows(batch)
            total = self.low[:, here, :].astype(f32) + self.got[...].astype(f32)
            self.low[:, here, :] = total.astype(bf16)
            self.copy = send(
                self.low.at[:, here, :], self.landed, fsend.at[self.n, 1], frecv.at[self.n, 1],
                other_y,
            )

        def finish(self):
            self.copy.wait_recv()

    def wide_got(k):
        return [got0.at[k], got1.at[k], got2.at[k]]

    x_first, z_first = ("x", "low", "high"), ("low", "x", "high")
    second = [Chunk(k, fc2, o_fc2, 256 * k, 128, x_first, wide_got(k)) for k in range(4)]
    first = [Chunk(4 + k, fc1, o_fc1, 256 * k, 128, z_first, wide_got(4 + k)) for k in range(4)]
    pairs = [item for both in zip(second, first) for item in both]
    for name in ("got0", "fc2", "fc1"):
        loads[name].wait()
    for item in pairs:
        item.advance(1)
    loads["bfar"].wait()
    b_copy = send(bfar, blanded, ysend.at[0], yrecv.at[0], other_y)

    for name in ("near", "other", "back", "resid", "cot", "branch", "bnear"):
        loads[name].wait()
    out_bias = jnp.zeros((1, agrows.shape[1]), f32)
    row_copies = []
    for f in range(4):
        own = slice(128 * f, 128 * f + 128)
        grad = near[own, :] + other[own, :].astype(f32) + back_in[own, :].astype(f32)
        unit, root = normal(resid[own, :])
        mod_grads[3, f : f + 1, :] = jnp.sum(grad, axis=0, keepdims=True)
        mod_grads[4, f : f + 1, :] = jnp.sum(grad * unit, axis=0, keepdims=True)
        source = jnp.concatenate([cot[2 * f], cot[2 * f + 1]], axis=0).astype(f32)
        side = bnear[own, :] + b2_ref[2:3, :]
        mod_grads[5, f : f + 1, :] = jnp.sum(source * side, axis=0, keepdims=True)
        bnear[own, :] = resid[own, :] + p5[f] * side
        through = source + normal_back(grad * (1.0 + p4[f]), unit, root)
        resid[own, :] = through
        value = (p2[f] * through).astype(bf16)
        agrows[256 * f : 256 * f + 128, :] = value
        mod_grads[2, f : f + 1, :] = jnp.sum(through * branch[own, :], axis=0, keepdims=True)
        out_bias += jnp.sum(value.astype(f32), axis=0, keepdims=True)
        row_copies.append(
            send(
                agrows.at[pl.ds(256 * f, 128), :], agrows.at[pl.ds(256 * f + 128, 128), :],
                csend.at[f], crecv.at[f], other_core,
            )
        )
    sums[0:1, :] = out_bias
    loads["wo"].wait()
    loads["wo_far"].wait()
    loads["mixed"].wait()
    for item in row_copies:
        item.wait_recv()
    for side in (1, 0):
        mgrad[side] = lax.dot_general(
            agrows[...], wo[side], NT, preferred_element_type=f32
        ).astype(bf16)
    out_far[0] = lax.dot_general(
        mixed[1], agrows[...], TN, preferred_element_type=f32
    ).astype(bf16)
    out_away = Away(0, out_far, out_far_got, out_arrived)
    out_away.start()
    loads["qkv"].wait()
    loads["lse"].wait()
    scale = 1.0 / math.sqrt(HD)

    def attend_back_pair(side, pair):
        spot = 2 * side + pair
        part = slice(pair * 128, (pair + 1) * 128)
        dk[...] = jnp.zeros_like(dk)
        dv[...] = jnp.zeros_like(dv)
        low_lane = lax.broadcasted_iota(jnp.int32, (PATCHES, 128), 1) < HD
        zero = jnp.bfloat16(0)
        for f in range(4):
            here = slice(f * PATCHES, (f + 1) * PATCHES)
            length = (f + 1) * PATCHES
            query, grad = qkv[spot, 0, here, :], mgrad[side, here, part]
            keys, values = qkv[spot, 1, :length, :], qkv[spot, 2, :length, :]
            outs = []
            for head in range(2):
                chosen = low_lane if head == 0 else jnp.logical_not(low_lane)
                query_head = jnp.where(chosen, query, zero)
                grad_head = jnp.where(chosen, grad, zero)
                scores = lax.dot_general(
                    query_head * jnp.bfloat16(scale), keys, NT, preferred_element_type=f32
                )
                column = 2 * spot + head
                prob = jnp.exp(scores - lse[here, column : column + 1])
                prob_grad = lax.dot_general(grad_head, values, NT, preferred_element_type=f32)
                row_dot = jnp.sum(prob * prob_grad, axis=1, keepdims=True)
                score_grad = (prob * ((prob_grad - row_dot) * scale)).astype(bf16)
                outs.append(jnp.dot(score_grad, keys, preferred_element_type=f32))
                dk[:length, :] += lax.dot_general(
                    score_grad, query_head, TN, preferred_element_type=f32
                )
                dv[:length, :] += lax.dot_general(
                    prob.astype(bf16), grad_head, TN, preferred_element_type=f32
                )
            back[side, 0, here, part] = turn_back(
                jnp.where(low_lane, outs[0], outs[1]), two, here
            ).astype(bf16)
        back[side, 1, :, part] = turn_back(dk[...], two, slice(0, 4 * PATCHES)).astype(bf16)
        back[side, 2, :, part] = dv[...].astype(bf16)

    def progress(items, phase):
        for item in items:
            item.advance(phase)

    progress(pairs, 2)
    attend_back_pair(1, 0)
    out_away.pass_on()
    attend_back_pair(1, 1)
    loads["rows"].wait()
    for kind in range(3):
        far_low[kind] = lax.dot_general(
            rows[...], back[1, kind], TN, preferred_element_type=f32
        ).astype(bf16)
    qkv_away = Away(1, far_low, far_got, arrived)
    qkv_away.start()
    progress(pairs[:4], 3)
    out_tot[0] = lax.dot_general(
        mixed[0], agrows[...], TN, preferred_element_type=f32
    ).astype(bf16)
    half_row = batch * 128
    late = [Chunk(8, out_tot, o_out, 0, 128, x_first, wide_got(8), (out_arrived, half_row))]
    progress(late, 0)
    progress(pairs[4:], 3)
    attend_back_pair(0, 0)
    b_copy.wait_recv()
    for f in range(4):
        own = slice(128 * f, 128 * f + 128)
        value = blanded[own, :].astype(f32)
        source = jnp.concatenate([cot[2 * f], cot[2 * f + 1]], axis=0).astype(f32)
        mod_grads[5, f : f + 1, :] += jnp.sum(source * value, axis=0, keepdims=True)
        value = (bnear[own, :] + p5[f] * value).astype(bf16)
        out_low[2 * f] = value[:64]
        out_low[2 * f + 1] = value[64:]
    landed = []

    def return_rows(src, dst, one, two_):
        for n, (_, spot, _, _) in enumerate(peers[:7]):
            landed.append(
                send(src.at[spot], dst.at[place], one.at[n], two_.at[n], targets[n])
            )
        dst[place] = src[place]

    progress(pairs[:4], 4)
    return_rows(out_low, out_landed, osend, orecv)
    attend_back_pair(0, 1)
    qkv_away.pass_on()
    for kind in range(3):
        qkv_tot[kind] = lax.dot_general(
            rows[...], back[0, kind], TN, preferred_element_type=f32
        ).astype(bf16)
    half_row = batch * 512
    last = [
        Chunk(
            9 + k, qkv_tot, o_qkv, 128 * k, 512, x_first, [gq0.at[k], gq1.at[k], gq2.at[k]],
            (arrived, half_row),
        )
        for k in range(4)
    ]
    progress(last, 0)
    progress(pairs[4:], 4)
    out_away.finish()
    progress(late, 1)
    loads["wq"].wait()
    loads["wq_far"].wait()
    term_copies = []
    for block in range(2):
        here = slice(512 * block, 512 * block + 512)
        total = None
        for side in range(2):
            for kind in range(3):
                term = lax.dot_general(
                    back[side, kind, here, :], wq[side, kind], NT,
                    preferred_element_type=f32,
                )
                total = term if total is None else total + term
        for f in range(2 * block, 2 * block + 2):
            own = slice(128 * f, 128 * f + 128)
            start = 256 * (f - 2 * block)
            near[own, :] = total[start : start + 128, :]
            t_send[own, :] = total[start + 128 : start + 256, :].astype(bf16)
            term_copies.append(
                send(
                    t_send.at[own, :], t_got.at[own, :],
                    csend.at[4 + f], crecv.at[4 + f], other_core,
                )
            )
    progress(pairs, 5)
    progress(late, 2)
    loads["tok"].wait()
    for f in range(4):
        term_copies[f].wait_recv()
        own = slice(128 * f, 128 * f + 128)
        grad = near[own, :] + t_got[own, :].astype(f32)
        source = jnp.concatenate([tok[2 * f], tok[2 * f + 1]], axis=0).astype(f32)
        unit, root = normal(source)
        mod_grads[0, f : f + 1, :] = jnp.sum(grad, axis=0, keepdims=True)
        mod_grads[1, f : f + 1, :] = jnp.sum(grad * unit, axis=0, keepdims=True)
        value = resid[own, :] + normal_back(grad * (1.0 + p1[f]), unit, root)
        value = value.astype(bf16)
        tokens_low[2 * f] = value[:64]
        tokens_low[2 * f + 1] = value[64:]
    width = small.shape[3]
    small[...] = jnp.zeros_like(small)
    for c in range(2):
        for y in range(2):
            start = (2 * y + c) * width
            for j in range(6):
                small[c, y, 4 * j : 4 * j + 4, :] = mod_grads[j, :, start : start + width]
            for j in range(4):
                part = slice(j * width, (j + 1) * width)
                small[c, y, 31 + j : 32 + j, :] = sums[0:1, part]
                small[c, y, 35 + j : 36 + j, :] = bias2_ref[:, part]
    core_copy = send(small.at[1 - core], small_got, csend.at[8], crecv.at[8], other_core)
    qkv_away.finish()
    progress(last, 1)
    return_rows(tokens_low, tokens_out, tsend, trecv)
    progress(late, 3)
    core_copy.wait_recv()
    for y in range(2):
        small_low[y] = (small[core, y] + small_got[y]).astype(bf16)
    for j in range(3):
        for side, spot in ((0, far), (1, 1 - far)):
            value = jnp.sum(back[side, j].astype(f32), axis=0, keepdims=True)
            small_low[spot, 24 + j : 25 + j, :] = value.astype(bf16)
    for j in range(4):
        part = slice(j * width, (j + 1) * width)
        small_low[far, 27 + j : 28 + j, :] = bias1_ref[:, part].astype(bf16)
    for y in range(2):
        small_low[y, 48:64, :] = cond_ref[...].astype(bf16)
    slot = 8 * batch + place
    for n, (_, _, _, y) in enumerate(peers):
        landed.append(
            send(small_low.at[y], gathered.at[slot], ssend.at[n], srecv.at[n], targets[n])
        )
    gathered[slot] = small_low[far]
    progress(last, 2)
    progress(late, 4)
    progress(last, 3)
    progress(late, 5)
    progress(last, 4)
    progress(pairs, 6)
    progress(last, 5)
    progress(late, 6)
    for item in landed:
        item.wait_recv()
    save(tokens_out, o_tokens)
    save(out_landed, o_output)
    progress(last, 6)
    for item in remote:
        item.wait_send()
    for item in saves:
        item.wait()


def backward(smalls, bigs, width, units, cols):
    f32, bf16 = jnp.float32, jnp.bfloat16
    like = jax.ShapeDtypeStruct
    count, half = 4 * PATCHES, 2 * PATCHES
    vmem = pl.BlockSpec(memory_space=pltpu.VMEM)
    mem = pltpu.VMEM
    dma = lambda *dims: pltpu.SemaphoreType.DMA(dims)
    clip = (8, 64, width)
    return pl.pallas_call(
        backward_kernel,
        in_specs=[vmem] * len(smalls) + [ANY] * len(bigs),
        out_specs=[vmem] + [ANY] * 6,
        out_shape=[
            like((16, SMALL_ROWS, cols), bf16), like((1, units, width), bf16),
            like((1, width, units), bf16), like((3, width, cols), bf16), like((1, cols, width), bf16),
            like(clip, bf16), like(clip, bf16),
        ],
        scratch_shapes=[
            mem((1, units, width), bf16), mem((1, width, units), bf16), mem((half, width), f32),
            mem((half, width), bf16), mem((half, width), bf16), mem((half, width), f32),
            mem(clip, bf16), mem((half, width), f32), mem((half, width), f32),
            mem((half, width), bf16), mem((2, cols, width), bf16), mem((2, count, cols), bf16),
            mem((4, 3, count, 128), bf16), mem((count, 8), f32), mem((2, 3, width, cols), bf16),
            mem((count, width), bf16), mem(clip, bf16),
            mem((count, width), bf16), mem((2, count, cols), bf16), mem((2, 3, count, cols), bf16),
            mem((count, 128), f32), mem((count, 128), f32), mem((3, width, cols), bf16),
            mem((3, width // 2, cols), bf16), mem((3, width // 2, cols), bf16),
            mem((1, cols, width), bf16), mem((1, cols // 2, width), bf16),
            mem((1, cols // 2, width), bf16),
            mem((3, width, cols), bf16), mem((1, cols, width), bf16), mem((half, width), bf16),
            mem((half, width), bf16), mem((half, width), bf16), mem(clip, bf16), mem(clip, bf16),
            mem(clip, bf16), mem(clip, bf16),
            mem((9, 1, 128, width), bf16), mem((9, 1, 64, width), bf16),
            mem((9, 1, 32, width), bf16), mem((4, 3, 128, cols), bf16),
            mem((4, 3, 64, cols), bf16), mem((4, 3, 32, cols), bf16),
            mem((6, 4, width), f32), mem((8, width), f32), mem((2, 2, SMALL_ROWS, cols), f32),
            mem((2, SMALL_ROWS, cols), f32), mem((2, SMALL_ROWS, cols), bf16),
            dma(24), dma(6), dma(13), dma(13, 6), dma(13, 6), dma(9), dma(9), dma(1), dma(1),
            dma(2, 2), dma(2, 2),
            dma(15), dma(15), dma(7), dma(7), dma(7), dma(7),
        ],
        compiler_params=pltpu.CompilerParams(
            collective_id=1, has_side_effects=True, vmem_limit_bytes=63 * MIB
        ),
        name="backward",
    )(*smalls, *bigs)


def fast_body(
    tokens,
    noise_level,
    w_ada,
    b_ada,
    w_qkv,
    b_qkv,
    w_out,
    b_out,
    w_fc1,
    b_fc1,
    w_fc2,
    b_fc2,
    cotangent,
):
    clips, _, quarter, width = tokens.shape
    frames = lax.axis_size("frame")
    cols = w_qkv.shape[2]
    core = lax.axis_index("tensor") % 2
    f32 = jnp.float32
    bf16 = jnp.bfloat16
    condition = jax.nn.silu(embedding(noise_level, width)).astype(bf16)
    mod_part = jnp.einsum(
        "cfd,dke->cfke", condition, w_ada, preferred_element_type=f32
    ) + b_ada.astype(f32)
    message = jnp.concatenate(
        [
            mod_part[:, 0],
            condition.astype(f32).reshape(clips, 4, cols),
            jnp.zeros((clips, 6, cols), f32),
        ],
        axis=1,
    )
    tables = rotary_tables(core, frames)
    two = jnp.stack([tables[0], (tables[2] + tables[4]) - (tables[1] + tables[3])])
    w_kinds = w_qkv.transpose(1, 0, 2)
    biases = jnp.stack([b_out, b_fc1, b_fc2]).astype(f32)
    (
        cond_own, p0, p1, p2, p3, p4, p5, fc1_bias, fc2_bias,
        tokens_own, attn_rows, w_kinds_far, w_out_far, qkv, mixed, lse, cot_own,
        attn_branch, resid_one, in_near, in_other, in_back, fc2_own, fc1_own, b_near, b_far,
        fc_got,
    ) = forward(
        tokens[:, 0], message, w_kinds, b_qkv.reshape(1, 3 * cols), two,
        w_out, biases, w_fc1, w_fc2, cotangent[:, 0],
    )
    gathered, fc2_sum, fc1_sum, qkv_sum, out_sum, tokens_grad, output = backward(
        [p1, p2, p4, p5, two, cond_own, fc1_bias, fc2_bias, biases],
        [
            fc2_own, fc1_own, in_near, in_other, in_back, resid_one, cot_own, attn_branch,
            b_near, b_far, w_out, w_out_far, mixed, qkv, lse, w_kinds,
            w_kinds_far, attn_rows, tokens_own, fc_got,
        ],
        width, w_fc1.shape[1], cols,
    )
    condition_all = gathered[:, 48:64].reshape(16 * frames, width)
    mod_all = gathered[:, : 6 * frames].reshape(16, 6, frames, cols).transpose(1, 0, 2, 3)
    ada_grad = jnp.einsum(
        "cd,kce->kde", condition_all, mod_all.reshape(6, 16 * frames, cols),
        preferred_element_type=f32,
    ).transpose(1, 0, 2)
    rows_sum = jnp.sum(gathered.astype(f32), axis=0)
    ada_bias_grad = jnp.sum(rows_sum[: 6 * frames].reshape(6, frames, cols), axis=1)
    return (
        output[:, None],
        tokens_grad.astype(f32)[:, None],
        ada_grad,
        ada_bias_grad,
        qkv_sum.astype(f32).transpose(1, 0, 2),
        rows_sum[24:27],
        out_sum[0].astype(f32),
        rows_sum[31:35].reshape(width),
        fc1_sum[0].astype(f32),
        rows_sum[27:31].reshape(4 * cols),
        fc2_sum[0].astype(f32),
        rows_sum[35:39].reshape(width),
    )


def pick_body(tokens, *rest):
    paired = (
        lax.axis_size("tensor") == 4
        and lax.axis_size("frame") == 4
        and lax.axis_size("batch") == 2
        and tokens.shape[0] == 8
        and rest[1].shape == (1024, 6, 256)
        and rest[7].shape[1] == 1024
    )
    return fast_body(tokens, *rest) if paired else general_body(tokens, *rest)


def solution(mesh):
    return jax.shard_map(
        pick_body,
        mesh=mesh,
        in_specs=(
            P("batch", "frame", "tensor", None),
            P("batch", "frame"),
            P(None, None, "tensor"),
            P(None, "tensor"),
            P(None, None, "tensor"),
            P(None, "tensor"),
            P("tensor", None),
            P(),
            P(None, "tensor"),
            P("tensor"),
            P("tensor", None),
            P(),
            P("batch", "frame", "tensor", None),
        ),
        out_specs=(
            P("batch", "frame", "tensor", None),
            P("batch", "frame", "tensor", None),
            P(None, None, "tensor"),
            P(None, "tensor"),
            P(None, None, "tensor"),
            P(None, "tensor"),
            P("tensor", None),
            P(),
            P(None, "tensor"),
            P("tensor"),
            P("tensor", None),
            P(),
        ),
        check_vma=False,
    )
```

```python
from functools import partial
import math

import jax
import jax.numpy as jnp
import numpy as np
from jax import lax
from jax.experimental import pallas as pl
from jax.experimental.pallas import tpu as pltpu
from jax.sharding import PartitionSpec as P

HD = 64
GRID = 16
PATCHES = 256


epsilon = 1e-06


def frequencies(count):
    return 10000.0 ** (-(jnp.arange(count, dtype=jnp.float32) / count))


def rotate_half(segment, position):
    half = segment.shape[-1] // 2
    angle = position[..., None] * frequencies(half)
    cosine = jnp.cos(angle)
    sine = jnp.sin(angle)
    first = segment[..., :half]
    second = segment[..., half:]
    return jnp.concatenate(
        [first * cosine - second * sine, first * sine + second * cosine], axis=-1
    )


def rotary(vector, frame_pos, row_pos, col_pos):
    width = vector.shape[-1]
    first = width // 4
    middle = (width - first) // 2
    return jnp.concatenate(
        [
            rotate_half(vector[..., :first], frame_pos),
            rotate_half(vector[..., first : first + middle], row_pos),
            rotate_half(vector[..., first + middle :], col_pos),
        ],
        axis=-1,
    )


def embedding(level, width):
    half = width // 2
    angle = 1000.0 * level[..., None] * frequencies(half)
    return jnp.concatenate([jnp.cos(angle), jnp.sin(angle)], axis=-1)


def normalize(value):
    center = value - jnp.mean(value, axis=-1, keepdims=True)
    spread = jnp.mean(center * center, axis=-1, keepdims=True)
    return center * lax.rsqrt(spread + epsilon)


def modulate(value, shift, scale):
    return normalize(value) * (1.0 + scale) + shift


def general_body(
    tokens,
    noise_level,
    w_ada,
    b_ada,
    w_qkv,
    b_qkv,
    w_out,
    b_out,
    w_fc1,
    b_fc1,
    w_fc2,
    b_fc2,
    cotangent,
):
    clips = tokens.shape[0]
    width = tokens.shape[3]
    head_cols = w_qkv.shape[2]
    heads_here = head_cols // HD
    frames = lax.axis_size("frame")
    frame_now = lax.axis_index("frame")
    scale = 1.0 / math.sqrt(HD)
    condition = jax.nn.silu(embedding(noise_level, width)).astype(jnp.bfloat16)
    mod_part = jnp.einsum(
        "cfd,dke->cfke", condition, w_ada, preferred_element_type=jnp.float32
    ) + b_ada.astype(jnp.float32)
    modulation = lax.all_gather(mod_part, "tensor", axis=3, tiled=True)
    pieces = [modulation[:, :, slot : slot + 1, :] for slot in range(6)]
    resid_in = tokens.astype(jnp.float32)
    attn_val, ln_one_back = jax.vjp(modulate, resid_in, pieces[0], pieces[1])
    attn_rows = lax.all_gather(attn_val.astype(jnp.bfloat16), "tensor", axis=2, tiled=True)
    projected = jnp.einsum(
        "cfpd,dke->cfpke", attn_rows, w_qkv, preferred_element_type=jnp.float32
    ) + b_qkv.astype(jnp.float32)
    projected = projected[:, 0]
    patch_ids = jnp.arange(PATCHES)
    row_pos = (patch_ids // GRID).astype(jnp.float32)[:, None]
    col_pos = (patch_ids % GRID).astype(jnp.float32)[:, None]
    frame_pos = frame_now.astype(jnp.float32)

    def turned(vector):
        return rotary(vector.reshape(clips, PATCHES, heads_here, HD), frame_pos, row_pos, col_pos)

    query_rot, query_back = jax.vjp(turned, projected[:, :, 0])
    key_rot, key_back = jax.vjp(turned, projected[:, :, 1])
    queries = query_rot.astype(jnp.bfloat16).reshape(clips, PATCHES, head_cols)
    keys_here = key_rot.astype(jnp.bfloat16).reshape(clips, PATCHES, head_cols)
    values_here = projected[:, :, 2].astype(jnp.bfloat16)
    kv_own = jnp.concatenate([keys_here, values_here], axis=-1)[:, None]
    allowed = jnp.arange(frames * PATCHES) // PATCHES <= frame_now
    kv_all = lax.all_gather(kv_own, "frame", axis=1, tiled=True)

    def fetch(index):
        return lax.dynamic_index_in_dim(kv_all, index, 0, False)

    def score_block(query_clip, kv_clip):
        keys = kv_clip[..., :head_cols].reshape(frames * PATCHES, heads_here, HD)
        values = kv_clip[..., head_cols:].reshape(frames * PATCHES, heads_here, HD)
        scores = (
            jnp.einsum(
                "qhd,khd->hqk",
                query_clip.reshape(PATCHES, heads_here, HD),
                keys,
                preferred_element_type=jnp.float32,
            )
            * scale
        )
        return (jnp.where(allowed[None, None, :], scores, -1e30), keys, values)

    def forward_step(carry, index):
        query_clip = lax.dynamic_index_in_dim(queries, index, 0, False)
        scores, keys, values = score_block(query_clip, fetch(index))
        row_max = jnp.max(scores, axis=-1, keepdims=True)
        exp_scores = jnp.exp(scores - row_max)
        row_sum = jnp.sum(exp_scores, axis=-1, keepdims=True)
        prob_map = exp_scores / row_sum
        mixed = jnp.einsum(
            "hqk,khd->qhd",
            prob_map.astype(jnp.bfloat16),
            values,
            preferred_element_type=jnp.float32,
        ).reshape(PATCHES, head_cols)
        return (carry, (mixed, (row_max + jnp.log(row_sum))[..., 0]))

    _, (mixed_all, log_sums) = lax.scan(forward_step, None, jnp.arange(clips))
    mixed_low = mixed_all.astype(jnp.bfloat16)
    attn_term = jnp.einsum("cpj,jd->cpd", mixed_low, w_out, preferred_element_type=jnp.float32)[
        :, None
    ]
    attn_branch = lax.psum_scatter(
        attn_term, "tensor", scatter_dimension=2, tiled=True
    ) + b_out.astype(jnp.float32)
    resid_one = resid_in + pieces[2] * attn_branch
    mlp_val, ln_two_back = jax.vjp(modulate, resid_one, pieces[3], pieces[4])
    mlp_rows = lax.all_gather(mlp_val.astype(jnp.bfloat16), "tensor", axis=2, tiled=True)
    pre_act = jnp.einsum(
        "cfpd,dj->cfpj", mlp_rows, w_fc1, preferred_element_type=jnp.float32
    ) + b_fc1.astype(jnp.float32)
    act_val, gelu_back = jax.vjp(partial(jax.nn.gelu, approximate=True), pre_act)
    activated = act_val.astype(jnp.bfloat16)
    mlp_term = jnp.einsum("cfpj,jd->cfpd", activated, w_fc2, preferred_element_type=jnp.float32)
    mlp_branch = lax.psum_scatter(
        mlp_term, "tensor", scatter_dimension=2, tiled=True
    ) + b_fc2.astype(jnp.float32)
    output = (resid_one + pieces[5] * mlp_branch).astype(jnp.bfloat16)
    upstream = cotangent.astype(jnp.float32)
    mlp_grad = (pieces[5] * upstream).astype(jnp.bfloat16)
    gate_two_grad = jnp.sum(upstream * mlp_branch, axis=2, keepdims=True)
    mlp_grad_rows = lax.all_gather(mlp_grad, "tensor", axis=2, tiled=True)
    fc2_grad = jnp.einsum(
        "cfpj,cfpd->jd", activated, mlp_grad_rows, preferred_element_type=jnp.float32
    )
    fc2_bias_grad = jnp.sum(mlp_grad_rows.astype(jnp.float32), axis=(0, 1, 2))
    act_grad = jnp.einsum("cfpd,jd->cfpj", mlp_grad_rows, w_fc2, preferred_element_type=jnp.float32)
    pre_grad = gelu_back(act_grad)[0].astype(jnp.bfloat16)
    fc1_grad = jnp.einsum("cfpd,cfpj->dj", mlp_rows, pre_grad, preferred_element_type=jnp.float32)
    fc1_bias_grad = jnp.sum(pre_grad.astype(jnp.float32), axis=(0, 1, 2))
    mlp_in_term = jnp.einsum("cfpj,dj->cfpd", pre_grad, w_fc1, preferred_element_type=jnp.float32)
    mlp_in_grad = lax.psum_scatter(mlp_in_term, "tensor", scatter_dimension=2, tiled=True)
    resid_part, shift_two_grad, scale_two_grad = ln_two_back(mlp_in_grad)
    resid_grad = upstream + resid_part
    attn_grad = (pieces[2] * resid_grad).astype(jnp.bfloat16)
    gate_one_grad = jnp.sum(resid_grad * attn_branch, axis=2, keepdims=True)
    attn_grad_rows = lax.all_gather(attn_grad, "tensor", axis=2, tiled=True)[:, 0]
    out_grad = jnp.einsum(
        "cpj,cpd->jd", mixed_low, attn_grad_rows, preferred_element_type=jnp.float32
    )
    out_bias_grad = jnp.sum(attn_grad_rows.astype(jnp.float32), axis=(0, 1))
    mixed_grad = jnp.einsum(
        "cpd,jd->cpj", attn_grad_rows, w_out, preferred_element_type=jnp.float32
    ).astype(jnp.bfloat16)

    def query_side(index):
        query_clip = lax.dynamic_index_in_dim(queries, index, 0, False)
        grad_clip = lax.dynamic_index_in_dim(mixed_grad, index, 0, False)
        lse_clip = lax.dynamic_index_in_dim(log_sums, index, 0, False)
        scores, keys, values = score_block(query_clip, fetch(index))
        prob_map = jnp.exp(scores - lse_clip[..., None])
        grad_heads = grad_clip.reshape(PATCHES, heads_here, HD)
        prob_grad = jnp.einsum(
            "qhd,khd->hqk", grad_heads, values, preferred_element_type=jnp.float32
        )
        row_dot = jnp.sum(prob_map * prob_grad, axis=-1, keepdims=True)
        score_grad = (scale * prob_map * (prob_grad - row_dot)).astype(jnp.bfloat16)
        query_grad = jnp.einsum(
            "hqk,khd->qhd", score_grad, keys, preferred_element_type=jnp.float32
        ).reshape(PATCHES, head_cols)
        return (query_clip, grad_heads, prob_map, score_grad, row_dot, query_grad)

    def backward_step(carry, index):
        query_clip, grad_heads, prob_map, score_grad, row_dot, query_grad = query_side(index)
        key_grad = jnp.einsum(
            "hqk,qhd->khd",
            score_grad,
            query_clip.reshape(PATCHES, heads_here, HD),
            preferred_element_type=jnp.float32,
        ).reshape(frames, PATCHES, head_cols)
        value_grad = jnp.einsum(
            "hqk,qhd->khd",
            prob_map.astype(jnp.bfloat16),
            grad_heads,
            preferred_element_type=jnp.float32,
        ).reshape(frames, PATCHES, head_cols)
        owned = lax.psum_scatter(
            jnp.concatenate([key_grad, value_grad], axis=-1),
            "frame",
            scatter_dimension=0,
            tiled=True,
        )
        return (carry, (query_grad, owned[0]))

    _, (query_grads, kv_grads) = lax.scan(backward_step, None, jnp.arange(clips))
    query_raw_grad = query_back(query_grads.reshape(clips, PATCHES, heads_here, HD))[0]
    key_raw_grad = key_back(kv_grads[..., :head_cols].reshape(clips, PATCHES, heads_here, HD))[0]
    projected_grad = jnp.stack([query_raw_grad, key_raw_grad, kv_grads[..., head_cols:]], axis=2)
    projected_grad = projected_grad.astype(jnp.bfloat16)[:, None]
    qkv_grad = jnp.einsum(
        "cfpd,cfpke->dke", attn_rows, projected_grad, preferred_element_type=jnp.float32
    )
    qkv_bias_grad = jnp.sum(projected_grad.astype(jnp.float32), axis=(0, 1, 2))
    attn_in_term = jnp.einsum(
        "cfpke,dke->cfpd", projected_grad, w_qkv, preferred_element_type=jnp.float32
    )
    attn_in_grad = lax.psum_scatter(attn_in_term, "tensor", scatter_dimension=2, tiled=True)
    input_part, shift_one_grad, scale_one_grad = ln_one_back(attn_in_grad)
    tokens_grad = resid_grad + input_part
    mod_grad_part = jnp.concatenate(
        [
            shift_one_grad,
            scale_one_grad,
            gate_one_grad,
            shift_two_grad,
            scale_two_grad,
            gate_two_grad,
        ],
        axis=2,
    )
    mod_grad = lax.psum_scatter(mod_grad_part, "tensor", scatter_dimension=3, tiled=True)
    ada_grad = jnp.einsum(
        "cfd,cfke->dke", condition.astype(jnp.float32), mod_grad, precision=lax.Precision.HIGHEST
    )
    ada_bias_grad = jnp.sum(mod_grad, axis=(0, 1))
    summed = lax.psum(
        (
            ada_grad,
            ada_bias_grad,
            qkv_grad,
            qkv_bias_grad,
            out_grad,
            out_bias_grad,
            fc1_grad,
            fc1_bias_grad,
            fc2_grad,
            fc2_bias_grad,
        ),
        ("batch", "frame"),
    )
    return (
        output,
        tokens_grad,
        summed[0],
        summed[1],
        summed[2],
        summed[3],
        summed[4],
        summed[5],
        summed[6],
        summed[7],
        summed[8],
        summed[9],
    )


MIB = 1 << 20


def rotary_ladders():
    first, middle = HD // 4, (HD - HD // 4) // 2
    bounds = [(0, first), (first, middle), (first + middle, HD - first - middle)]
    ladders = []
    for slot, (start, width) in enumerate(bounds):
        half = width // 2
        powers = np.arange(half, dtype=np.float32) / np.float32(half)
        freq = (np.float32(10000.0) ** -powers).astype(np.float32)
        angle = np.arange(GRID, dtype=np.float32)[:, None] * freq[None, :]
        cosine, sine = np.cos(angle), np.sin(angle)
        table = np.zeros((5, GRID, HD), np.float32)
        up, down = (1, 2) if slot == 0 else (3, 4)
        table[0, :, start : start + half] = cosine
        table[0, :, start + half : start + width] = cosine
        table[up, :, start : start + half] = -sine
        table[down, :, start + half : start + width] = sine
        ladders.append(np.tile(table, (1, 1, 2)))
    return ladders


def half_turn(cols):
    first, middle = HD // 4, (HD - HD // 4) // 2
    one = np.zeros((HD, HD), np.float32)
    for start, width in ((0, first), (first, middle), (first + middle, HD - first - middle)):
        half = width // 2
        for k in range(half):
            one[start + half + k, start + k] = -1.0
            one[start + k, start + half + k] = 1.0
    return np.kron(np.eye(cols // HD, dtype=np.float32), one)


def rotary_tables(core, frames):
    by_frame, by_row, by_col = rotary_ladders()
    quarter = PATCHES // 4
    steps = quarter // GRID
    order = np.zeros((2, 2, 2, steps), np.int64)
    for own in range(2):
        for side in range(2):
            for far in range(2):
                order[own, side, far] = (2 * far + (own ^ side)) * steps + np.arange(steps)
    order = order.reshape(2, GRID)
    rows = jnp.where(core == 0, by_row[:, order[0]], by_row[:, order[1]])
    full = (
        jnp.asarray(by_frame)[:, :frames, None, None, :]
        + rows[:, None, :, None, :]
        + jnp.asarray(by_col)[:, None, None, :, :]
    )
    return full.reshape(5, frames * PATCHES, 2 * HD)


ANY = pl.BlockSpec(memory_space=pl.ANY)


def normal(value):
    center = value - jnp.mean(value, axis=-1, keepdims=True)
    root = lax.rsqrt(jnp.mean(center * center, axis=-1, keepdims=True) + epsilon)
    return center * root, root


def normal_back(grad, unit, root):
    tilt = jnp.mean(grad * unit, axis=-1, keepdims=True)
    return (grad - jnp.mean(grad, axis=-1, keepdims=True) - unit * tilt) * root


def places(batch, flips):
    place_now = 2 * lax.axis_index("frame") + lax.div(lax.axis_index("tensor"), 2)
    found = []
    for flip in range(flips):
        for gap in range(8):
            if flip or gap:
                spot = lax.rem(place_now + gap, 8)
                b = batch + flip - 2 * flip * batch
                found.append((b, spot, lax.div(spot, 2), lax.rem(spot, 2)))
    return found


def signal_all(targets):
    barrier = pltpu.get_barrier_semaphore()
    for target in targets:
        pl.semaphore_signal(
            barrier, inc=1, device_id=target, device_id_type=pl.DeviceIdType.MESH
        )
    pl.semaphore_wait(barrier, len(targets))


def start_copy(src, dst, send, recv, target):
    item = pltpu.make_async_remote_copy(
        src_ref=src, dst_ref=dst, send_sem=send, recv_sem=recv,
        device_id=target, device_id_type=pl.DeviceIdType.MESH,
    )
    item.start()
    return item


def attend_rows(load_query, load_key, load_value, frame, store):
    length = (frame + 1) * PATCHES
    query = load_query(frame) * jnp.bfloat16(1.0 / math.sqrt(HD))
    keys, values = load_key(length), load_value(length)
    low_lane = lax.broadcasted_iota(jnp.int32, query.shape, 1) < HD
    outs, sums = [], []
    for head in range(2):
        chosen = low_lane if head == 0 else jnp.logical_not(low_lane)
        scores = lax.dot_general(
            jnp.where(chosen, query, jnp.bfloat16(0)),
            keys,
            (((1,), (1,)), ((), ())),
            preferred_element_type=jnp.float32,
        )
        top = jnp.max(scores, axis=1, keepdims=True)
        grown = jnp.exp(scores - top)
        total = jnp.sum(grown, axis=1, keepdims=True)
        prob = (grown * (1.0 / total)).astype(jnp.bfloat16)
        outs.append(jnp.dot(prob, values, preferred_element_type=jnp.float32))
        sums.append(top + jnp.log(total))
    store(
        jnp.where(low_lane, outs[0], outs[1]).astype(jnp.bfloat16),
        jnp.concatenate(sums, axis=1),
    )


def mlp_side(pre):
    root = math.sqrt(2.0 / math.pi)
    square = pre * pre
    tanh = jnp.tanh(pre * (root + (root * 0.044715) * square))
    side = 0.5 + 0.5 * tanh
    slope = side + pre * (side * (1.0 - tanh)) * (root + (3 * root * 0.044715) * square)
    return pre * side, slope


NT = (((1,), (1,)), ((), ()))
TN = (((0,), (0,)), ((), ()))


def forward_kernel(
    tokens_ref, mod_ref, w_ref, bq_ref, two_ref, swing_ref, wo_ref, biases,
    w1_hbm, w2_hbm, cot_ref,
    cond_out, p0, p1, p2, p3, p4, p5, bias1_out, bias2_out,
    o_tok, o_rows, o_wq, o_wo, o_qkv, o_mixed, o_lse, o_cot,
    o_branch, o_resid, o_near, o_got, o_back, o_fc2, o_fc1, o_bnear, o_bfar,
    o_got0,
    tok, mods, rows, wq, wo_far, bq_far, p5_far, got0, qkv, mixed, lse, cotb, grad, mrows,
    branch, resid, t_send, t_got, wf1, wf2, act, pre_low, total, in_near, in_send, in_got, in_back, b_got,
    token_send, token_recv, cot_send, cot_recv, mod_send, mod_recv, row_send, row_recv,
    wide_send, wide_recv, frame_send, frame_recv, first_send, first_recv, local,
):
    f32, bf16 = jnp.float32, jnp.bfloat16
    batch, frame_now, tensor = (lax.axis_index(name) for name in ("batch", "frame", "tensor"))
    core, far = lax.rem(tensor, 2), lax.div(tensor, 2)
    other_core = (batch, frame_now, tensor + 1 - 2 * core)
    other_y = (batch, frame_now, lax.rem(tensor + 2, 4))
    other_x = (1 - batch, frame_now, tensor)
    low_bit = lax.rem(frame_now, 2)
    other_low = (batch, frame_now + 1 - 2 * low_bit, tensor)
    place = 2 * frame_now + far
    peers = places(batch, 1)
    targets = [(b, f, 2 * y + core) for b, _, f, y in peers]
    saves = []

    def save(src, dst):
        item = pltpu.make_async_copy(src, dst, local.at[2 + len(saves)])
        item.start()
        saves.append(item)
        return item

    load_1 = pltpu.make_async_copy(w1_hbm, wf1, local.at[0])
    load_2 = pltpu.make_async_copy(w2_hbm, wf2, local.at[1])
    load_1.start()
    load_2.start()
    signal_all(targets + [other_core, other_x])
    mod_copies, token_copies = [], []
    for n, (_, spot, _, _) in enumerate(peers):
        mod_copies.append(
            start_copy(
                mod_ref.at[spot], mods.at[core, place], mod_send.at[n], mod_recv.at[n], targets[n]
            )
        )
    for n, (_, spot, _, _) in enumerate(peers):
        token_copies.append(
            start_copy(
                tokens_ref.at[spot], tok.at[place], token_send.at[n], token_recv.at[n], targets[n]
            )
        )
    mods[core, place] = mod_ref[place]
    tok[place] = tokens_ref[place]
    cols = w_ref.shape[2]
    wide = lambda n: (wide_send.at[n], wide_recv.at[n])
    w_rows = pl.ds(pl.multiple_of(batch * (w_ref.shape[1] // 2), 128), w_ref.shape[1] // 2)
    o_rows_half = pl.ds(pl.multiple_of(batch * (cols // 2), 128), cols // 2)
    w_copies = []

    def send_weights(kinds):
        for kind in kinds:
            w_copies.append(
                start_copy(w_ref.at[kind, w_rows, :], wq.at[kind, w_rows, :], *wide(kind), other_y)
            )

    send_weights((0,))
    w_onward = []

    def pass_on(n):
        w_copies[n].wait_recv()
        ref = wo_far.at[o_rows_half, :] if n == 3 else wq.at[n, w_rows, :]
        w_onward.append(start_copy(ref, ref, *wide(5 + n), other_x))

    for item in mod_copies:
        item.wait_recv()
    swap = start_copy(mods.at[core], mods.at[core], mod_send.at[7], mod_recv.at[7], other_core)
    swap.wait_recv()
    pieces = (p0, p1, p2, p3, p4, p5)
    for f in range(4):
        for y in range(2):
            for c in range(2):
                lanes = slice((2 * y + c) * cols, (2 * y + c + 1) * cols)
                for j, ref in enumerate(pieces):
                    ref[f, :, lanes] = mods[c, 2 * f + y, j : j + 1, :]
        for k in range(4):
            cond_out[4 * f + k : 4 * f + k + 1, :] = mods[0, 2 * f, 6 + k : 7 + k, :]
    gate_copy = start_copy(p5, p5_far, *wide(9), other_y)
    row_copies, cot_copies, cot_far_copies = [], [], []
    for n in range(8):
        spot = place if n == 0 else lax.rem(place + 8 - n, 8)
        if n:
            token_copies[n - 1].wait_recv()
        if n == 4:
            send_weights((1, 2))
            w_copies.append(
                start_copy(wo_ref.at[o_rows_half, :], wo_far.at[o_rows_half, :], *wide(3), other_y)
            )
            w_copies.append(start_copy(bq_ref, bq_far, *wide(4), other_y))
        f, y = lax.div(spot, 2), lax.rem(spot, 2)
        unit, _ = normal(tok[spot].astype(f32))
        low = (unit * (1.0 + p1[f]) + p0[f]).astype(bf16)
        here = pl.ds(pl.multiple_of(f * 256 + y * 64, 64), 64)
        there = pl.ds(pl.multiple_of(f * 256 + y * 64 + 128, 64), 64)
        rows[here, :] = low
        row_copies.append(
            start_copy(
                rows.at[here, :], rows.at[there, :], row_send.at[n], row_recv.at[n], other_core
            )
        )
    for n, (_, spot, _, _) in enumerate(peers):
        cot_copies.append(
            start_copy(
                cot_ref.at[spot], cotb.at[0, place], cot_send.at[n], cot_recv.at[n], targets[n]
            )
        )
    cotb[0, place] = cot_ref[place]
    cotb[1, place] = cot_ref[2 * frame_now + 1 - far]
    for item in row_copies:
        item.wait_recv()
    pass_on(0)

    def project_heads(side):
        for kind in range(3):
            w = (w_ref if side == 0 else wq)[kind]
            bias = (bq_ref if side == 0 else bq_far)[:, kind * cols : (kind + 1) * cols]
            if kind < 2:
                turned = jnp.dot(w, swing_ref[...], preferred_element_type=f32).astype(bf16)
                bias_turned = jnp.dot(bias, swing_ref[...], preferred_element_type=f32)[:1]
            bias = bias[:1].astype(f32)
            for start in range(0, rows.shape[0], 512):
                here = slice(start, start + 512)
                value = jnp.dot(rows[here, :], w, preferred_element_type=f32) + bias
                if kind < 2:
                    moved = jnp.dot(rows[here, :], turned, preferred_element_type=f32)
                    moved += bias_turned
                for pair in range(2):
                    part = slice(pair * 128, (pair + 1) * 128)
                    out = value[:, part]
                    if kind < 2:
                        out = out * two_ref[0, here, :] + moved[:, part] * two_ref[1, here, :]
                    qkv[2 * side + pair, kind, here, :] = out.astype(bf16)

    def attend_pair(side, pair):
        spot = 2 * side + pair
        for f in range(4):
            here = slice(f * PATCHES, (f + 1) * PATCHES)

            def store(out, sums):
                mixed[side, here, pair * 128 : (pair + 1) * 128] = out
                lse[here, 2 * spot : 2 * spot + 2] = sums

            attend_rows(
                lambda f: qkv[spot, 0, here, :],
                lambda length: qkv[spot, 1, :length, :],
                lambda length: qkv[spot, 2, :length, :],
                f,
                store,
            )

    def to_frames(src, dst, number, target, start_there):
        found = []
        for f in range(4):
            here, there = pl.ds(256 * f, 128), pl.ds(256 * f + start_there, 128)
            found.append(
                start_copy(
                    src.at[here, :], dst.at[there, :],
                    frame_send.at[number, f], frame_recv.at[number, f], target,
                )
            )
        return found

    def gate_cot(side, gate):
        sums = jnp.zeros_like(bias2_out[...])
        for f in range(4):
            for y in range(2):
                low = (gate[f] * cotb[side, 2 * f + y].astype(f32)).astype(bf16)
                grad[side, 256 * f + 64 * y : 256 * f + 64 * y + 64, :] = low
                sums += jnp.sum(low.astype(f32), axis=0, keepdims=True)
        if side == 0:
            bias2_out[...] = sums

    pass_on(1)
    project_heads(0)
    pass_on(2)
    attend_pair(0, 0)
    pass_on(3)
    attend_pair(0, 1)
    save(tok, o_tok)
    rows_save = save(rows, o_rows)
    w_copies[4].wait_recv()
    for item in w_onward:
        item.wait_recv()
    save(wq, o_wq)
    save(wo_far, o_wo)
    project_heads(1)
    for n, (_, _, f, y) in enumerate(peers):
        cot_far_copies.append(
            start_copy(
                cot_ref.at[2 * f + 1 - y], cotb.at[1, place],
                cot_send.at[7 + n], cot_recv.at[7 + n], targets[n],
            )
        )
    save(qkv, o_qkv)
    for pair in range(2):
        attend_pair(1, pair)
    save(mixed, o_mixed)
    save(lse, o_lse)
    term_core = []
    for f in range(4):
        here = slice(256 * f, 256 * f + 256)
        own = slice(128 * f, 128 * f + 128)
        term = jnp.dot(mixed[0, here, :], wo_ref[...], preferred_element_type=f32)
        term += jnp.dot(mixed[1, here, :], wo_far[...], preferred_element_type=f32)
        branch[own, :] = term[:128]
        t_send[own, :] = term[128:].astype(bf16)
        term_core.append(
            start_copy(
                t_send.at[own, :], t_got.at[own, :],
                frame_send.at[2, f], frame_recv.at[2, f], other_core,
            )
        )
    row_core, row_y = [], []
    for f in range(4):
        term_core[f].wait_recv()
        own = slice(128 * f, 128 * f + 128)
        value = branch[own, :] + t_got[own, :].astype(f32) + biases[0:1, :]
        branch[own, :] = value
        source = jnp.concatenate([tok[2 * f], tok[2 * f + 1]], axis=0).astype(f32)
        value = source + p2[f] * value
        resid[own, :] = value
        unit, _ = normal(value)
        here = pl.ds(256 * f, 128)
        mrows[0, 256 * f : 256 * f + 128, :] = (unit * (1.0 + p4[f]) + p3[f]).astype(bf16)
        row_y.append(
            start_copy(
                mrows.at[0, here, :], mrows.at[1, here, :],
                frame_send.at[4, f], frame_recv.at[4, f], other_y,
            )
        )
        row_core.append(
            start_copy(
                mrows.at[0, here, :], mrows.at[0, pl.ds(256 * f + 128, 128), :],
                frame_send.at[5, f], frame_recv.at[5, f], other_core,
            )
        )
    for item in cot_copies:
        item.wait_recv()
    save(cotb.at[0], o_cot)
    gate_cot(0, p5)
    grad_core = to_frames(grad.at[0], grad.at[0], 0, other_core, 128)
    save(branch, o_branch)
    resid_save = save(resid, o_resid)
    load_1.wait()
    load_2.wait()
    units = wf1.shape[1]
    step = 256

    def hidden_block(side, first, size):
        here = slice(first, first + size)
        for start in range(0, units, step):
            part = slice(start, start + step)
            pre = jnp.dot(mrows[side, here, :], wf1[:, part], preferred_element_type=f32)
            pre += biases[1:2, part]
            back = lax.dot_general(
                grad[side, here, :], wf2[part, :], NT, preferred_element_type=f32
            )
            value, slope = mlp_side(pre)
            act[side, here, part] = value.astype(bf16)
            low = (back * slope).astype(bf16)
            pre_low[side, here, part] = low
            sums = jnp.sum(low.astype(f32), axis=0, keepdims=True)
            if side == 0 and first == 0:
                bias1_out[:, part] = sums
            else:
                bias1_out[:, part] += sums
            term = lax.dot_general(low, wf1[:, part], NT, preferred_element_type=f32)
            if start == 0:
                total[here, :] = term
            else:
                total[here, :] += term

    def swap_terms(side, f):
        own = slice(128 * f, 128 * f + 128)
        in_send[side, own, :] = total[256 * f + 128 : 256 * f + 256, :].astype(bf16)
        if side == 0:
            in_near[own, :] = total[256 * f : 256 * f + 128, :]
        part = pl.ds(128 * f, 128)
        return start_copy(
            in_send.at[side, part, :], in_got.at[side, part, :],
            *wide(10 + 4 * side + f), other_core,
        )

    for item in row_core + grad_core:
        item.wait_recv()
    hidden_block(0, 0, 512)
    near_swaps = [swap_terms(0, 0), swap_terms(0, 1)]
    for item in cot_far_copies:
        item.wait_recv()
    gate_copy.wait_recv()
    gate_cot(1, p5_far)
    far_core = to_frames(grad.at[1], grad.at[1], 3, other_core, 128)
    hidden_block(0, 512, 512)
    near_swaps += [swap_terms(0, 2), swap_terms(0, 3)]
    save(in_near, o_near)
    for item in far_core:
        item.wait_recv()
    far_swaps, back_copies, rows_far_core = [], [], []

    def far_rows(f):
        row_y[f].wait_recv()
        rows_far_core.append(
            start_copy(
                mrows.at[1, pl.ds(256 * f, 128), :], mrows.at[1, pl.ds(256 * f + 128, 128), :],
                frame_send.at[6, f], frame_recv.at[6, f], other_core,
            )
        )

    def far_return(f):
        far_swaps[f].wait_recv()
        own = slice(128 * f, 128 * f + 128)
        t_got[own, :] = (
            total[256 * f : 256 * f + 128, :] + in_got[1, own, :].astype(f32)
        ).astype(bf16)
        part = pl.ds(128 * f, 128)
        back_copies.append(
            start_copy(t_got.at[part, :], in_back.at[part, :], *wide(18 + f), other_y)
        )

    far_rows(0)
    for f in range(4):
        rows_far_core[f].wait_recv()
        hidden_block(1, 256 * f, 256)
        far_swaps.append(swap_terms(1, f))
        if f < 3:
            far_rows(f + 1)
        far_return(f)
    for item in near_swaps:
        item.wait_recv()
    save(in_got.at[0], o_got)
    rows_save.wait()
    resid_save.wait()
    for item in near_swaps + far_swaps + term_core + row_copies:
        item.wait_send()
    firsts = []

    def outer(left, right, out, base, bit, target):
        for k in range(4):
            part = slice(256 * k, 256 * k + 256)
            value = lax.dot_general(
                left[0, :, part], right[0], TN, preferred_element_type=f32
            ) + lax.dot_general(left[1, :, part], right[1], TN, preferred_element_type=f32)
            out[part, :] = value.astype(bf16)
            if target is not None:
                away = pl.ds(pl.multiple_of(256 * k + (1 - bit) * 128, 128), 128)
                firsts.append(
                    start_copy(
                        out.at[away, :], got0.at[base + k],
                        first_send.at[base + k], first_recv.at[base + k], target,
                    )
                )

    outer(act, grad, rows, 0, batch, other_x)
    save(rows, o_fc2)
    outer(mrows, pre_low, wf1, 4, low_bit, other_low)
    save(wf1, o_fc1)
    branch_swaps = []
    for side in (1, 0):
        for f in range(4):
            own = slice(128 * f, 128 * f + 128)
            here = slice(256 * f, 256 * f + 256)
            value = jnp.dot(act[side, here, :], wf2[...], preferred_element_type=f32)
            (resid if side == 0 else total)[own, :] = value[:128]
            in_send[side, own, :] = value[128:].astype(bf16)
        branch_swaps.append(
            start_copy(
                in_send.at[side], b_got.at[side], *wide(22 + side), other_core,
            )
        )
    for item in branch_swaps:
        item.wait_recv()
    resid[...] = resid[...] + b_got[0].astype(f32)
    save(resid, o_bnear)
    t_send[...] = (total[: resid.shape[0], :] + b_got[1].astype(f32)).astype(bf16)
    save(t_send, o_bfar)
    for item in back_copies:
        item.wait_recv()
    save(in_back, o_back)
    for item in firsts:
        item.wait_recv()
    save(got0, o_got0)
    remote = mod_copies + token_copies + w_copies + w_onward + [swap, gate_copy]
    remote += cot_copies + cot_far_copies + grad_core + far_core + row_core + row_y
    for item in remote + rows_far_core + back_copies + branch_swaps + firsts:
        item.wait_send()
    for item in saves:
        if item is not rows_save and item is not resid_save:
            item.wait()


def forward(tokens, mod, w_qkv, b_qkv, two, w_out, biases, w_fc1, w_fc2, cot):
    f32, bf16 = jnp.float32, jnp.bfloat16
    clips, quarter, width = tokens.shape
    cols = mod.shape[2]
    units = w_fc1.shape[1]
    count = 2 * clips * quarter
    half = count // 2
    vmem = pl.BlockSpec(memory_space=pltpu.VMEM)
    like = jax.ShapeDtypeStruct
    swing = jnp.asarray(half_turn(cols), bf16)
    small = [like((16, cols), f32)] + [like((4, 1, width), f32)] * 6
    small += [like((1, units), f32), like((1, width), f32)]
    inside = dict(
        grad=((2, count, width), bf16), mrows=((2, count, width), bf16),
        act=((2, count, units), bf16), pre=((2, count, units), bf16),
    )
    buffers = dict(
        tok=((8, 64, width), bf16), rows=((count, width), bf16),
        wq=((3, width, cols), bf16), wo=((cols, width), bf16),
        qkv=((4, 3, count, 128), bf16), mixed=((2, count, cols), bf16),
        lse=((count, 8), f32), cot=((8, 64, width), bf16),
        branch=((half, width), f32), resid=((half, width), f32),
        near=((half, width), f32), got=((half, width), bf16), back=((half, width), bf16),
        fc2=((units, width), bf16), fc1=((width, units), bf16),
        bnear=((half, width), f32), bfar=((half, width), bf16),
        got0=((8, 128, width), bf16),
    )
    shape = {name: pltpu.VMEM(*item) for name, item in {**inside, **buffers}.items()}
    dma = lambda *dims: pltpu.SemaphoreType.DMA(dims)
    return pl.pallas_call(
        forward_kernel,
        in_specs=[vmem] * 8 + [ANY] * 2 + [vmem],
        out_specs=[vmem] * len(small) + [ANY] * len(buffers),
        out_shape=small + [like(*item) for item in buffers.values()],
        scratch_shapes=[
            shape["tok"], pltpu.VMEM((2,) + mod.shape, f32), shape["rows"], shape["wq"],
            shape["wo"], pltpu.VMEM((16, 3 * cols), bf16), pltpu.VMEM((4, 1, width), f32),
            shape["got0"], shape["qkv"], shape["mixed"],
            shape["lse"], pltpu.VMEM((2,) + tokens.shape, bf16), shape["grad"], shape["mrows"], shape["branch"],
            shape["resid"], shape["got"], shape["got"],
            pltpu.VMEM((width, units), bf16), pltpu.VMEM((units, width), bf16),
            shape["act"], shape["pre"], pltpu.VMEM((count, width), f32), shape["near"],
            pltpu.VMEM((2, half, width), bf16), pltpu.VMEM((2, half, width), bf16),
            shape["back"], pltpu.VMEM((2, half, width), bf16),
            dma(7), dma(7), dma(14), dma(14), dma(8), dma(8), dma(8), dma(8),
            dma(24), dma(24), dma(7, 4), dma(7, 4), dma(8), dma(8), dma(24),
        ],
        compiler_params=pltpu.CompilerParams(
            collective_id=2, has_side_effects=True, vmem_limit_bytes=63 * MIB
        ),
        name="forward",
    )(
        tokens, mod, w_qkv, jnp.broadcast_to(b_qkv, (16, 3 * cols)), two, swing, w_out,
        biases, w_fc1, w_fc2, cot,
    )


def turn_back(value, two, rows):
    lane = lax.rem(lax.broadcasted_iota(jnp.int32, (1, 128), 1), HD)
    first, middle = HD // 4, (HD - HD // 4) // 2
    near, far = first // 2, middle // 2
    swung = value * two[1, rows, :]
    moved = jnp.where(
        lane < near,
        pltpu.roll(swung, 128 - near, 1),
        jnp.where(
            lane < first,
            -pltpu.roll(swung, near, 1),
            jnp.where(
                lax.rem(lane + middle - first, middle) < far,
                pltpu.roll(swung, 128 - far, 1),
                -pltpu.roll(swung, far, 1),
            ),
        ),
    )
    return value * two[0, rows, :] + moved


SMALL_ROWS = 64


def backward_kernel(
    p1, p2, p4, p5, two, cond_ref, bias1_ref, bias2_ref, b2_ref,
    h_fc2, h_fc1, h_near, h_other, h_back, h_resid, h_cot, h_branch, h_bnear, h_bfar,
    h_wo, h_wo_far, h_mixed, h_qkv, h_lse, h_wq, h_wq_far, h_rows, h_tok, h_got0,
    mod_all, cond_all, ada_sum, qkv_bias, line_sums, o_fc2, o_fc1, o_qkv, o_out, o_tokens, o_output,
    fc2, fc1, near, other, back_in, resid, cot, branch, bnear, bfar,
    wo, mixed, qkv, lse, wq, rows, tok,
    agrows, mgrad, back, dk, dv, far_low, far_got, arrived, out_far, out_far_got, out_arrived,
    qkv_tot, out_tot,
    t_send, t_got, blanded, tokens_low, tokens_out, out_low, out_landed,
    got0, got1, got2, gq0, gq1, gq2, mod_grads, sums, small, small_got, small_low,
    gathered,
    load, store, own_sem, msend, mrecv, csend, crecv, ysend, yrecv, fsend, frecv, ssend, srecv, tsend, trecv,
    osend, orecv,
):
    f32, bf16 = jnp.float32, jnp.bfloat16
    batch, frame, tensor = (lax.axis_index(name) for name in ("batch", "frame", "tensor"))
    core, far = lax.rem(tensor, 2), lax.div(tensor, 2)
    low, high = lax.rem(frame, 2), lax.div(frame, 2)
    place = 2 * frame + far
    other_core = (batch, frame, tensor + 1 - 2 * core)
    other_y = (batch, frame, lax.rem(tensor + 2, 4))
    peers = places(batch, 2)
    targets = [(b, f, 2 * y + core) for b, _, f, y in peers]
    ways = {
        "x": (batch, (1 - batch, frame, tensor)),
        "low": (low, (batch, frame + 1 - 2 * low, tensor)),
        "high": (high, (batch, lax.rem(frame + 2, 4), tensor)),
    }
    loads = {}
    sources = (
        ("got0", h_got0, got0.at[pl.ds(0, 8), 0]), ("fc2", h_fc2, fc2.at[0]),
        ("fc1", h_fc1, fc1.at[0]), ("near", h_near, near),
        ("other", h_other, other), ("back", h_back, back_in), ("resid", h_resid, resid),
        ("cot", h_cot, cot), ("branch", h_branch, branch), ("bfar", h_bfar, bfar),
        ("wo", h_wo, wo.at[0]), ("wo_far", h_wo_far, wo.at[1]), ("mixed", h_mixed, mixed), ("qkv", h_qkv, qkv), ("lse", h_lse, lse),
        ("rows", h_rows, rows), ("bnear", h_bnear, bnear), ("wq", h_wq, wq.at[0]), ("wq_far", h_wq_far, wq.at[1]),
        ("tok", h_tok, tok),
    )
    for n, (name, src, dst) in enumerate(sources):
        loads[name] = pltpu.make_async_copy(src, dst, load.at[n])
        loads[name].start()
    signal_all(targets + [other_core])

    remote, saves = [], []

    def send(src, dst, one, two_, target):
        item = start_copy(src, dst, one, two_, target)
        remote.append(item)
        return item

    def save(src, dst):
        item = pltpu.make_async_copy(src, dst, store.at[len(saves)])
        item.start()
        saves.append(item)

    class Chunk:
        def __init__(self, number, buffer, out, base, stride, order, got, extra=None):
            self.k, self.buffer, self.got, self.extra = number, buffer, got, extra
            self.out = out
            self.bits = [ways[name][0] for name in order]
            self.partners = [ways[name][1] for name in order]
            self.starts, self.away = [base], []
            for bit, step in zip(self.bits, (stride, 64, 32)):
                self.away.append(self.starts[-1] + (1 - bit) * step)
                self.starts.append(self.starts[-1] + bit * step)
            self.copy = None

        def rows(self, start, size):
            return pl.ds(pl.multiple_of(start, 32), size)

        def sum_of(self, level, start, size):
            total = self.buffer[:, self.rows(start, size), :].astype(f32)
            for step in range(level):
                inside = start - self.starts[step + 1]
                total += self.got[step][:, self.rows(inside, size), :].astype(f32)
            if self.extra is not None:
                ref, first_row = self.extra
                total += ref[:, self.rows(start - first_row, size), :].astype(f32)
            return total

        def halve(self, level):
            size = (128, 64, 32)[level]
            here = self.rows(self.away[level], size)
            if level:
                if self.copy is not None:
                    self.copy.wait_recv()
                self.buffer[:, here, :] = self.sum_of(level, self.away[level], size).astype(bf16)
            self.copy = send(
                self.buffer.at[:, here, :], self.got[level],
                msend.at[self.k, level], mrecv.at[self.k, level], self.partners[level],
            )

        def join(self, level):
            size = (128, 64, 32)[level]
            self.copy.wait_recv()
            here = self.rows(self.starts[level + 1], size)
            source = self.out
            if level == 2:
                self.buffer[:, here, :] = self.sum_of(3, self.starts[3], 32).astype(bf16)
                source = self.buffer
                self.own = pltpu.make_async_copy(
                    source.at[:, here, :], self.out.at[:, here, :], own_sem.at[self.k]
                )
                self.own.start()
            if level == 1:
                self.own.wait()
            self.copy = send(
                source.at[:, here, :], self.out.at[:, here, :],
                msend.at[self.k, 3 + level], mrecv.at[self.k, 3 + level], self.partners[level],
            )

        def advance(self, phase):
            if phase < 3:
                self.halve(phase)
            elif phase < 6:
                self.join(5 - phase)
            else:
                self.copy.wait_recv()

    class Away:
        def __init__(self, number, low_ref, got, landed_ref):
            self.n, self.low, self.got, self.landed = number, low_ref, got, landed_ref
            self.half = low_ref.shape[1] // 2

        def rows(self, bit):
            return pl.ds(pl.multiple_of(bit * self.half, 128), self.half)

        def start(self):
            self.copy = send(
                self.low.at[:, self.rows(1 - batch), :], self.got,
                fsend.at[self.n, 0], frecv.at[self.n, 0], ways["x"][1],
            )

        def pass_on(self):
            self.copy.wait_recv()
            here = self.rows(batch)
            total = self.low[:, here, :].astype(f32) + self.got[...].astype(f32)
            self.low[:, here, :] = total.astype(bf16)
            self.copy = send(
                self.low.at[:, here, :], self.landed, fsend.at[self.n, 1], frecv.at[self.n, 1],
                other_y,
            )

        def finish(self):
            self.copy.wait_recv()

    def wide_got(k):
        return [got0.at[k], got1.at[k], got2.at[k]]

    x_first, z_first = ("x", "low", "high"), ("low", "x", "high")
    second = [Chunk(k, fc2, o_fc2, 256 * k, 128, x_first, wide_got(k)) for k in range(4)]
    first = [Chunk(4 + k, fc1, o_fc1, 256 * k, 128, z_first, wide_got(4 + k)) for k in range(4)]
    pairs = [item for both in zip(second, first) for item in both]
    for name in ("got0", "fc2", "fc1"):
        loads[name].wait()
    for item in pairs:
        item.advance(1)
    loads["bfar"].wait()
    b_copy = send(bfar, blanded, ysend.at[0], yrecv.at[0], other_y)

    for name in ("near", "other", "back", "resid", "cot", "branch", "bnear"):
        loads[name].wait()
    out_bias = jnp.zeros((1, agrows.shape[1]), f32)
    row_copies = []
    for f in range(4):
        own = slice(128 * f, 128 * f + 128)
        grad = near[own, :] + other[own, :].astype(f32) + back_in[own, :].astype(f32)
        unit, root = normal(resid[own, :])
        mod_grads[3, f : f + 1, :] = jnp.sum(grad, axis=0, keepdims=True)
        mod_grads[4, f : f + 1, :] = jnp.sum(grad * unit, axis=0, keepdims=True)
        source = jnp.concatenate([cot[2 * f], cot[2 * f + 1]], axis=0).astype(f32)
        side = bnear[own, :] + b2_ref[2:3, :]
        mod_grads[5, f : f + 1, :] = jnp.sum(source * side, axis=0, keepdims=True)
        bnear[own, :] = resid[own, :] + p5[f] * side
        through = source + normal_back(grad * (1.0 + p4[f]), unit, root)
        resid[own, :] = through
        value = (p2[f] * through).astype(bf16)
        agrows[256 * f : 256 * f + 128, :] = value
        mod_grads[2, f : f + 1, :] = jnp.sum(through * branch[own, :], axis=0, keepdims=True)
        out_bias += jnp.sum(value.astype(f32), axis=0, keepdims=True)
        row_copies.append(
            send(
                agrows.at[pl.ds(256 * f, 128), :], agrows.at[pl.ds(256 * f + 128, 128), :],
                csend.at[f], crecv.at[f], other_core,
            )
        )
    sums[0:1, :] = out_bias
    for item in pairs[:4]:
        item.advance(2)
    loads["wo"].wait()
    loads["wo_far"].wait()
    loads["mixed"].wait()
    for item in row_copies:
        item.wait_recv()
    for side in (1, 0):
        mgrad[side] = lax.dot_general(
            agrows[...], wo[side], NT, preferred_element_type=f32
        ).astype(bf16)
    out_far[0] = lax.dot_general(
        mixed[1], agrows[...], TN, preferred_element_type=f32
    ).astype(bf16)
    out_away = Away(0, out_far, out_far_got, out_arrived)
    out_away.start()
    loads["qkv"].wait()
    loads["lse"].wait()
    scale = 1.0 / math.sqrt(HD)

    def attend_back_pair(side, pair):
        spot = 2 * side + pair
        part = slice(pair * 128, (pair + 1) * 128)
        dk[...] = jnp.zeros_like(dk)
        dv[...] = jnp.zeros_like(dv)
        low_lane = lax.broadcasted_iota(jnp.int32, (PATCHES, 128), 1) < HD
        zero = jnp.bfloat16(0)
        for f in range(4):
            here = slice(f * PATCHES, (f + 1) * PATCHES)
            length = (f + 1) * PATCHES
            query, grad = qkv[spot, 0, here, :], mgrad[side, here, part]
            keys, values = qkv[spot, 1, :length, :], qkv[spot, 2, :length, :]
            outs = []
            for head in range(2):
                chosen = low_lane if head == 0 else jnp.logical_not(low_lane)
                query_head = jnp.where(chosen, query, zero)
                grad_head = jnp.where(chosen, grad, zero)
                scores = lax.dot_general(
                    query_head * jnp.bfloat16(scale), keys, NT, preferred_element_type=f32
                )
                column = 2 * spot + head
                prob = jnp.exp(scores - lse[here, column : column + 1])
                prob_grad = lax.dot_general(grad_head, values, NT, preferred_element_type=f32)
                row_dot = jnp.sum(prob * prob_grad, axis=1, keepdims=True)
                score_grad = (prob * ((prob_grad - row_dot) * scale)).astype(bf16)
                outs.append(jnp.dot(score_grad, keys, preferred_element_type=f32))
                dk[:length, :] += lax.dot_general(
                    score_grad, query_head, TN, preferred_element_type=f32
                )
                dv[:length, :] += lax.dot_general(
                    prob.astype(bf16), grad_head, TN, preferred_element_type=f32
                )
            back[side, 0, here, part] = turn_back(
                jnp.where(low_lane, outs[0], outs[1]), two, here
            ).astype(bf16)
        back[side, 1, :, part] = turn_back(dk[...], two, slice(0, 4 * PATCHES)).astype(bf16)
        back[side, 2, :, part] = dv[...].astype(bf16)

    def progress(items, phase):
        for item in items:
            item.advance(phase)

    progress(pairs[4:], 2)
    attend_back_pair(1, 0)
    progress(pairs[:4], 3)
    out_away.pass_on()
    attend_back_pair(1, 1)
    progress(pairs[4:], 3)
    loads["rows"].wait()
    for kind in range(3):
        far_low[kind] = lax.dot_general(
            rows[...], back[1, kind], TN, preferred_element_type=f32
        ).astype(bf16)
    qkv_away = Away(1, far_low, far_got, arrived)
    qkv_away.start()
    progress(pairs[:4], 4)
    out_tot[0] = lax.dot_general(
        mixed[0], agrows[...], TN, preferred_element_type=f32
    ).astype(bf16)
    half_row = batch * 128
    late = [Chunk(8, out_tot, o_out, 0, 128, x_first, wide_got(8), (out_arrived, half_row))]
    progress(late, 0)
    attend_back_pair(0, 0)
    b_copy.wait_recv()
    for f in range(4):
        own = slice(128 * f, 128 * f + 128)
        value = blanded[own, :].astype(f32)
        source = jnp.concatenate([cot[2 * f], cot[2 * f + 1]], axis=0).astype(f32)
        mod_grads[5, f : f + 1, :] += jnp.sum(source * value, axis=0, keepdims=True)
        value = (bnear[own, :] + p5[f] * value).astype(bf16)
        out_low[2 * f] = value[:64]
        out_low[2 * f + 1] = value[64:]
    landed = []

    def return_rows(src, dst, one, two_):
        for n, (_, spot, _, _) in enumerate(peers[:7]):
            landed.append(
                send(src.at[spot], dst.at[place], one.at[n], two_.at[n], targets[n])
            )
        dst[place] = src[place]

    qkv_away.pass_on()
    return_rows(out_low, out_landed, osend, orecv)
    progress(pairs[4:], 4)
    attend_back_pair(0, 1)
    for kind in range(3):
        qkv_tot[kind] = lax.dot_general(
            rows[...], back[0, kind], TN, preferred_element_type=f32
        ).astype(bf16)
    half_row = batch * 512
    last = [
        Chunk(
            9 + k, qkv_tot, o_qkv, 128 * k, 512, x_first, [gq0.at[k], gq1.at[k], gq2.at[k]],
            (arrived, half_row),
        )
        for k in range(4)
    ]
    progress(last, 0)
    out_away.finish()
    progress(late, 1)
    loads["wq"].wait()
    loads["wq_far"].wait()
    term_copies = []
    for block in range(2):
        here = slice(512 * block, 512 * block + 512)
        total = None
        for side in range(2):
            for kind in range(3):
                term = lax.dot_general(
                    back[side, kind, here, :], wq[side, kind], NT,
                    preferred_element_type=f32,
                )
                total = term if total is None else total + term
        for f in range(2 * block, 2 * block + 2):
            own = slice(128 * f, 128 * f + 128)
            start = 256 * (f - 2 * block)
            near[own, :] = total[start : start + 128, :]
            t_send[own, :] = total[start + 128 : start + 256, :].astype(bf16)
            term_copies.append(
                send(
                    t_send.at[own, :], t_got.at[own, :],
                    csend.at[4 + f], crecv.at[4 + f], other_core,
                )
            )
    progress(late, 2)
    loads["tok"].wait()
    for f in range(4):
        term_copies[f].wait_recv()
        own = slice(128 * f, 128 * f + 128)
        grad = near[own, :] + t_got[own, :].astype(f32)
        source = jnp.concatenate([tok[2 * f], tok[2 * f + 1]], axis=0).astype(f32)
        unit, root = normal(source)
        mod_grads[0, f : f + 1, :] = jnp.sum(grad, axis=0, keepdims=True)
        mod_grads[1, f : f + 1, :] = jnp.sum(grad * unit, axis=0, keepdims=True)
        value = resid[own, :] + normal_back(grad * (1.0 + p1[f]), unit, root)
        value = value.astype(bf16)
        tokens_low[2 * f] = value[:64]
        tokens_low[2 * f + 1] = value[64:]
    width = small.shape[3]
    small[...] = jnp.zeros_like(small)
    for c in range(2):
        for y in range(2):
            start = (2 * y + c) * width
            for j in range(6):
                small[c, y, 4 * j : 4 * j + 4, :] = mod_grads[j, :, start : start + width]
            for j in range(4):
                part = slice(j * width, (j + 1) * width)
                small[c, y, 31 + j : 32 + j, :] = sums[0:1, part]
                small[c, y, 35 + j : 36 + j, :] = bias2_ref[:, part]
    core_copy = send(small.at[1 - core], small_got, csend.at[8], crecv.at[8], other_core)
    qkv_away.finish()
    progress(last, 1)
    progress(late, 3)
    core_copy.wait_recv()
    for y in range(2):
        small_low[y] = (small[core, y] + small_got[y]).astype(bf16)
    for j in range(3):
        for side, spot in ((0, far), (1, 1 - far)):
            value = jnp.sum(back[side, j].astype(f32), axis=0, keepdims=True)
            small_low[spot, 24 + j : 25 + j, :] = value.astype(bf16)
    for j in range(4):
        part = slice(j * width, (j + 1) * width)
        small_low[far, 27 + j : 28 + j, :] = bias1_ref[:, part].astype(bf16)
    for y in range(2):
        small_low[y, 48:64, :] = cond_ref[...].astype(bf16)
    progress(pairs, 5)
    return_rows(tokens_low, tokens_out, tsend, trecv)
    progress(last, 2)
    progress(late, 4)
    progress(last, 3)
    slot = 8 * batch + place
    for n, (_, _, _, y) in enumerate(peers):
        landed.append(
            send(small_low.at[y], gathered.at[slot], ssend.at[n], srecv.at[n], targets[n])
        )
    gathered[slot] = small_low[far]
    progress(late, 5)
    progress(last, 4)
    progress(pairs, 6)
    progress(last, 5)
    progress(late, 6)
    for item in landed:
        item.wait_recv()
    sum_rows = jnp.zeros(gathered.shape[1:], f32)
    for spot in range(16):
        value = gathered[spot].astype(f32)
        sum_rows += value
        for j in range(6):
            mod_all[j, 4 * spot : 4 * spot + 4, :] = value[4 * j : 4 * j + 4]
        for f in range(4):
            for k in range(4):
                row = 48 + 4 * f + k
                cond_all[4 * spot + f : 4 * spot + f + 1, k * 256 : (k + 1) * 256] = value[
                    row : row + 1
                ]
    for j in range(6):
        ada_sum[j : j + 1, :] = jnp.sum(sum_rows[4 * j : 4 * j + 4], axis=0, keepdims=True)
    for j in range(3):
        qkv_bias[j : j + 1, :] = sum_rows[24 + j : 25 + j]
    for j in range(4):
        part = slice(j * 256, (j + 1) * 256)
        for n, row in enumerate((27, 31, 35)):
            line_sums[n : n + 1, part] = sum_rows[row + j : row + j + 1]
    save(tokens_out, o_tokens)
    save(out_landed, o_output)
    progress(last, 6)
    for item in remote:
        item.wait_send()
    for item in saves:
        item.wait()


def backward(smalls, bigs, width, units, cols):
    f32, bf16 = jnp.float32, jnp.bfloat16
    like = jax.ShapeDtypeStruct
    count, half = 4 * PATCHES, 2 * PATCHES
    vmem = pl.BlockSpec(memory_space=pltpu.VMEM)
    mem = pltpu.VMEM
    dma = lambda *dims: pltpu.SemaphoreType.DMA(dims)
    clip = (8, 64, width)
    return pl.pallas_call(
        backward_kernel,
        in_specs=[vmem] * len(smalls) + [ANY] * len(bigs),
        out_specs=[vmem] * 5 + [ANY] * 6,
        out_shape=[
            like((6, 64, cols), f32), like((64, width), f32), like((6, cols), f32),
            like((3, cols), f32), like((3, width), f32), like((1, units, width), bf16),
            like((1, width, units), bf16), like((3, width, cols), bf16), like((1, cols, width), bf16),
            like(clip, bf16), like(clip, bf16),
        ],
        scratch_shapes=[
            mem((1, units, width), bf16), mem((1, width, units), bf16), mem((half, width), f32),
            mem((half, width), bf16), mem((half, width), bf16), mem((half, width), f32),
            mem(clip, bf16), mem((half, width), f32), mem((half, width), f32),
            mem((half, width), bf16), mem((2, cols, width), bf16), mem((2, count, cols), bf16),
            mem((4, 3, count, 128), bf16), mem((count, 8), f32), mem((2, 3, width, cols), bf16),
            mem((count, width), bf16), mem(clip, bf16),
            mem((count, width), bf16), mem((2, count, cols), bf16), mem((2, 3, count, cols), bf16),
            mem((count, 128), f32), mem((count, 128), f32), mem((3, width, cols), bf16),
            mem((3, width // 2, cols), bf16), mem((3, width // 2, cols), bf16),
            mem((1, cols, width), bf16), mem((1, cols // 2, width), bf16),
            mem((1, cols // 2, width), bf16),
            mem((3, width, cols), bf16), mem((1, cols, width), bf16), mem((half, width), bf16),
            mem((half, width), bf16), mem((half, width), bf16), mem(clip, bf16), mem(clip, bf16),
            mem(clip, bf16), mem(clip, bf16),
            mem((9, 1, 128, width), bf16), mem((9, 1, 64, width), bf16),
            mem((9, 1, 32, width), bf16), mem((4, 3, 128, cols), bf16),
            mem((4, 3, 64, cols), bf16), mem((4, 3, 32, cols), bf16),
            mem((6, 4, width), f32), mem((8, width), f32), mem((2, 2, SMALL_ROWS, cols), f32),
            mem((2, SMALL_ROWS, cols), f32), mem((2, SMALL_ROWS, cols), bf16),
            mem((16, SMALL_ROWS, cols), bf16),
            dma(24), dma(6), dma(13), dma(13, 6), dma(13, 6), dma(9), dma(9), dma(1), dma(1),
            dma(2, 2), dma(2, 2),
            dma(15), dma(15), dma(7), dma(7), dma(7), dma(7),
        ],
        compiler_params=pltpu.CompilerParams(
            collective_id=1, has_side_effects=True, vmem_limit_bytes=63 * MIB
        ),
        name="backward",
    )(*smalls, *bigs)


def fast_body(
    tokens,
    noise_level,
    w_ada,
    b_ada,
    w_qkv,
    b_qkv,
    w_out,
    b_out,
    w_fc1,
    b_fc1,
    w_fc2,
    b_fc2,
    cotangent,
):
    clips, _, quarter, width = tokens.shape
    frames = lax.axis_size("frame")
    cols = w_qkv.shape[2]
    core = lax.axis_index("tensor") % 2
    f32 = jnp.float32
    bf16 = jnp.bfloat16
    condition = jax.nn.silu(embedding(noise_level, width)).astype(bf16)
    mod_part = jnp.einsum(
        "cfd,dke->cfke", condition, w_ada, preferred_element_type=f32
    ) + b_ada.astype(f32)
    message = jnp.concatenate(
        [
            mod_part[:, 0],
            condition.astype(f32).reshape(clips, 4, cols),
            jnp.zeros((clips, 6, cols), f32),
        ],
        axis=1,
    )
    tables = rotary_tables(core, frames)
    two = jnp.stack([tables[0], (tables[2] + tables[4]) - (tables[1] + tables[3])])
    w_kinds = w_qkv.transpose(1, 0, 2)
    biases = jnp.stack([b_out, b_fc1, b_fc2]).astype(f32)
    (
        cond_own, p0, p1, p2, p3, p4, p5, fc1_bias, fc2_bias,
        tokens_own, attn_rows, w_kinds_far, w_out_far, qkv, mixed, lse, cot_own,
        attn_branch, resid_one, in_near, in_other, in_back, fc2_own, fc1_own, b_near, b_far,
        fc_got,
    ) = forward(
        tokens[:, 0], message, w_kinds, b_qkv.reshape(1, 3 * cols), two,
        w_out, biases, w_fc1, w_fc2, cotangent[:, 0],
    )
    mod_all, cond_all, ada_bias, qkv_bias, lines, fc2_sum, fc1_sum, qkv_sum, out_sum, tokens_grad, output = backward(
        [p1, p2, p4, p5, two, cond_own, fc1_bias, fc2_bias, biases],
        [
            fc2_own, fc1_own, in_near, in_other, in_back, resid_one, cot_own, attn_branch,
            b_near, b_far, w_out, w_out_far, mixed, qkv, lse, w_kinds,
            w_kinds_far, attn_rows, tokens_own, fc_got,
        ],
        width, w_fc1.shape[1], cols,
    )
    ada_grad = jnp.einsum(
        "cd,kce->kde", cond_all.astype(bf16), mod_all.astype(bf16), preferred_element_type=f32
    ).transpose(1, 0, 2)
    return (
        output[:, None],
        tokens_grad.astype(f32)[:, None],
        ada_grad,
        ada_bias,
        qkv_sum.astype(f32).transpose(1, 0, 2),
        qkv_bias,
        out_sum[0].astype(f32),
        lines[1],
        fc1_sum[0].astype(f32),
        lines[0],
        fc2_sum[0].astype(f32),
        lines[2],
    )


def pick_body(tokens, *rest):
    paired = (
        lax.axis_size("tensor") == 4
        and lax.axis_size("frame") == 4
        and lax.axis_size("batch") == 2
        and tokens.shape[0] == 8
        and rest[1].shape == (1024, 6, 256)
        and rest[7].shape[1] == 1024
    )
    return fast_body(tokens, *rest) if paired else general_body(tokens, *rest)


def solution(mesh):
    return jax.shard_map(
        pick_body,
        mesh=mesh,
        in_specs=(
            P("batch", "frame", "tensor", None),
            P("batch", "frame"),
            P(None, None, "tensor"),
            P(None, "tensor"),
            P(None, None, "tensor"),
            P(None, "tensor"),
            P("tensor", None),
            P(),
            P(None, "tensor"),
            P("tensor"),
            P("tensor", None),
            P(),
            P("batch", "frame", "tensor", None),
        ),
        out_specs=(
            P("batch", "frame", "tensor", None),
            P("batch", "frame", "tensor", None),
            P(None, None, "tensor"),
            P(None, "tensor"),
            P(None, None, "tensor"),
            P(None, "tensor"),
            P("tensor", None),
            P(),
            P(None, "tensor"),
            P("tensor"),
            P("tensor", None),
            P(),
        ),
        check_vma=False,
    )
```
